256 devices in a mesh: modes: 4 (over x), elem: 64 (over y, z, core).
Axes of the slice: x: 4, y: 4, z: 8, core: 2. Of those that a mesh axis runs over, the one named last changes fastest.
Arguments:
- velocity: float32 [3, 256, 10, 10, 512], P(None, 'elem', None, None, 'modes'), may hold values from -0.3 to 0.3
- element_slot: int32 [64, 4], P('elem'), may hold values from 0 to 3, each once within a row
- lid_noslip: int32 [256], P('modes'), may hold values 0 or 1
Outputs:
- new_velocity: float32 [3, 256, 10, 10, 512], P(None, 'elem', None, None, 'modes')
The draws below stay inside these ranges and needn't reach their ends.
Inputs may be any that keep to these rules, and one draw needn't show every extreme that they name: `element_slot`: each row orders the 4 slots of one index block, each slot once.
All inputs are finite; a program needn't handle non-finite values. No bound on the sum of `lid_noslip` on one device may be relied on, other than what follows from the above.
Results may differ from the reference program's by a relative error of at most 0.0003.
Values sent between devices are 32-bit elements; how exact they have to be, the bound alone decides.
A program may use at most 128 MiB of HBM per device.

```python
import math
import jax
import jax.numpy as jnp
import numpy as np
from jax import lax

P_SIZE = 10
M = 256
Q = 768
ER = 4
E_DEV = 4
NZ = 64
ELEMS = 256
BLOCKS = 64
ITERS = 3
N_MODES = 4


def plant(result, rng, least, top_value):
    longest = result.shape.index(max(result.shape))
    spots = []
    for shift in (0, 1):
        where = [jax.random.randint(jax.random.fold_in(rng, axis), (), 0, length) for axis, length in enumerate(result.shape)]
        where[longest] = (where[longest] + shift) % result.shape[longest]
        spots.append(tuple(where))
    return result.at[spots[0]].set(least).at[spots[1]].set(top_value)


def shard_levels(stream_key, shape, pieces, low, top_value):
    def one(position, shards_of):
        steps = jax.random.uniform(jax.random.fold_in(jax.random.fold_in(stream_key, 6), position), (shards_of,), jnp.float32, low / len(pieces), top_value / len(pieces))
        return jnp.repeat(jnp.exp(steps), shape[position] // shards_of).reshape((-1,) + (1,) * (len(shape) - position - 1))

    loudness = one(*pieces[0])
    for cut in pieces[1:]:
        loudness = loudness * one(*cut)
    return loudness


def gaussian(rng, dims, scale, limit, cuts=(), held_as=jnp.bfloat16):
    loudness = shard_levels(rng, dims, cuts, -0.22, 0.18) if cuts else 1.0
    entries = jax.random.normal(rng, dims, jnp.float32) * scale * loudness
    return jnp.minimum(jnp.maximum(entries, -limit), limit).astype(held_as)


def setup_inputs(seed: int = 0) -> dict:
    keys = jax.random.split(jax.random.key(seed), 4)
    return {
        "velocity": gaussian(keys[0], (3, ELEMS, P_SIZE, P_SIZE, 2 * M), 0.05, 0.3, ((1, 64), (4, 4)), jnp.float32),
        "element_slot": jax.vmap(lambda own: jax.random.permutation(own, E_DEV))(jax.random.split(keys[1], BLOCKS)).reshape((BLOCKS, E_DEV)).astype(jnp.int32),
        "lid_noslip": plant((jax.random.randint(keys[2], (M,), 0, 2) < 1).astype(jnp.int32), jax.random.fold_in(keys[2], 1), 0, 1),
    }


LAMBDA_COEF = 20.0
INV_NU = 10.0
R_INNER = 1.0
SWIRL_SLOPE = -1.0 / 3.0
SWIRL_CURVE = 4.0 / 3.0
highest = lax.Precision.HIGHEST


def legendre_rows(abscissa, degree):
    table_rows = [abscissa * 0.0 + 1.0, abscissa.copy()]
    for degree_now in range(2, degree + 1):
        table_rows.append(((2 * degree_now - 1) * abscissa * table_rows[-1] - (degree_now - 1) * table_rows[-2]) / degree_now)
    return table_rows


def gll_tables(points):
    degree = points - 1
    abscissa = -np.cos(np.pi * np.arange(points) / degree)
    for _ in range(60):
        legendre = legendre_rows(abscissa, degree)
        abscissa = abscissa - (abscissa * legendre[degree] - legendre[degree - 1]) / (points * legendre[degree])
    legendre = legendre_rows(abscissa, degree)
    last_row = legendre[degree]
    weights = 2.0 / (degree * points * last_row ** 2)
    identity = np.eye(points)
    distance = abscissa[:, None] - abscissa[None, :] + identity
    derivative = last_row[:, None] / (last_row[None, :] * distance) * (1.0 - identity)
    derivative[0, 0] = -degree * points / 4.0
    derivative[degree, degree] = degree * points / 4.0
    return (jnp.asarray(abscissa, jnp.float32), jnp.asarray(weights, jnp.float32), jnp.asarray(derivative, jnp.float32))


def radial_nodes(abscissa, column_ids):
    return R_INNER + (column_ids[:, None] + 0.5 * (abscissa[None, :] + 1.0)) / ER


def fourier_tables(mode_count, planes):
    mode_ids = jnp.arange(mode_count, dtype=jnp.int32)
    plane_ids = jnp.arange(planes, dtype=jnp.int32)
    phase_ids = (mode_ids[:, None] * plane_ids[None, :]) % planes
    angles = phase_ids.astype(jnp.float32) * (2.0 * math.pi / planes)
    cosine = jnp.cos(angles)
    sine_part = jnp.sin(angles)
    weight = jnp.where(mode_ids == 0, 1.0, 2.0).astype(jnp.float32)[:, None]
    inverse_table = jnp.stack([weight * cosine, -weight * sine_part], axis=1).reshape(2 * mode_count, planes)
    forward_table = (jnp.stack([cosine, -sine_part], axis=1).reshape(2 * mode_count, planes) / planes).T
    return inverse_table, forward_table


def times_unit(values):
    pair_view = values.reshape(values.shape[:-1] + (values.shape[-1] // 2, 2))
    return jnp.stack([-pair_view[..., 1], pair_view[..., 0]], axis=-1).reshape(values.shape)


def curl_modes(velocity_hat, derivative, inv_radius, wave_number):
    radial_u, swirl_u, axial_u = velocity_hat[0], velocity_hat[1], velocity_hat[2]
    metric_scale = 2.0 * ER

    def along_r(field_data):
        return jnp.einsum('ia,...ajc->...ijc', derivative, field_data, precision=highest) * metric_scale

    def along_z(field_data):
        return jnp.einsum('jb,...ibc->...ijc', derivative, field_data, precision=highest) * metric_scale

    def beside_all(field_data):
        return wave_number * times_unit(field_data)

    curl_r = beside_all(axial_u) * inv_radius - along_z(swirl_u)
    curl_t = along_z(radial_u) - along_r(axial_u)
    curl_z = along_r(swirl_u) + swirl_u * inv_radius - beside_all(radial_u) * inv_radius
    return jnp.stack([curl_r, curl_t, curl_z])


def plane_products(velocity_hat, curl_hat, radius, inverse_table, forward_table):
    dims_in = velocity_hat.shape
    row_count = math.prod(dims_in[1:-1])
    stacked = jnp.concatenate([velocity_hat, curl_hat]).reshape(6 * row_count, dims_in[-1])
    planes = jnp.dot(stacked, inverse_table, precision=highest).reshape(6, row_count, -1)
    radius_rows = jnp.broadcast_to(radius, dims_in[1:-1]).reshape(row_count, 1)
    swirl_base = SWIRL_SLOPE * radius_rows + SWIRL_CURVE / radius_rows
    spin_base = 2.0 * SWIRL_SLOPE
    radial_u, swirl_u, axial_u = planes[0], planes[1], planes[2]
    curl_r, curl_t, curl_z = planes[3], planes[4], planes[5]
    push_r = swirl_u * curl_z - axial_u * curl_t + spin_base * swirl_u + swirl_base * curl_z
    push_t = axial_u * curl_r - radial_u * curl_z - spin_base * radial_u
    push_z = radial_u * curl_t - swirl_u * curl_r - swirl_base * curl_r
    pushed = jnp.stack([push_r, push_t, push_z]).reshape(3 * row_count, -1)
    return jnp.dot(pushed, forward_table, precision=highest).reshape(dims_in)


def to_helical(field_data):
    turned = times_unit(field_data[1])
    return jnp.stack([field_data[0] + turned, field_data[0] - turned, field_data[2]])


def from_helical(field_data):
    radial_u = (field_data[0] + field_data[1]) * 0.5
    swirl_u = times_unit(field_data[1] - field_data[0]) * 0.5
    return jnp.stack([radial_u, swirl_u, field_data[2]])


def helmholtz_parts(abscissa, weights, derivative, wave_cols):
    radius = radial_nodes(abscissa, jnp.arange(ER).astype(jnp.float32))
    outer_w = weights[:, None] * weights[None, :]
    weighted_r = outer_w[None] * radius[:, :, None]
    quarter_h = 0.25 / (ER * ER)
    mass_r = outer_w[None] * quarter_h * radius[:, :, None]
    mass_over_r = outer_w[None] * quarter_h / radius[:, :, None]
    offsets = jnp.array([1.0, -1.0, 0.0], dtype=jnp.float32)
    wave_number = wave_cols[None, :] + offsets[:, None]
    mode_mass = mass_over_r[None, :, :, :, None] * (wave_number * wave_number)[:, None, None, None, :] + LAMBDA_COEF * mass_r[None, :, :, :, None]
    deriv_square = derivative * derivative
    stiff_diag = jnp.einsum('qi,eqj->eij', deriv_square, weighted_r, precision=highest) + jnp.einsum('qj,eiq->eij', deriv_square, weighted_r, precision=highest)
    return weighted_r, mode_mass[:, None], stiff_diag


def apply_local(field_data, derivative, weighted_r, mode_mass):
    grad_i = jnp.einsum('ia,szeajc->szeijc', derivative, field_data, precision=highest)
    grad_j = jnp.einsum('jb,szeibc->szeijc', derivative, field_data, precision=highest)
    flux_weight = weighted_r[None, None, :, :, :, None]
    stiff_part = jnp.einsum('ia,szeijc->szeajc', derivative, flux_weight * grad_i, precision=highest) + jnp.einsum('jb,szeijc->szeibc', derivative, flux_weight * grad_j, precision=highest)
    return stiff_part + mode_mass * field_data


def sum_columns(field_data):
    shared = field_data[..., :, :-1, -1, :, :] + field_data[..., :, 1:, 0, :, :]
    field_data = field_data.at[..., :, :-1, -1, :, :].set(shared)
    return field_data.at[..., :, 1:, 0, :, :].set(shared)


def sum_rows(field_data):
    shared = field_data[..., :-1, :, :, -1, :] + field_data[..., 1:, :, :, 0, :]
    field_data = field_data.at[..., :-1, :, :, -1, :].set(shared)
    return field_data.at[..., 1:, :, :, 0, :].set(shared)


def keep_mask(z_ids, total_rows, noslip_cols):
    node_ids = jnp.arange(P_SIZE, dtype=jnp.int32)[None, :]
    column_grid = jnp.arange(ER, dtype=jnp.int32)[:, None]
    wall_nodes = ((column_grid == 0) & (node_ids == 0)) | ((column_grid == ER - 1) & (node_ids == P_SIZE - 1))
    wall_keep = 1.0 - wall_nodes.astype(jnp.float32)
    row_grid = z_ids[:, None]
    lid_nodes = (((row_grid == 0) & (node_ids == 0)) | ((row_grid == total_rows - 1) & (node_ids == P_SIZE - 1))).astype(jnp.float32)
    lid_comp = jnp.stack([noslip_cols, noslip_cols, jnp.ones_like(noslip_cols)])
    return wall_keep[None, None, :, :, None, None] * (1.0 - lid_nodes[None, :, None, None, :, None] * lid_comp[:, None, None, None, None, :])


def inverse_multiplicity(z_ids, total_rows):
    node_ids = jnp.arange(P_SIZE, dtype=jnp.int32)[None, :]
    column_grid = jnp.arange(ER, dtype=jnp.int32)[:, None]
    share_col = (((node_ids == 0) & (column_grid > 0)) | ((node_ids == P_SIZE - 1) & (column_grid < ER - 1))).astype(jnp.float32)
    row_grid = z_ids[:, None]
    share_row = (((node_ids == 0) & (row_grid > 0)) | ((node_ids == P_SIZE - 1) & (row_grid < total_rows - 1))).astype(jnp.float32)
    counted = (1.0 + share_col)[None, :, :, None] * (1.0 + share_row)[:, None, None, :]
    return (1.0 / counted)[None, :, :, :, :, None]


def mode_inner(left_vec, right_vec, inv_mult):
    local_sum = jnp.sum(left_vec * right_vec * inv_mult, axis=(1, 2, 3, 4))
    return local_sum.reshape(3, -1, 2).sum(-1)


def spread(coefficients):
    return jnp.repeat(coefficients, 2, axis=-1).reshape(3, 1, 1, 1, 1, -1)


def reference(velocity, element_slot, lid_noslip):
    abscissa, weights, derivative = gll_tables(P_SIZE)
    blocks, per_block = element_slot.shape
    columns = 2 * M
    grid_of = (jnp.arange(blocks, dtype=jnp.int32)[:, None] * per_block + element_slot).reshape(-1)
    grid_vel = velocity[:, grid_of].reshape(3, NZ, ER, P_SIZE, P_SIZE, columns)
    inverse_table, forward_table = fourier_tables(M, Q)
    radius = radial_nodes(abscissa, jnp.arange(ER).astype(jnp.float32))
    inv_radius = (1.0 / radius)[:, :, None, None]
    wave_all = (jnp.arange(columns, dtype=jnp.int32) // 2).astype(jnp.float32)

    def row_products(row_vel):
        curl_hat = curl_modes(row_vel, derivative, inv_radius, wave_all)
        return plane_products(row_vel, curl_hat, radius[:, :, None], inverse_table, forward_table)

    nonlinear = jnp.moveaxis(lax.map(row_products, jnp.moveaxis(grid_vel, 1, 0)), 0, 1)
    forcing = LAMBDA_COEF * grid_vel + INV_NU * nonlinear
    outer_w = weights[:, None] * weights[None, :]
    mass_r = outer_w[None] * (0.25 / (ER * ER)) * radius[:, :, None]
    loads = mass_r[None, None, :, :, :, None] * to_helical(forcing)
    block_cols = columns // N_MODES
    load_blocks = jnp.moveaxis(loads.reshape(3, NZ, ER, P_SIZE, P_SIZE, N_MODES, block_cols), 5, 0)
    noslip_blocks = lid_noslip.reshape(N_MODES, M // N_MODES)
    wave_blocks = wave_all.reshape(N_MODES, block_cols)
    z_ids = jnp.arange(NZ, dtype=jnp.int32)
    inv_mult = inverse_multiplicity(z_ids, NZ)

    def solve_block(packed):
        block_loads, block_noslip, block_wave = packed
        weighted_r, mode_mass, stiff_diag = helmholtz_parts(abscissa, weights, derivative, block_wave)
        noslip_cols = jnp.repeat(block_noslip.astype(jnp.float32), 2)
        keep_nodes = keep_mask(z_ids, NZ, noslip_cols)
        diag_local = jnp.broadcast_to(stiff_diag[None, None, :, :, :, None] + mode_mass, block_loads.shape)
        residual = keep_nodes * sum_rows(sum_columns(block_loads))
        jacobi_inv = keep_nodes / sum_rows(sum_columns(diag_local))
        solution = jnp.zeros_like(residual)
        precond = jacobi_inv * residual
        direction = precond
        precond_dot = mode_inner(residual, precond, inv_mult)
        for turn_index in range(ITERS):
            image_vec = keep_nodes * sum_rows(sum_columns(apply_local(direction, derivative, weighted_r, mode_mass)))
            step_length = precond_dot / mode_inner(direction, image_vec, inv_mult)
            solution = solution + spread(step_length) * direction
            if turn_index + 1 < ITERS:
                residual = residual - spread(step_length) * image_vec
                precond = jacobi_inv * residual
                next_dot = mode_inner(residual, precond, inv_mult)
                direction = precond + spread(next_dot / precond_dot) * direction
                precond_dot = next_dot
        return solution

    solved = lax.map(solve_block, (load_blocks, noslip_blocks, wave_blocks))
    solved = jnp.moveaxis(solved, 0, 5).reshape(3, NZ, ER, P_SIZE, P_SIZE, columns)
    result_grid = from_helical(solved).reshape(3, ELEMS, P_SIZE, P_SIZE, columns)
    return jnp.zeros_like(velocity).at[:, grid_of].set(result_grid)
```

```python
import functools

import jax
import jax.numpy as jnp
import ml_dtypes
import numpy as np
from jax import lax
from jax.experimental import pallas as pl
from jax.experimental.pallas import tpu as pltpu
from jax.sharding import PartitionSpec as P

PS = 10
NODES = PS * PS
R = 112
M = 256
Q = 768
ER = 4
LANES = 128
LAMBDA_COEF = 20.0
INV_NU = 10.0
R_INNER = 1.0
SWIRL_SLOPE = -1.0 / 3.0
SWIRL_CURVE = 4.0 / 3.0
MESH = pl.DeviceIdType.MESH
F32 = jnp.float32
BF16 = jnp.bfloat16


def legendre_rows(abscissa, degree):
    table_rows = [abscissa * 0.0 + 1.0, abscissa.copy()]
    for degree_now in range(2, degree + 1):
        table_rows.append(
            ((2 * degree_now - 1) * abscissa * table_rows[-1] - (degree_now - 1) * table_rows[-2])
            / degree_now
        )
    return table_rows


def gll_tables(points):
    degree = points - 1
    abscissa = -np.cos(np.pi * np.arange(points) / degree)
    for _ in range(60):
        legendre = legendre_rows(abscissa, degree)
        abscissa = abscissa - (abscissa * legendre[degree] - legendre[degree - 1]) / (
            points * legendre[degree]
        )
    legendre = legendre_rows(abscissa, degree)
    last_row = legendre[degree]
    weights = 2.0 / (degree * points * last_row**2)
    identity = np.eye(points)
    distance = abscissa[:, None] - abscissa[None, :] + identity
    derivative = last_row[:, None] / (last_row[None, :] * distance) * (1.0 - identity)
    derivative[0, 0] = -degree * points / 4.0
    derivative[degree, degree] = degree * points / 4.0
    return abscissa, weights, derivative


def halves(values):
    high = values.astype(ml_dtypes.bfloat16)
    low = (values - high.astype(np.float64)).astype(ml_dtypes.bfloat16)
    return high, low


@functools.cache
def constants():
    xi, w, deriv = gll_tables(PS)
    eye = np.eye(PS)
    radius = R_INNER + (np.arange(ER)[:, None] + 0.5 * (xi[None, :] + 1.0)) / ER
    ww = np.outer(w, w)

    def operator(rows):
        padded = np.zeros((R, LANES))
        padded[:NODES, :NODES] = rows
        high, low = halves(padded)
        return np.concatenate([high, high, low], axis=1)

    slope_r = operator(2.0 * ER * np.kron(deriv, eye))
    slope_z = operator(2.0 * ER * np.kron(eye, deriv))
    slopes = np.concatenate([slope_r, slope_z], axis=0)

    stiff, stiff_diag = [], np.zeros((ER, PS, PS))
    for ir in range(ER):
        along_i = deriv.T @ np.diag(w * radius[ir]) @ deriv
        along_j = deriv.T @ np.diag(w) @ deriv
        whole = np.kron(along_i, np.diag(w)) + np.kron(np.diag(w * radius[ir]), along_j)
        stiff_diag[ir] = np.diag(whole).reshape(PS, PS)
        stiff.append(operator(whole - np.diag(np.diag(whole))))
    stiff = np.stack(stiff)

    quarter_h = 0.25 / (ER * ER)
    mass_r = ww[None] * quarter_h * radius[:, :, None]
    mass_over_r = ww[None] * quarter_h / radius[:, :, None]

    def radial_sum(values):
        total = values.copy()
        total[:-1, -1] += values[1:, 0]
        total[1:, 0] += values[:-1, -1]
        return total

    diag_fixed = radial_sum(stiff_diag + LAMBDA_COEF * mass_r)
    diag_square = radial_sum(mass_over_r)
    diag_fixed[0, 0] = 0.0
    diag_fixed[-1, -1] = 0.0

    geometry = np.zeros((3 * ER + 2, R, LANES))
    geometry[0:ER, :NODES] = mass_r.reshape(ER, NODES, 1)
    geometry[ER : 2 * ER, :NODES] = diag_fixed.reshape(ER, NODES, 1)
    geometry[2 * ER : 3 * ER, :NODES] = diag_square.reshape(ER, NODES, 1)
    geometry[3 * ER] = 1.0
    geometry[3 * ER, :NODES] = (R_INNER + 0.5 * (np.repeat(xi, PS) + 1.0) / ER)[:, None]
    face = np.zeros((PS, PS))
    face[:, 0] = 1.0
    face[:, -1] = 2.0
    geometry[3 * ER + 1, :NODES] = face.reshape(NODES, 1)

    modes = np.arange(M)
    angles = (modes[:, None] * np.arange(Q)[None, :] % Q) * (2.0 * np.pi / Q)
    weight = np.where(modes == 0, 1.0, 2.0)[:, None]
    inverse = np.stack([weight * np.cos(angles), -weight * np.sin(angles)], axis=1)
    inverse = inverse.reshape(2 * M // LANES, LANES, Q)
    high, low = halves(inverse)
    to_planes = np.concatenate([high, high, low], axis=1)
    forward = np.stack([np.cos(angles), -np.sin(angles)], axis=1) / Q
    forward = forward.reshape(2 * M // LANES, LANES, Q).transpose(0, 2, 1)
    high, low = halves(forward)
    to_modes = np.concatenate([high, low], axis=2)
    return slopes, stiff, geometry.astype(np.float32), to_planes, to_modes


def split(values):
    high = values.astype(BF16)
    low = (values - high.astype(F32)).astype(BF16)
    return high, low


def dot(left, right):
    return jnp.dot(left, right, preferred_element_type=F32)


def kernel(
    grid_shape,
    slot_ref,
    lid_ref,
    vel_ref,
    slopes_hbm,
    stiff_hbm,
    geo_hbm,
    planes_hbm,
    modes_hbm,
    out_ref,
    vel,
    recv,
    slopes,
    stiff,
    geo,
    to_planes,
    to_modes,
    nodes,
    rhs,
    fields,
    planes,
    push_hi,
    push_lo,
    sendb,
    back,
    own,
    jac,
    vec,
    img,
    krhs,
    face_out,
    face_in,
    moment,
    red_a,
    red_b,
    local_sem,
    fwd_send,
    fwd_recv,
    bwd_send,
    bwd_recv,
    halo_send,
    halo_recv,
    a_send,
    a_recv,
    b_send,
    b_recv,
):
    ny, nz, nc = grid_shape
    n_elem = ny * nz * nc
    n_modes = ER
    mi = lax.axis_index("modes")
    e = lax.axis_index("elem")
    core = lax.rem(e, nc)
    zc = lax.rem(e // nc, nz)
    yc = e // (nc * nz)
    size_a = ny * nc
    rank_a = yc * nc + core

    def member_a(t):
        return ((t // nc) * nz + zc) * nc + lax.rem(t, nc)

    def member_b(t):
        return (yc * nz + t) * nc + core

    above = lax.rem(e + 1, n_elem)
    below = lax.rem(e + n_elem - 1, n_elem)

    local_pairs = [
        (vel_ref, vel),
        (slopes_hbm, slopes),
        (planes_hbm, to_planes),
        (geo_hbm, geo),
        (modes_hbm, to_modes),
        (stiff_hbm, stiff),
    ]
    local = [
        pltpu.make_async_copy(src, dst, local_sem.at[i]) for i, (src, dst) in enumerate(local_pairs)
    ]
    for copy in local:
        copy.start()

    barrier = pltpu.get_barrier_semaphore()
    greeted = [(lax.rem(mi + t, n_modes), e) for t in range(1, n_modes)]
    greeted += [(mi, above), (mi, below)]
    greeted += [(mi, member_a(lax.rem(rank_a + t, size_a))) for t in range(1, size_a)]
    greeted += [(mi, member_b(lax.rem(zc + t, nz))) for t in range(1, nz)]
    for who in greeted:
        pl.semaphore_signal(barrier, inc=1, device_id=who, device_id_type=MESH)
    pl.semaphore_wait(barrier, len(greeted))

    forward = {}
    for off in (2, 1, 3):
        to = lax.rem(mi + off, n_modes)
        forward[off] = pltpu.make_async_remote_copy(
            src_ref=vel_ref.at[:, to],
            dst_ref=recv.at[off],
            send_sem=fwd_send.at[off],
            recv_sem=fwd_recv.at[off],
            device_id=(to, e),
            device_id_type=MESH,
        )
        forward[off].start()

    lane = lax.broadcasted_iota(jnp.int32, (1, LANES), 1)
    even = lax.rem(lane, 2) == 0
    pair = (lane // 2).astype(F32)

    def times_unit(values):
        return jnp.where(even, -pltpu.roll(values, LANES - 1, 1), pltpu.roll(values, 1, 1))

    def pair_sum(values):
        return values + jnp.where(even, pltpu.roll(values, LANES - 1, 1), pltpu.roll(values, 1, 1))

    zero_rows = jnp.zeros((R - NODES + 4, LANES), F32)
    for s in range(3):
        nodes[s, NODES - 4 :, :] = zero_rows
        for g in range(ER):
            own[s, g, NODES - 4 :, :] = zero_rows
    no_rows = jnp.zeros((LANES - R, 3 * LANES), BF16)
    for part in range(3):
        rhs[part * LANES + R : (part + 1) * LANES, :] = no_rows
        for g in range(ER):
            krhs[g, part * LANES + R : (part + 1) * LANES, :] = no_rows
    moment[...] = jnp.zeros_like(moment)

    local[0].wait()
    for copy in local[1:3]:
        copy.wait()
    local[3].wait()

    cell = jnp.int32(0)
    for g in range(ER):
        cell = jnp.where(slot_ref[0, g] == mi, g, cell)
    radius = geo[3 * ER, :, :] + cell.astype(F32) * (1.0 / ER)
    inv_radius = 1.0 / radius
    swirl_base = SWIRL_SLOPE * radius + SWIRL_CURVE * inv_radius

    def add_modes(block, source, first):
        for s in range(3):
            for i in range(PS):
                nodes[s, PS * i : PS * (i + 1), :] = block(s, i)
        for s in range(3):
            high, low = split(nodes[s])
            cols = slice(s * LANES, (s + 1) * LANES)
            rhs[0:R, cols] = high
            rhs[LANES : LANES + R, cols] = low
            rhs[2 * LANES : 2 * LANES + R, cols] = high
        slope = dot(slopes[...], rhs[...])
        d_r = [slope[:R, s * LANES : (s + 1) * LANES] for s in range(3)]
        d_z = [slope[R:, s * LANES : (s + 1) * LANES] for s in range(3)]
        wave = pair + (source * (LANES // 2)).astype(F32)
        u_r, u_t, u_z = nodes[0], nodes[1], nodes[2]
        curl_r = wave * times_unit(u_z) * inv_radius - d_z[1]
        curl_t = d_z[0] - d_r[2]
        curl_z = d_r[1] + (u_t - wave * times_unit(u_r)) * inv_radius
        for f, values in enumerate((u_r, u_t, u_z, curl_r, curl_t, curl_z)):
            high, low = split(values)
            rows = slice(f * R, (f + 1) * R)
            fields[rows, 0:LANES] = high
            fields[rows, LANES : 2 * LANES] = low
            fields[rows, 2 * LANES :] = high
        terms = dot(fields[...], to_planes[source])
        if first:
            planes[...] = terms
        else:
            planes[...] += terms

    add_modes(lambda s, i: vel[s, mi, i], mi, True)

    for g in range(ER):
        held = slot_ref[0, g]
        for s in range(3):
            for i in range(PS):
                own[s, g, PS * i : PS * (i + 1), :] = vel[s, held, i]

    lid = lid_ref[...].astype(BF16)
    wide = lax.broadcasted_iota(jnp.int32, (LANES // 2, LANES), 1) // 2
    tall = lax.broadcasted_iota(jnp.int32, (LANES // 2, LANES), 0)
    noslip = dot(lid, (wide == tall).astype(BF16))
    side = geo[3 * ER + 1, :, :]
    low_side, high_side = side == 1.0, side == 2.0
    at_low, at_high = (e == 0).astype(F32), (e == n_elem - 1).astype(F32)
    lid_rows = jnp.where(low_side, at_low, 0.0) + jnp.where(high_side, at_high, 0.0)
    sharing = 1.0 + jnp.where(low_side, 1.0 - at_low, 0.0) + jnp.where(high_side, 1.0 - at_high, 0.0)
    wave_own = pair + (mi * (LANES // 2)).astype(F32)
    for s, offset in enumerate((1.0, -1.0, 0.0)):
        square = (wave_own + offset) * (wave_own + offset)
        lid_keep = 1.0 - lid_rows * (noslip if s < 2 else 1.0)
        for g in range(ER):
            fixed = geo[ER + g]
            diag = (fixed + square * geo[2 * ER + g]) * sharing
            jac[s, g] = jnp.where(fixed > 0.0, lid_keep / jnp.where(fixed > 0.0, diag, 1.0), 0.0)

    for off in (1, 3, 2):
        forward[off].wait_recv()
        source = lax.rem(mi + n_modes - off, n_modes)
        add_modes(lambda s, i: recv[off, s, i], source, False)

    block_rows = 16

    def push_rows(step, _):
        start = pl.multiple_of(step * block_rows, block_rows)

        def field(f, cols):
            return planes[pl.ds(pl.multiple_of(f * R + start, block_rows), block_rows), cols]

        geo_rows = geo[3 * ER, pl.ds(start, block_rows), :]
        rad = geo_rows + cell.astype(F32) * (1.0 / ER)
        swirl = SWIRL_SLOPE * rad + SWIRL_CURVE / rad
        swirl = jnp.concatenate([swirl] * 3, axis=1)
        spin = 2.0 * SWIRL_SLOPE
        for cols in (slice(0, 3 * LANES), slice(3 * LANES, 6 * LANES)):
            u_r, u_t, u_z, w_r, w_t, w_z = [field(f, cols) for f in range(6)]
            turned = u_t + swirl
            results = (
                turned * w_z - u_z * w_t + spin * u_t,
                u_z * w_r - u_r * w_z - spin * u_r,
                u_r * w_t - turned * w_r,
            )
            for s, values in enumerate(results):
                high, low = split(values)
                rows = pl.ds(pl.multiple_of(s * R + start, block_rows), block_rows)
                push_hi[rows, cols] = high
                push_lo[rows, cols] = low
        return 0

    lax.fori_loop(0, R // block_rows, push_rows, 0)

    local[4].wait()
    backward = {}
    for off in (2, 1, 3, 0):
        to = lax.rem(mi + off, n_modes)
        two = dot(push_hi[...], to_modes[to])
        one = dot(push_lo[...], to_modes[to, :, 0:LANES])
        result = two[:, :LANES] + (two[:, LANES:] + one)
        for s in range(3):
            if off == 0:
                back[mi, s] = result[s * R : (s + 1) * R]
            else:
                sendb[off, s] = result[s * R : (s + 1) * R]
        if off:
            backward[off] = pltpu.make_async_remote_copy(
                src_ref=sendb.at[off],
                dst_ref=back.at[mi],
                send_sem=bwd_send.at[off],
                recv_sem=bwd_recv.at[off],
                device_id=(to, e),
                device_id_type=MESH,
            )
            backward[off].start()
    local[5].wait()
    for off in (1, 3, 2):
        backward[off].wait_recv()

    for g in range(ER):
        held = slot_ref[0, g]
        force = [LAMBDA_COEF * own[s, g] + INV_NU * back[held, s] for s in range(3)]
        turned = times_unit(force[1])
        mass = geo[g]
        img[0, 0, g] = mass * (force[0] + turned)
        img[0, 1, g] = mass * (force[0] - turned)
        img[0, 2, g] = mass * force[2]

    face_row = lax.broadcasted_iota(jnp.int32, (ER * PS, 1), 0)
    inner_high = (lax.rem(face_row, PS) == PS - 1) & (face_row < ER * PS - 1)
    inner_low = (lax.rem(face_row, PS) == 0) & (face_row > 0)

    def low_rows():
        return pl.ds(0, PS, stride=PS)

    def high_rows():
        return pl.ds(PS - 1, PS, stride=PS)

    halos = []

    def send_faces(k):
        for s in range(3):
            for g in range(ER):
                rows = slice(g * PS, (g + 1) * PS)
                face_out[k, 0, s, rows, :] = img[k, s, g, low_rows(), :]
                face_out[k, 1, s, rows, :] = img[k, s, g, high_rows(), :]
        pairs = []
        for side_out, who in ((0, below), (1, above)):
            copy = pltpu.make_async_remote_copy(
                src_ref=face_out.at[k, side_out],
                dst_ref=face_in.at[k, 1 - side_out],
                send_sem=halo_send.at[k, side_out],
                recv_sem=halo_recv.at[k, 1 - side_out],
                device_id=(mi, who),
                device_id_type=MESH,
            )
            copy.start()
            pairs.append(copy)
        halos.append(pairs)

    def inner_part(k):
        for s in range(3):
            for g in range(ER):
                vec[k, s, g] = img[k, s, g]
            for g in range(ER - 1):
                shared = img[k, s, g, NODES - PS : NODES, :] + img[k, s, g + 1, 0:PS, :]
                vec[k, s, g, NODES - PS : NODES, :] = shared
                vec[k, s, g + 1, 0:PS, :] = shared
            for g in range(ER):
                vec[k, s, g] = vec[k, s, g] * jac[s, g]

    def outer_part(k):
        for copy in halos[k]:
            copy.wait_recv()
        for side_in, present, row_set in ((0, 1.0 - at_low, low_rows), (1, 1.0 - at_high, high_rows)):
            for s in range(3):
                values = face_in[k, side_in, s]
                values = values + jnp.where(inner_high, pltpu.roll(values, ER * PS - 1, 0), 0.0)
                after = face_in[k, side_in, s]
                values = values + jnp.where(inner_low, pltpu.roll(after, 1, 0), 0.0)
                values = values * present
                for g in range(ER):
                    part = values[g * PS : (g + 1) * PS] * jac[s, g, row_set(), :]
                    vec[k, s, g, row_set(), :] = vec[k, s, g, row_set(), :] + part

    def apply_stiff(k):
        for g in range(ER):
            for s in range(3):
                high, low = split(vec[k, s, g])
                cols = slice(s * LANES, (s + 1) * LANES)
                krhs[g, 0:R, cols] = high
                krhs[g, LANES : LANES + R, cols] = low
                krhs[g, 2 * LANES : 2 * LANES + R, cols] = high
            image = dot(stiff[g], krhs[g])
            for s in range(3):
                img[k + 1, s, g] = image[:, s * LANES : (s + 1) * LANES]

    def inner(k, left, right):
        for s in range(3):
            total = jnp.zeros((1, LANES), F32)
            for g in range(ER):
                products = vec[left, s, g] * img[right, s, g]
                total = total + jnp.sum(products, axis=0, keepdims=True)
            index = k * 3 + s
            moment[index // 9, index % 9 : index % 9 + 1, :] = total

    send_faces(0)
    inner_part(0)
    outer_part(0)
    apply_stiff(0)
    send_faces(1)
    inner(0, 0, 0)
    inner(1, 0, 1)
    inner_part(1)
    outer_part(1)
    apply_stiff(1)
    send_faces(2)
    inner(2, 1, 1)
    inner(3, 1, 2)
    inner_part(2)
    outer_part(2)
    apply_stiff(2)
    inner(4, 2, 2)
    inner(5, 2, 3)

    def exchange(buffer, rank, size, member, send_sems, recv_sems):
        copies = []
        for off in range(1, size):
            copy = pltpu.make_async_remote_copy(
                src_ref=buffer.at[rank],
                dst_ref=buffer.at[rank],
                send_sem=send_sems.at[off],
                recv_sem=recv_sems.at[off],
                device_id=(mi, member(lax.rem(rank + off, size))),
                device_id_type=MESH,
            )
            copy.start()
            copies.append(copy)
        for copy in copies:
            copy.wait_recv()
        total = buffer[0]
        for t in range(1, size):
            total = total + buffer[t]
        return total, copies

    red_a[rank_a] = jnp.where(even, pair_sum(moment[0]), pair_sum(moment[1]))
    total, copies_a = exchange(red_a, rank_a, size_a, member_a, a_send, a_recv)
    red_b[zc] = total
    total, copies_b = exchange(red_b, zc, nz, member_b, b_send, b_recv)
    first = jnp.where(even, total, pltpu.roll(total, 1, 1))
    second = jnp.where(even, pltpu.roll(total, LANES - 1, 1), total)

    coefs = []
    for s in range(3):
        h = [(first if k < 3 else second)[(k % 3) * 3 + s : (k % 3) * 3 + s + 1] for k in range(6)]
        g00, g01, g02, g12, g22 = [h[k] + h[k + 1] for k in range(5)]
        g11 = g02
        ratio1, ratio2 = g01 / g00, g02 / g00
        d1 = g11 - ratio1 * g01
        left = g12 - ratio1 * g02
        ratio = left / d1
        d2 = g22 - ratio2 * g02 - ratio * left
        y1 = h[1] - ratio1 * h[0]
        y2 = h[2] - ratio2 * h[0] - ratio * y1
        c2 = y2 / d2
        c1 = y1 / d1 - ratio * c2
        c0 = h[0] / g00 - ratio1 * c1 - ratio2 * c2
        coefs.append((c0, c1, c2))

    for slot in range(ER):
        held = jnp.int32(0)
        for g in range(ER):
            held = jnp.where(slot_ref[0, g] == slot, g, held)
        plus, minus, axial = [
            coefs[s][0] * vec[0, s, held] + coefs[s][1] * vec[1, s, held] + coefs[s][2] * vec[2, s, held]
            for s in range(3)
        ]
        results = ((plus + minus) * 0.5, times_unit(minus - plus) * 0.5, axial)
        for s, values in enumerate(results):
            for i in range(PS):
                out_ref[s, slot, i] = values[PS * i : PS * (i + 1)]

    for copies in (forward.values(), backward.values(), copies_a, copies_b, *halos):
        for copy in copies:
            copy.wait_send()


def on_device(grid_shape, velocity, element_slot, lid_noslip):
    ny, nz, nc = grid_shape
    slopes, stiff, geometry, to_planes, to_modes = constants()
    any_spec = pl.BlockSpec(memory_space=pl.ANY)
    vmem = pltpu.VMEM
    dma = pltpu.SemaphoreType.DMA
    return pl.pallas_call(
        functools.partial(kernel, grid_shape),
        out_shape=jax.ShapeDtypeStruct(velocity.shape, F32),
        in_specs=[
            pl.BlockSpec(memory_space=pltpu.SMEM),
            pl.BlockSpec(memory_space=vmem),
        ]
        + [any_spec] * 6,
        out_specs=pl.BlockSpec(memory_space=vmem),
        scratch_shapes=[
            vmem(velocity.shape, F32),
            vmem((ER, 3, PS, PS, LANES), F32),
            vmem(slopes.shape, BF16),
            vmem(stiff.shape, BF16),
            vmem(geometry.shape, F32),
            vmem(to_planes.shape, BF16),
            vmem(to_modes.shape, BF16),
            vmem((3, R, LANES), F32),
            vmem((3 * LANES, 3 * LANES), BF16),
            vmem((6 * R, 3 * LANES), BF16),
            vmem((6 * R, Q), F32),
            vmem((3 * R, Q), BF16),
            vmem((3 * R, Q), BF16),
            vmem((ER, 3, R, LANES), F32),
            vmem((ER, 3, R, LANES), F32),
            vmem((3, ER, R, LANES), F32),
            vmem((3, ER, R, LANES), F32),
            vmem((3, 3, ER, R, LANES), F32),
            vmem((4, 3, ER, R, LANES), F32),
            vmem((ER, 3 * LANES, 3 * LANES), BF16),
            vmem((3, 2, 3, ER * PS, LANES), F32),
            vmem((3, 2, 3, ER * PS, LANES), F32),
            vmem((2, 16, LANES), F32),
            vmem((ny * nc, 16, LANES), F32),
            vmem((nz, 16, LANES), F32),
            dma((6,)),
            dma((ER,)),
            dma((ER,)),
            dma((ER,)),
            dma((ER,)),
            dma((3, 2)),
            dma((3, 2)),
            dma((ny * nc,)),
            dma((ny * nc,)),
            dma((nz,)),
            dma((nz,)),
        ],
        compiler_params=pltpu.CompilerParams(
            collective_id=0, has_side_effects=True, vmem_limit_bytes=48 * 1024 * 1024
        ),
    )(
        element_slot,
        lid_noslip.reshape(1, -1),
        velocity,
        jnp.asarray(slopes),
        jnp.asarray(stiff),
        jnp.asarray(geometry),
        jnp.asarray(to_planes),
        jnp.asarray(to_modes),
    )


def solution(mesh):
    n_elem = mesh.shape["elem"]
    nc = 2
    nz = min(8, n_elem // nc)
    ny = n_elem // (nc * nz)
    return jax.shard_map(
        functools.partial(on_device, (ny, nz, nc)),
        mesh=mesh,
        in_specs=(P(None, "elem", None, None, "modes"), P("elem", None), P("modes")),
        out_specs=P(None, "elem", None, None, "modes"),
        check_vma=False,
    )
```

```python
import functools

import jax
import jax.numpy as jnp
import ml_dtypes
import numpy as np
from jax import lax
from jax.experimental import pallas as pl
from jax.experimental.pallas import tpu as pltpu
from jax.sharding import PartitionSpec as P

PS = 10
NODES = PS * PS
R = 112
M = 256
Q = 768
ER = 4
LANES = 128
LAMBDA_COEF = 20.0
INV_NU = 10.0
R_INNER = 1.0
SWIRL_SLOPE = -1.0 / 3.0
SWIRL_CURVE = 4.0 / 3.0
MESH = pl.DeviceIdType.MESH
F32 = jnp.float32
BF16 = jnp.bfloat16


def legendre_rows(abscissa, degree):
    table_rows = [abscissa * 0.0 + 1.0, abscissa.copy()]
    for degree_now in range(2, degree + 1):
        table_rows.append(
            ((2 * degree_now - 1) * abscissa * table_rows[-1] - (degree_now - 1) * table_rows[-2])
            / degree_now
        )
    return table_rows


def gll_tables(points):
    degree = points - 1
    abscissa = -np.cos(np.pi * np.arange(points) / degree)
    for _ in range(60):
        legendre = legendre_rows(abscissa, degree)
        abscissa = abscissa - (abscissa * legendre[degree] - legendre[degree - 1]) / (
            points * legendre[degree]
        )
    legendre = legendre_rows(abscissa, degree)
    last_row = legendre[degree]
    weights = 2.0 / (degree * points * last_row**2)
    identity = np.eye(points)
    distance = abscissa[:, None] - abscissa[None, :] + identity
    derivative = last_row[:, None] / (last_row[None, :] * distance) * (1.0 - identity)
    derivative[0, 0] = -degree * points / 4.0
    derivative[degree, degree] = degree * points / 4.0
    return abscissa, weights, derivative


def halves(values):
    high = values.astype(ml_dtypes.bfloat16)
    low = (values - high.astype(np.float64)).astype(ml_dtypes.bfloat16)
    return high, low


@functools.cache
def constants():
    xi, w, deriv = gll_tables(PS)
    eye = np.eye(PS)
    radius = R_INNER + (np.arange(ER)[:, None] + 0.5 * (xi[None, :] + 1.0)) / ER
    ww = np.outer(w, w)

    def operator(rows):
        padded = np.zeros((R, LANES))
        padded[:NODES, :NODES] = rows
        high, low = halves(padded)
        return np.concatenate([high, high, low], axis=1)

    slope_r = operator(2.0 * ER * np.kron(deriv, eye))
    slope_z = operator(2.0 * ER * np.kron(eye, deriv))
    slopes = np.concatenate([slope_r, slope_z], axis=0)

    stiff, stiff_diag = [], np.zeros((ER, PS, PS))
    for ir in range(ER):
        along_i = deriv.T @ np.diag(w * radius[ir]) @ deriv
        along_j = deriv.T @ np.diag(w) @ deriv
        whole = np.kron(along_i, np.diag(w)) + np.kron(np.diag(w * radius[ir]), along_j)
        stiff_diag[ir] = np.diag(whole).reshape(PS, PS)
        stiff.append(operator(whole - np.diag(np.diag(whole))))
    stiff = np.stack(stiff)

    quarter_h = 0.25 / (ER * ER)
    mass_r = ww[None] * quarter_h * radius[:, :, None]
    mass_over_r = ww[None] * quarter_h / radius[:, :, None]

    def radial_sum(values):
        total = values.copy()
        total[:-1, -1] += values[1:, 0]
        total[1:, 0] += values[:-1, -1]
        return total

    diag_fixed = radial_sum(stiff_diag + LAMBDA_COEF * mass_r)
    diag_square = radial_sum(mass_over_r)
    diag_fixed[0, 0] = 0.0
    diag_fixed[-1, -1] = 0.0

    geometry = np.zeros((3 * ER + 2, R, LANES))
    geometry[0:ER, :NODES] = mass_r.reshape(ER, NODES, 1)
    geometry[ER : 2 * ER, :NODES] = diag_fixed.reshape(ER, NODES, 1)
    geometry[2 * ER : 3 * ER, :NODES] = diag_square.reshape(ER, NODES, 1)
    geometry[3 * ER] = 1.0
    geometry[3 * ER, :NODES] = (R_INNER + 0.5 * (np.repeat(xi, PS) + 1.0) / ER)[:, None]
    face = np.zeros((PS, PS))
    face[:, 0] = 1.0
    face[:, -1] = 2.0
    geometry[3 * ER + 1, :NODES] = face.reshape(NODES, 1)

    modes = np.arange(M)
    angles = (modes[:, None] * np.arange(Q)[None, :] % Q) * (2.0 * np.pi / Q)
    weight = np.where(modes == 0, 1.0, 2.0)[:, None]
    inverse = np.stack([weight * np.cos(angles), -weight * np.sin(angles)], axis=1)
    inverse = inverse.reshape(2 * M // LANES, LANES, Q)
    high, low = halves(inverse)
    to_planes = np.concatenate([high, high, low], axis=1)
    forward = np.stack([np.cos(angles), -np.sin(angles)], axis=1) / Q
    forward = forward.reshape(2 * M // LANES, LANES, Q).transpose(0, 2, 1)
    high, low = halves(forward)
    to_modes = np.concatenate([high, low], axis=2)
    return slopes, stiff, geometry.astype(np.float32), to_planes, to_modes


def split(values):
    high = values.astype(BF16)
    low = (values - high.astype(F32)).astype(BF16)
    return high, low


def dot(left, right):
    return jnp.dot(left, right, preferred_element_type=F32)


def kernel(
    grid_shape,
    slot_hbm,
    lid_hbm,
    vel_hbm,
    slopes_hbm,
    stiff_hbm,
    geo_hbm,
    planes_hbm,
    modes_hbm,
    out_ref,
    slot_ref,
    lid_ref,
    vel,
    slots,
    recv,
    slopes,
    stiff,
    geo,
    to_planes,
    to_modes,
    rhs,
    fields,
    planes,
    push_hi,
    push_lo,
    sendb,
    back,
    jac,
    vec,
    img,
    krhs,
    face_out,
    face_in,
    moment,
    red_a,
    red_b,
    local_sem,
    fwd_send,
    fwd_recv,
    bwd_send,
    bwd_recv,
    halo_send,
    halo_recv,
    a_send,
    a_recv,
    b_send,
    b_recv,
):
    ny, nz, nc = grid_shape
    n_elem = ny * nz * nc
    n_modes = ER
    mi = lax.axis_index("modes")
    e = lax.axis_index("elem")
    core = lax.rem(e, nc)
    zc = lax.rem(e // nc, nz)
    yc = e // (nc * nz)
    size_a = ny * nc
    rank_a = yc * nc + core

    def member_a(t):
        return ((t // nc) * nz + zc) * nc + lax.rem(t, nc)

    def member_b(t):
        return (yc * nz + t) * nc + core

    above = lax.rem(e + 1, n_elem)
    below = lax.rem(e + n_elem - 1, n_elem)

    local_pairs = [
        (vel_hbm, vel),
        (slopes_hbm, slopes),
        (planes_hbm, to_planes),
        (geo_hbm, geo),
        (slot_hbm, slot_ref),
        (lid_hbm, lid_ref),
        (modes_hbm, to_modes),
        (stiff_hbm, stiff),
    ]
    local = [
        pltpu.make_async_copy(src, dst, local_sem.at[i]) for i, (src, dst) in enumerate(local_pairs)
    ]
    for copy in local:
        copy.start()

    for g in range(ER):
        for s in range(3):
            slots[g, s, R - 16 :, :] = jnp.zeros((16, LANES), F32)
    no_rows = jnp.zeros((LANES - R, 3 * LANES), BF16)
    for part in range(3):
        rhs[part * LANES + R : (part + 1) * LANES, :] = no_rows
        for g in range(ER):
            krhs[g, part * LANES + R : (part + 1) * LANES, :] = no_rows
    moment[...] = jnp.zeros_like(moment)

    def gather_slot(slot):
        for s in range(3):
            rows = pl.ds(s * NODES * ER + slot, NODES, stride=ER)
            slots[slot, s, 0:NODES, :] = vel[rows, :]

    barrier = pltpu.get_barrier_semaphore()
    greeted = [(lax.rem(mi + t, n_modes), e) for t in range(1, n_modes)]
    greeted += [(mi, above), (mi, below)]
    greeted += [(mi, member_a(lax.rem(rank_a + t, size_a))) for t in range(1, size_a)]
    greeted += [(mi, member_b(lax.rem(zc + t, nz))) for t in range(1, nz)]
    for who in greeted:
        pl.semaphore_signal(barrier, inc=1, device_id=who, device_id_type=MESH)
    pl.semaphore_wait(barrier, len(greeted))

    local[0].wait()
    forward = {}
    for off in (2, 1, 3):
        to = lax.rem(mi + off, n_modes)
        gather_slot(to)
        forward[off] = pltpu.make_async_remote_copy(
            src_ref=slots.at[to],
            dst_ref=recv.at[off],
            send_sem=fwd_send.at[off],
            recv_sem=fwd_recv.at[off],
            device_id=(to, e),
            device_id_type=MESH,
        )
        forward[off].start()

    lane = lax.broadcasted_iota(jnp.int32, (1, LANES), 1)
    even = lax.rem(lane, 2) == 0
    pair = (lane // 2).astype(F32)

    def times_unit(values):
        return jnp.where(even, -pltpu.roll(values, LANES - 1, 1), pltpu.roll(values, 1, 1))

    def pair_sum(values):
        return values + jnp.where(even, pltpu.roll(values, LANES - 1, 1), pltpu.roll(values, 1, 1))

    gather_slot(mi)
    for copy in local[1:6]:
        copy.wait()

    cell = jnp.int32(0)
    for g in range(ER):
        cell = jnp.where(slot_ref[0, g] == mi, g, cell)
    radius = geo[3 * ER, :, :] + cell.astype(F32) * (1.0 / ER)
    inv_radius = 1.0 / radius
    swirl_base = SWIRL_SLOPE * radius + SWIRL_CURVE * inv_radius

    def add_modes(block, source, first):
        for s in range(3):
            high, low = split(block[s])
            cols = slice(s * LANES, (s + 1) * LANES)
            rhs[0:R, cols] = high
            rhs[LANES : LANES + R, cols] = low
            rhs[2 * LANES : 2 * LANES + R, cols] = high
        slope = dot(slopes[...], rhs[...])
        d_r = [slope[:R, s * LANES : (s + 1) * LANES] for s in range(3)]
        d_z = [slope[R:, s * LANES : (s + 1) * LANES] for s in range(3)]
        wave = pair + (source * (LANES // 2)).astype(F32)
        u_r, u_t, u_z = block[0], block[1], block[2]
        curl_r = wave * times_unit(u_z) * inv_radius - d_z[1]
        curl_t = d_z[0] - d_r[2]
        curl_z = d_r[1] + (u_t - wave * times_unit(u_r)) * inv_radius
        for f, values in enumerate((u_r, u_t, u_z, curl_r, curl_t, curl_z)):
            high, low = split(values)
            rows = slice(f * R, (f + 1) * R)
            fields[rows, 0:LANES] = high
            fields[rows, LANES : 2 * LANES] = low
            fields[rows, 2 * LANES :] = high
        terms = dot(fields[...], to_planes[source])
        if first:
            planes[...] = terms
        else:
            planes[...] += terms

    add_modes(slots.at[mi], mi, True)

    lid = lid_ref[...].astype(BF16)
    wide = lax.broadcasted_iota(jnp.int32, (LANES // 2, LANES), 1) // 2
    tall = lax.broadcasted_iota(jnp.int32, (LANES // 2, LANES), 0)
    noslip = dot(lid, (wide == tall).astype(BF16))
    side = geo[3 * ER + 1, :, :]
    low_side, high_side = side == 1.0, side == 2.0
    at_low, at_high = (e == 0).astype(F32), (e == n_elem - 1).astype(F32)
    lid_rows = jnp.where(low_side, at_low, 0.0) + jnp.where(high_side, at_high, 0.0)
    sharing = 1.0 + jnp.where(low_side, 1.0 - at_low, 0.0) + jnp.where(high_side, 1.0 - at_high, 0.0)
    wave_own = pair + (mi * (LANES // 2)).astype(F32)
    for s, offset in enumerate((1.0, -1.0, 0.0)):
        square = (wave_own + offset) * (wave_own + offset)
        lid_keep = 1.0 - lid_rows * (noslip if s < 2 else 1.0)
        for g in range(ER):
            fixed = geo[ER + g]
            diag = (fixed + square * geo[2 * ER + g]) * sharing
            jac[s, g] = jnp.where(fixed > 0.0, lid_keep / jnp.where(fixed > 0.0, diag, 1.0), 0.0)

    for off in (1, 3, 2):
        forward[off].wait_recv()
        source = lax.rem(mi + n_modes - off, n_modes)
        add_modes(recv.at[off], source, False)

    block_rows = 16

    def push_rows(step, _):
        start = pl.multiple_of(step * block_rows, block_rows)

        def field(f, cols):
            return planes[pl.ds(pl.multiple_of(f * R + start, block_rows), block_rows), cols]

        geo_rows = geo[3 * ER, pl.ds(start, block_rows), :]
        rad = geo_rows + cell.astype(F32) * (1.0 / ER)
        swirl = SWIRL_SLOPE * rad + SWIRL_CURVE / rad
        swirl = jnp.concatenate([swirl] * 3, axis=1)
        spin = 2.0 * SWIRL_SLOPE
        for cols in (slice(0, 3 * LANES), slice(3 * LANES, 6 * LANES)):
            u_r, u_t, u_z, w_r, w_t, w_z = [field(f, cols) for f in range(6)]
            turned = u_t + swirl
            results = (
                turned * w_z - u_z * w_t + spin * u_t,
                u_z * w_r - u_r * w_z - spin * u_r,
                u_r * w_t - turned * w_r,
            )
            for s, values in enumerate(results):
                high, low = split(values)
                rows = pl.ds(pl.multiple_of(s * R + start, block_rows), block_rows)
                push_hi[rows, cols] = high
                push_lo[rows, cols] = low
        return 0

    lax.fori_loop(0, R // block_rows, push_rows, 0)

    local[6].wait()
    backward = {}
    for off in (2, 1, 3, 0):
        to = lax.rem(mi + off, n_modes)
        two = dot(push_hi[...], to_modes[to])
        one = dot(push_lo[...], to_modes[to, :, 0:LANES])
        result = two[:, :LANES] + (two[:, LANES:] + one)
        for s in range(3):
            if off == 0:
                back[mi, s] = result[s * R : (s + 1) * R]
            else:
                sendb[off, s] = result[s * R : (s + 1) * R]
        if off:
            backward[off] = pltpu.make_async_remote_copy(
                src_ref=sendb.at[off],
                dst_ref=back.at[mi],
                send_sem=bwd_send.at[off],
                recv_sem=bwd_recv.at[off],
                device_id=(to, e),
                device_id_type=MESH,
            )
            backward[off].start()
    local[7].wait()
    for off in (1, 3, 2):
        backward[off].wait_recv()

    for g in range(ER):
        held = slot_ref[0, g]
        force = [LAMBDA_COEF * slots[held, s] + INV_NU * back[held, s] for s in range(3)]
        turned = times_unit(force[1])
        mass = geo[g]
        img[0, 0, g] = mass * (force[0] + turned)
        img[0, 1, g] = mass * (force[0] - turned)
        img[0, 2, g] = mass * force[2]

    face_row = lax.broadcasted_iota(jnp.int32, (ER * PS, 1), 0)
    inner_high = (lax.rem(face_row, PS) == PS - 1) & (face_row < ER * PS - 1)
    inner_low = (lax.rem(face_row, PS) == 0) & (face_row > 0)

    def low_rows():
        return pl.ds(0, PS, stride=PS)

    def high_rows():
        return pl.ds(PS - 1, PS, stride=PS)

    halos = []

    def send_faces(k):
        for s in range(3):
            for g in range(ER):
                rows = slice(g * PS, (g + 1) * PS)
                face_out[k, 0, s, rows, :] = img[k, s, g, low_rows(), :]
                face_out[k, 1, s, rows, :] = img[k, s, g, high_rows(), :]
        pairs = []
        for side_out, who in ((0, below), (1, above)):
            copy = pltpu.make_async_remote_copy(
                src_ref=face_out.at[k, side_out],
                dst_ref=face_in.at[k, 1 - side_out],
                send_sem=halo_send.at[k, side_out],
                recv_sem=halo_recv.at[k, 1 - side_out],
                device_id=(mi, who),
                device_id_type=MESH,
            )
            copy.start()
            pairs.append(copy)
        halos.append(pairs)

    def inner_part(k):
        for s in range(3):
            for g in range(ER):
                vec[k, s, g] = img[k, s, g]
            for g in range(ER - 1):
                shared = img[k, s, g, NODES - PS : NODES, :] + img[k, s, g + 1, 0:PS, :]
                vec[k, s, g, NODES - PS : NODES, :] = shared
                vec[k, s, g + 1, 0:PS, :] = shared
            for g in range(ER):
                vec[k, s, g] = vec[k, s, g] * jac[s, g]

    def outer_part(k):
        for copy in halos[k]:
            copy.wait_recv()
        for side_in, present, row_set in ((0, 1.0 - at_low, low_rows), (1, 1.0 - at_high, high_rows)):
            for s in range(3):
                values = face_in[k, side_in, s]
                values = values + jnp.where(inner_high, pltpu.roll(values, ER * PS - 1, 0), 0.0)
                after = face_in[k, side_in, s]
                values = values + jnp.where(inner_low, pltpu.roll(after, 1, 0), 0.0)
                values = values * present
                for g in range(ER):
                    part = values[g * PS : (g + 1) * PS] * jac[s, g, row_set(), :]
                    vec[k, s, g, row_set(), :] = vec[k, s, g, row_set(), :] + part

    def apply_stiff(k):
        for g in range(ER):
            for s in range(3):
                high, low = split(vec[k, s, g])
                cols = slice(s * LANES, (s + 1) * LANES)
                krhs[g, 0:R, cols] = high
                krhs[g, LANES : LANES + R, cols] = low
                krhs[g, 2 * LANES : 2 * LANES + R, cols] = high
            image = dot(stiff[g], krhs[g])
            for s in range(3):
                img[k + 1, s, g] = image[:, s * LANES : (s + 1) * LANES]

    def inner(k, left, right):
        for s in range(3):
            total = jnp.zeros((1, LANES), F32)
            for g in range(ER):
                products = vec[left, s, g] * img[right, s, g]
                total = total + jnp.sum(products, axis=0, keepdims=True)
            index = k * 3 + s
            moment[index // 9, index % 9 : index % 9 + 1, :] = total

    send_faces(0)
    inner_part(0)
    outer_part(0)
    apply_stiff(0)
    send_faces(1)
    inner(0, 0, 0)
    inner(1, 0, 1)
    inner_part(1)
    outer_part(1)
    apply_stiff(1)
    send_faces(2)
    inner(2, 1, 1)
    inner(3, 1, 2)
    inner_part(2)
    outer_part(2)
    apply_stiff(2)
    inner(4, 2, 2)
    inner(5, 2, 3)

    def exchange(buffer, rank, size, member, send_sems, recv_sems):
        copies = []
        for off in range(1, size):
            copy = pltpu.make_async_remote_copy(
                src_ref=buffer.at[rank],
                dst_ref=buffer.at[rank],
                send_sem=send_sems.at[off],
                recv_sem=recv_sems.at[off],
                device_id=(mi, member(lax.rem(rank + off, size))),
                device_id_type=MESH,
            )
            copy.start()
            copies.append(copy)
        for copy in copies:
            copy.wait_recv()
        total = buffer[0]
        for t in range(1, size):
            total = total + buffer[t]
        return total, copies

    red_a[rank_a] = jnp.where(even, pair_sum(moment[0]), pair_sum(moment[1]))
    total, copies_a = exchange(red_a, rank_a, size_a, member_a, a_send, a_recv)
    red_b[zc] = total
    total, copies_b = exchange(red_b, zc, nz, member_b, b_send, b_recv)
    first = jnp.where(even, total, pltpu.roll(total, 1, 1))
    second = jnp.where(even, pltpu.roll(total, LANES - 1, 1), total)

    coefs = []
    for s in range(3):
        h = [(first if k < 3 else second)[(k % 3) * 3 + s : (k % 3) * 3 + s + 1] for k in range(6)]
        g00, g01, g02, g12, g22 = [h[k] + h[k + 1] for k in range(5)]
        g11 = g02
        ratio1, ratio2 = g01 / g00, g02 / g00
        d1 = g11 - ratio1 * g01
        left = g12 - ratio1 * g02
        ratio = left / d1
        d2 = g22 - ratio2 * g02 - ratio * left
        y1 = h[1] - ratio1 * h[0]
        y2 = h[2] - ratio2 * h[0] - ratio * y1
        c2 = y2 / d2
        c1 = y1 / d1 - ratio * c2
        c0 = h[0] / g00 - ratio1 * c1 - ratio2 * c2
        coefs.append((c0, c1, c2))

    for slot in range(ER):
        held = jnp.int32(0)
        for g in range(ER):
            held = jnp.where(slot_ref[0, g] == slot, g, held)
        plus, minus, axial = [
            coefs[s][0] * vec[0, s, held] + coefs[s][1] * vec[1, s, held] + coefs[s][2] * vec[2, s, held]
            for s in range(3)
        ]
        results = ((plus + minus) * 0.5, times_unit(minus - plus) * 0.5, axial)
        for s, values in enumerate(results):
            rows = pl.ds(s * NODES * ER + slot, NODES, stride=ER)
            out_ref[rows, :] = values[:NODES]

    for copies in (forward.values(), backward.values(), copies_a, copies_b, *halos):
        for copy in copies:
            copy.wait_send()


def on_device(grid_shape, velocity, element_slot, lid_noslip):
    ny, nz, nc = grid_shape
    slopes, stiff, geometry, to_planes, to_modes = constants()
    vmem = pltpu.VMEM
    dma = pltpu.SemaphoreType.DMA
    flat = velocity.transpose(0, 2, 3, 1, 4).reshape(3 * NODES * ER, LANES)
    result = pl.pallas_call(
        functools.partial(kernel, grid_shape),
        out_shape=jax.ShapeDtypeStruct((3 * NODES * ER, LANES), F32),
        in_specs=[pl.BlockSpec(memory_space=pltpu.HBM)] * 8,
        out_specs=pl.BlockSpec(memory_space=vmem),
        scratch_shapes=[
            pltpu.SMEM((1, ER), jnp.int32),
            vmem((1, LANES // 2), jnp.int32),
            vmem((3 * NODES * ER, LANES), F32),
            vmem((ER, 3, R, LANES), F32),
            vmem((ER, 3, R, LANES), F32),
            vmem(slopes.shape, BF16),
            vmem(stiff.shape, BF16),
            vmem(geometry.shape, F32),
            vmem(to_planes.shape, BF16),
            vmem(to_modes.shape, BF16),
            vmem((3 * LANES, 3 * LANES), BF16),
            vmem((6 * R, 3 * LANES), BF16),
            vmem((6 * R, Q), F32),
            vmem((3 * R, Q), BF16),
            vmem((3 * R, Q), BF16),
            vmem((ER, 3, R, LANES), F32),
            vmem((ER, 3, R, LANES), F32),
            vmem((3, ER, R, LANES), F32),
            vmem((3, 3, ER, R, LANES), F32),
            vmem((4, 3, ER, R, LANES), F32),
            vmem((ER, 3 * LANES, 3 * LANES), BF16),
            vmem((3, 2, 3, ER * PS, LANES), F32),
            vmem((3, 2, 3, ER * PS, LANES), F32),
            vmem((2, 16, LANES), F32),
            vmem((ny * nc, 16, LANES), F32),
            vmem((nz, 16, LANES), F32),
            dma((8,)),
            dma((ER,)),
            dma((ER,)),
            dma((ER,)),
            dma((ER,)),
            dma((3, 2)),
            dma((3, 2)),
            dma((ny * nc,)),
            dma((ny * nc,)),
            dma((nz,)),
            dma((nz,)),
        ],
        compiler_params=pltpu.CompilerParams(
            collective_id=0, has_side_effects=True, vmem_limit_bytes=62 * 1024 * 1024
        ),
    )(
        element_slot,
        lid_noslip.reshape(1, -1),
        flat,
        jnp.asarray(slopes),
        jnp.asarray(stiff),
        jnp.asarray(geometry),
        jnp.asarray(to_planes),
        jnp.asarray(to_modes),
    )
    return result.reshape(3, PS, PS, ER, LANES).transpose(0, 3, 1, 2, 4)


def solution(mesh):
    n_elem = mesh.shape["elem"]
    nc = 2
    nz = min(8, n_elem // nc)
    ny = n_elem // (nc * nz)
    return jax.shard_map(
        functools.partial(on_device, (ny, nz, nc)),
        mesh=mesh,
        in_specs=(P(None, "elem", None, None, "modes"), P("elem", None), P("modes")),
        out_specs=P(None, "elem", None, None, "modes"),
        check_vma=False,
    )
```

```python
import functools

import jax
import jax.numpy as jnp
import ml_dtypes
import numpy as np
from jax import lax
from jax.experimental import pallas as pl
from jax.experimental.pallas import tpu as pltpu
from jax.sharding import PartitionSpec as P

PS = 10
NODES = PS * PS
R = 112
SENT = 104
TOP = 88
FACE = 16
MID = TOP - FACE
BULK = 80
M = 256
Q = 768
ER = 4
LANES = 128
LAMBDA_COEF = 20.0
INV_NU = 10.0
R_INNER = 1.0
SWIRL_SLOPE = -1.0 / 3.0
SWIRL_CURVE = 4.0 / 3.0
MESH = pl.DeviceIdType.MESH
F32 = jnp.float32
BF16 = jnp.bfloat16


def legendre_rows(abscissa, degree):
    table_rows = [abscissa * 0.0 + 1.0, abscissa.copy()]
    for degree_now in range(2, degree + 1):
        table_rows.append(
            ((2 * degree_now - 1) * abscissa * table_rows[-1] - (degree_now - 1) * table_rows[-2])
            / degree_now
        )
    return table_rows


def gll_tables(points):
    degree = points - 1
    abscissa = -np.cos(np.pi * np.arange(points) / degree)
    for _ in range(60):
        legendre = legendre_rows(abscissa, degree)
        abscissa = abscissa - (abscissa * legendre[degree] - legendre[degree - 1]) / (
            points * legendre[degree]
        )
    legendre = legendre_rows(abscissa, degree)
    last_row = legendre[degree]
    weights = 2.0 / (degree * points * last_row**2)
    identity = np.eye(points)
    distance = abscissa[:, None] - abscissa[None, :] + identity
    derivative = last_row[:, None] / (last_row[None, :] * distance) * (1.0 - identity)
    derivative[0, 0] = -degree * points / 4.0
    derivative[degree, degree] = degree * points / 4.0
    return abscissa, weights, derivative


def halves(values):
    high = values.astype(ml_dtypes.bfloat16)
    low = (values - high.astype(np.float64)).astype(ml_dtypes.bfloat16)
    return high, low


@functools.cache
def constants():
    xi, w, deriv = gll_tables(PS)
    eye = np.eye(PS)
    radius = R_INNER + (np.arange(ER)[:, None] + 0.5 * (xi[None, :] + 1.0)) / ER
    ww = np.outer(w, w)

    def operator(rows):
        padded = np.zeros((R, LANES))
        padded[:NODES, :NODES] = rows
        high, low = halves(padded)
        return np.concatenate([high, high, low], axis=1)

    slope_r = operator(2.0 * ER * np.kron(eye, deriv))
    slope_z = operator(2.0 * ER * np.kron(deriv, eye))
    slopes = np.concatenate([slope_r, slope_z], axis=0)

    stiff, stiff_diag = [], np.zeros((ER, PS, PS))
    for ir in range(ER):
        along_i = deriv.T @ np.diag(w * radius[ir]) @ deriv
        along_j = deriv.T @ np.diag(w) @ deriv
        whole = np.kron(np.diag(w), along_i) + np.kron(along_j, np.diag(w * radius[ir]))
        stiff_diag[ir] = np.diag(whole).reshape(PS, PS).T
        stiff.append(operator(whole - np.diag(np.diag(whole))))
    stiff = np.stack(stiff)

    quarter_h = 0.25 / (ER * ER)
    mass_r = ww[None] * quarter_h * radius[:, :, None]
    mass_over_r = ww[None] * quarter_h / radius[:, :, None]

    def radial_sum(values):
        total = values.copy()
        total[:-1, -1] += values[1:, 0]
        total[1:, 0] += values[:-1, -1]
        return total

    diag_fixed = radial_sum(stiff_diag + LAMBDA_COEF * mass_r)
    diag_square = radial_sum(mass_over_r)
    diag_fixed[0, 0] = 0.0
    diag_fixed[-1, -1] = 0.0

    geometry = np.zeros((3 * ER + 2, R, LANES))
    for part, values in enumerate((mass_r, diag_fixed, diag_square)):
        rows = values.transpose(0, 2, 1).reshape(ER, NODES, 1)
        geometry[part * ER : (part + 1) * ER, :NODES] = rows
    geometry[3 * ER] = 1.0
    geometry[3 * ER, :NODES] = (R_INNER + 0.5 * (np.tile(xi, PS) + 1.0) / ER)[:, None]
    geometry[3 * ER + 1, :PS] = 1.0
    geometry[3 * ER + 1, NODES - PS : NODES] = 2.0

    modes = np.arange(M)
    angles = (modes[:, None] * np.arange(Q)[None, :] % Q) * (2.0 * np.pi / Q)
    weight = np.where(modes == 0, 1.0, 2.0)[:, None]
    inverse = np.stack([weight * np.cos(angles), -weight * np.sin(angles)], axis=1)
    inverse = inverse.reshape(2 * M // LANES, LANES, Q)
    high, low = halves(inverse)
    to_planes = np.concatenate([high, high, low], axis=1)
    forward = np.stack([np.cos(angles), -np.sin(angles)], axis=1) / Q
    forward = forward.reshape(2 * M // LANES, LANES, Q).transpose(0, 2, 1)
    high, low = halves(forward)
    to_modes = np.concatenate([high, low], axis=2)
    return slopes, stiff, geometry.astype(np.float32), to_planes, to_modes


def split(values):
    high = values.astype(BF16)
    low = (values - high.astype(F32)).astype(BF16)
    return high, low


def dot(left, right):
    return jnp.dot(left, right, preferred_element_type=F32)


def kernel(
    grid_shape,
    slot_hbm,
    lid_hbm,
    vel_hbm,
    slopes_hbm,
    stiff_hbm,
    geo_hbm,
    planes_hbm,
    modes_hbm,
    out_ref,
    slot_ref,
    lid_ref,
    vel_r,
    vel_t,
    vel_z,
    cells,
    recv,
    slopes,
    stiff,
    geo,
    to_planes,
    to_modes,
    rhs,
    fields,
    planes,
    push_hi,
    push_lo,
    side_hi,
    side_lo,
    sendb,
    back,
    side_out,
    side_in,
    side_send,
    side_back,
    jac,
    vec,
    img,
    krhs,
    face_in,
    moment,
    red_a,
    red_b,
    local_sem,
    fwd_send,
    fwd_recv,
    bwd_send,
    bwd_recv,
    side_sems,
    fb_send,
    fb_recv,
    halo_send,
    halo_recv,
    a_send,
    a_recv,
    b_send,
    b_recv,
):
    ny, nz, nc = grid_shape
    n_elem = ny * nz * nc
    n_modes = ER
    mi = lax.axis_index("modes")
    e = lax.axis_index("elem")
    core = lax.rem(e, nc)
    zc = lax.rem(e // nc, nz)
    yc = e // (nc * nz)
    size_a = ny * nc
    rank_a = yc * nc + core

    def member_a(t):
        return ((t // nc) * nz + zc) * nc + lax.rem(t, nc)

    def member_b(t):
        return (yc * nz + t) * nc + core

    above = lax.rem(e + 1, n_elem)
    below = lax.rem(e + n_elem - 1, n_elem)

    span = NODES * ER
    vel = (vel_r, vel_t, vel_z)
    local_pairs = [
        *[
            (vel_hbm.at[pl.ds(s * span, span)], vel[s])
            for s in range(3)
        ],
        (slopes_hbm, slopes),
        (planes_hbm, to_planes),
        (geo_hbm, geo),
        (slot_hbm, slot_ref),
        (lid_hbm, lid_ref),
        (modes_hbm, to_modes),
        (stiff_hbm, stiff),
    ]
    local = [
        pltpu.make_async_copy(src, dst, local_sem.at[i]) for i, (src, dst) in enumerate(local_pairs)
    ]
    for copy in local:
        copy.start()

    for g in range(ER):
        for s in range(3):
            cells[g, s, R - 16 :, :] = jnp.zeros((16, LANES), F32)
            recv[g, s, R - 16 :, :] = jnp.zeros((16, LANES), F32)
            img[0, s, g, SENT:, :] = jnp.zeros((R - SENT, LANES), F32)
    no_rows = jnp.zeros((LANES - R, 3 * LANES), BF16)
    for part in range(3):
        rhs[part * LANES + R : (part + 1) * LANES, :] = no_rows
        for g in range(ER):
            krhs[g, part * LANES + R : (part + 1) * LANES, :] = no_rows
    moment[...] = jnp.zeros_like(moment)

    def gather_cell(g, s, target):
        held = slot_ref[0, g]
        for j in range(PS):
            rows = pl.ds(j * ER + held, PS, stride=ER * PS)
            target[g, s, j * PS : (j + 1) * PS, :] = vel[s][rows, :]

    barrier = pltpu.get_barrier_semaphore()
    greeted = [(lax.rem(mi + t, n_modes), e) for t in range(1, n_modes)]
    greeted += [(mi, above), (mi, below)]
    greeted += [(mi, member_a(lax.rem(rank_a + t, size_a))) for t in range(1, size_a)]
    greeted += [(mi, member_b(lax.rem(zc + t, nz))) for t in range(1, nz)]
    for who in greeted:
        pl.semaphore_signal(barrier, inc=1, device_id=who, device_id_type=MESH)
    pl.semaphore_wait(barrier, len(greeted))

    forward = {}
    local[6].wait()
    for s in range(3):
        local[s].wait()
        for off in (2, 1, 3):
            to = lax.rem(mi + off, n_modes)
            gather_cell(to, s, cells)
            forward[off, s] = pltpu.make_async_remote_copy(
                src_ref=cells.at[to, s, pl.ds(0, SENT)],
                dst_ref=recv.at[mi, s, pl.ds(0, SENT)],
                send_sem=fwd_send.at[off, s],
                recv_sem=fwd_recv.at[off, s],
                device_id=(to, e),
                device_id_type=MESH,
            )
            forward[off, s].start()

    lane = lax.broadcasted_iota(jnp.int32, (1, LANES), 1)
    even = lax.rem(lane, 2) == 0
    pair = (lane // 2).astype(F32)

    def times_unit(values):
        return jnp.where(even, -pltpu.roll(values, LANES - 1, 1), pltpu.roll(values, 1, 1))

    def pair_sum(values):
        return values + jnp.where(even, pltpu.roll(values, LANES - 1, 1), pltpu.roll(values, 1, 1))

    for s in range(3):
        gather_cell(mi, s, recv)
    for copy in (*local[3:6], local[7]):
        copy.wait()

    cell_radius = mi.astype(F32) * (1.0 / ER)
    radius = geo[3 * ER, :, :] + cell_radius
    inv_radius = 1.0 / radius
    swirl_base = SWIRL_SLOPE * radius + SWIRL_CURVE * inv_radius

    def add_modes(block, source, first):
        for s in range(3):
            high, low = split(block[s])
            cols = slice(s * LANES, (s + 1) * LANES)
            rhs[0:R, cols] = high
            rhs[LANES : LANES + R, cols] = low
            rhs[2 * LANES : 2 * LANES + R, cols] = high
        slope = dot(slopes[...], rhs[...])
        d_r = [slope[:R, s * LANES : (s + 1) * LANES] for s in range(3)]
        d_z = [slope[R:, s * LANES : (s + 1) * LANES] for s in range(3)]
        wave = pair + (source * (LANES // 2)).astype(F32)
        u_r, u_t, u_z = block[0], block[1], block[2]
        curl_r = wave * times_unit(u_z) * inv_radius - d_z[1]
        curl_t = d_z[0] - d_r[2]
        curl_z = d_r[1] + (u_t - wave * times_unit(u_r)) * inv_radius
        for f, values in enumerate((u_r, u_t, u_z, curl_r, curl_t, curl_z)):
            high, low = split(values)
            rows = slice(f * R, (f + 1) * R)
            fields[rows, 0:LANES] = high
            fields[rows, LANES : 2 * LANES] = low
            fields[rows, 2 * LANES :] = high
        terms = dot(fields[...], to_planes[source])
        if first:
            planes[...] = terms
        else:
            planes[...] += terms

    add_modes(recv.at[mi], mi, True)

    lid = lid_ref[...].astype(BF16)
    wide = lax.broadcasted_iota(jnp.int32, (LANES // 2, LANES), 1) // 2
    tall = lax.broadcasted_iota(jnp.int32, (LANES // 2, LANES), 0)
    noslip = dot(lid, (wide == tall).astype(BF16))
    side = geo[3 * ER + 1, :, :]
    low_side, high_side = side == 1.0, side == 2.0
    at_low, at_high = (e == 0).astype(F32), (e == n_elem - 1).astype(F32)
    lid_rows = jnp.where(low_side, at_low, 0.0) + jnp.where(high_side, at_high, 0.0)
    sharing = 1.0 + jnp.where(low_side, 1.0 - at_low, 0.0) + jnp.where(high_side, 1.0 - at_high, 0.0)
    wave_own = pair + (mi * (LANES // 2)).astype(F32)
    for s, offset in enumerate((1.0, -1.0, 0.0)):
        square = (wave_own + offset) * (wave_own + offset)
        lid_keep = 1.0 - lid_rows * (noslip if s < 2 else 1.0)
        for g in range(ER):
            fixed = geo[ER + g]
            diag = (fixed + square * geo[2 * ER + g]) * sharing
            jac[s, g] = jnp.where(fixed > 0.0, lid_keep / jnp.where(fixed > 0.0, diag, 1.0), 0.0)

    for off in (1, 3, 2):
        for s in range(3):
            forward[off, s].wait_recv()
        source = lax.rem(mi + n_modes - off, n_modes)
        add_modes(recv.at[source], source, False)

    def push_rows(start, to_hi, to_lo, first, pitch):
        def field(f, cols):
            return planes[pl.ds(pl.multiple_of(f * R + start, 8), FACE), cols]

        rad = geo[3 * ER, pl.ds(start, FACE), :] + cell_radius
        swirl = SWIRL_SLOPE * rad + SWIRL_CURVE / rad
        swirl = jnp.concatenate([swirl] * 3, axis=1)
        spin = 2.0 * SWIRL_SLOPE
        for cols in (slice(0, 3 * LANES), slice(3 * LANES, 6 * LANES)):
            u_r, u_t, u_z, w_r, w_t, w_z = [field(f, cols) for f in range(6)]
            turned = u_t + swirl
            results = (
                turned * w_z - u_z * w_t + spin * u_t,
                u_z * w_r - u_r * w_z - spin * u_r,
                u_r * w_t - turned * w_r,
            )
            for s, values in enumerate(results):
                high, low = split(values)
                rows = pl.ds(pl.multiple_of(first + s * pitch, FACE), FACE)
                to_hi[rows, cols] = high
                to_lo[rows, cols] = low

    def bulk_step(step, _):
        start = pl.multiple_of(step * FACE, FACE)
        push_rows(start + FACE, push_hi, push_lo, start, BULK)
        return 0

    lax.fori_loop(0, BULK // FACE, bulk_step, 0)

    def coefficients(high, low, chunk):
        two = dot(high[...], to_modes[chunk])
        one = dot(low[...], to_modes[chunk, :, 0:LANES])
        return INV_NU * (two[:, :LANES] + (two[:, LANES:] + one))

    backward = {}

    def return_bulk(off):
        to = lax.rem(mi + off, n_modes)
        result = coefficients(push_hi, push_lo, to)
        for s in range(3):
            force = result[s * BULK : (s + 1) * BULK] + LAMBDA_COEF * recv[to, s, FACE : FACE + BULK, :]
            if off == 0:
                back[mi, s] = force
            else:
                sendb[off, s] = force
        if off:
            backward[off] = pltpu.make_async_remote_copy(
                src_ref=sendb.at[off, :, pl.ds(0, MID)],
                dst_ref=back.at[mi, :, pl.ds(0, MID)],
                send_sem=bwd_send.at[off],
                recv_sem=bwd_recv.at[off],
                device_id=(to, e),
                device_id_type=MESH,
            )
            backward[off].start()

    local[8].wait()
    return_bulk(2)
    for side, start in enumerate((0, TOP)):
        push_rows(start, side_hi, side_lo, side * FACE, 2 * FACE)
    for chunk in range(n_modes):
        result = coefficients(side_hi, side_lo, chunk)
        for s in range(3):
            for side, start in enumerate((0, TOP)):
                rows = slice((2 * s + side) * FACE, (2 * s + side + 1) * FACE)
                force = result[rows] + LAMBDA_COEF * recv[chunk, s, start : start + FACE, :]
                side_out[side, chunk, s] = force
    side_copies = []
    for side, who in ((0, below), (1, above)):
        copy = pltpu.make_async_remote_copy(
            src_ref=side_out.at[side],
            dst_ref=side_in.at[1 - side],
            send_sem=side_sems.at[0, side],
            recv_sem=side_sems.at[1, 1 - side],
            device_id=(mi, who),
            device_id_type=MESH,
        )
        copy.start()
        side_copies.append(copy)
    for off in (1, 3, 0):
        return_bulk(off)

    block_row = lax.broadcasted_iota(jnp.int32, (FACE, LANES), 0)
    met = (
        jnp.where(block_row < PS, 1.0 - at_low, 0.0),
        jnp.where((block_row >= 2) & (block_row < 2 + PS), 1.0 - at_high, 0.0),
    )

    def meet(side, other):
        return met[side] * pltpu.roll(other, 2 if side else FACE - 2, 0)

    for copy in side_copies:
        copy.wait_recv()
    side_returns = []
    for off in (2, 1, 3, 0):
        to = lax.rem(mi + off, n_modes)
        for s in range(3):
            for side in range(2):
                total = side_out[side, to, s] + meet(side, side_in[side, to, s])
                if off == 0:
                    side_back[mi, s, side] = total
                else:
                    side_send[off, s, side] = total
        if off:
            copy = pltpu.make_async_remote_copy(
                src_ref=side_send.at[off],
                dst_ref=side_back.at[mi],
                send_sem=fb_send.at[off],
                recv_sem=fb_recv.at[off],
                device_id=(to, e),
                device_id_type=MESH,
            )
            copy.start()
            side_returns.append(copy)
    local[9].wait()
    for off in (1, 3, 2):
        backward[off].wait_recv()
    for copy in side_returns:
        copy.wait_recv()

    for g in range(ER):
        pieces = (
            (slice(0, FACE), [side_back[g, s, 0] for s in range(3)]),
            (slice(FACE, TOP), [back[g, s, 0:MID, :] for s in range(3)]),
            (slice(TOP, SENT), [side_back[g, s, 1] for s in range(3)]),
        )
        for rows, force in pieces:
            turned = times_unit(force[1])
            mass = geo[g, rows, :]
            img[0, 0, g, rows, :] = mass * (force[0] + turned)
            img[0, 1, g, rows, :] = mass * (force[0] - turned)
            img[0, 2, g, rows, :] = mass * force[2]

    halos = []

    def send_faces(k):
        pairs = []
        for side, start, who in ((0, 0, below), (1, TOP, above)):
            copy = pltpu.make_async_remote_copy(
                src_ref=img.at[k, :, :, pl.ds(start, FACE)],
                dst_ref=face_in.at[k - 1, 1 - side],
                send_sem=halo_send.at[k - 1, side],
                recv_sem=halo_recv.at[k - 1, 1 - side],
                device_id=(mi, who),
                device_id_type=MESH,
            )
            copy.start()
            pairs.append(copy)
        halos.append(pairs)

    def inner_part(k):
        for s in range(3):
            for g in range(ER):
                vec[k, s, g] = img[k, s, g]
            for g in range(ER - 1):
                last = pl.ds(2 * PS - 1, PS - 2, stride=PS)
                first = pl.ds(PS, PS - 2, stride=PS)
                shared = img[k, s, g, last, :] + img[k, s, g + 1, first, :]
                vec[k, s, g, last, :] = shared
                vec[k, s, g + 1, first, :] = shared
            for g in range(ER):
                vec[k, s, g, FACE:TOP, :] = vec[k, s, g, FACE:TOP, :] * jac[s, g, FACE:TOP, :]

    def outer_part(k):
        if k > 0:
            for copy in halos[k - 1]:
                copy.wait_recv()
        for side, start, last in ((0, 0, PS - 1), (1, TOP, PS + 1)):
            rows = slice(start, start + FACE)
            for s in range(3):
                block = [vec[k, s, g, rows, :] for g in range(ER)]
                if k > 0:
                    block = [block[g] + meet(side, face_in[k - 1, side, s, g]) for g in range(ER)]
                for g in range(ER):
                    total = block[g]
                    if g + 1 < ER:
                        nearby = pltpu.roll(block[g + 1], PS - 1, 0)
                        total = total + jnp.where(block_row == last, nearby, 0.0)
                    if g > 0:
                        nearby = pltpu.roll(block[g - 1], FACE - PS + 1, 0)
                        total = total + jnp.where(block_row == last - PS + 1, nearby, 0.0)
                    vec[k, s, g, rows, :] = total * jac[s, g, rows, :]

    def apply_stiff(k):
        for g in range(ER):
            for s in range(3):
                high, low = split(vec[k, s, g])
                cols = slice(s * LANES, (s + 1) * LANES)
                krhs[g, 0:R, cols] = high
                krhs[g, LANES : LANES + R, cols] = low
                krhs[g, 2 * LANES : 2 * LANES + R, cols] = high
            image = dot(stiff[g], krhs[g])
            for s in range(3):
                img[k + 1, s, g] = image[:, s * LANES : (s + 1) * LANES]

    share = 1.0 / sharing

    def inner(k, left, right):
        for s in range(3):
            total = jnp.zeros((1, LANES), F32)
            for g in range(ER):
                products = vec[left, s, g] * img[right, s, g]
                if right == 0:
                    products = products * share
                total = total + jnp.sum(products, axis=0, keepdims=True)
            index = k * 3 + s
            moment[index // 9, index % 9 : index % 9 + 1, :] = total

    inner_part(0)
    outer_part(0)
    apply_stiff(0)
    send_faces(1)
    inner(0, 0, 0)
    inner(1, 0, 1)
    inner_part(1)
    outer_part(1)
    apply_stiff(1)
    send_faces(2)
    inner(2, 1, 1)
    inner(3, 1, 2)
    inner_part(2)
    outer_part(2)
    apply_stiff(2)
    inner(4, 2, 2)
    inner(5, 2, 3)

    def exchange(buffer, rank, size, member, send_sems, recv_sems):
        copies = []
        for off in range(1, size):
            copy = pltpu.make_async_remote_copy(
                src_ref=buffer.at[rank],
                dst_ref=buffer.at[rank],
                send_sem=send_sems.at[off],
                recv_sem=recv_sems.at[off],
                device_id=(mi, member(lax.rem(rank + off, size))),
                device_id_type=MESH,
            )
            copy.start()
            copies.append(copy)
        for copy in copies:
            copy.wait_recv()
        total = buffer[0]
        for t in range(1, size):
            total = total + buffer[t]
        return total, copies

    red_a[rank_a] = jnp.where(even, pair_sum(moment[0]), pair_sum(moment[1]))
    total, copies_a = exchange(red_a, rank_a, size_a, member_a, a_send, a_recv)
    red_b[zc] = total
    total, copies_b = exchange(red_b, zc, nz, member_b, b_send, b_recv)
    first = jnp.where(even, total, pltpu.roll(total, 1, 1))
    second = jnp.where(even, pltpu.roll(total, LANES - 1, 1), total)

    coefs = []
    for s in range(3):
        h = [(first if k < 3 else second)[(k % 3) * 3 + s : (k % 3) * 3 + s + 1] for k in range(6)]
        g00, g01, g02, g12, g22 = [h[k] + h[k + 1] for k in range(5)]
        g11 = g02
        ratio1, ratio2 = g01 / g00, g02 / g00
        d1 = g11 - ratio1 * g01
        left = g12 - ratio1 * g02
        ratio = left / d1
        d2 = g22 - ratio2 * g02 - ratio * left
        y1 = h[1] - ratio1 * h[0]
        y2 = h[2] - ratio2 * h[0] - ratio * y1
        c2 = y2 / d2
        c1 = y1 / d1 - ratio * c2
        c0 = h[0] / g00 - ratio1 * c1 - ratio2 * c2
        coefs.append((c0, c1, c2))

    for slot in range(ER):
        held = jnp.int32(0)
        for g in range(ER):
            held = jnp.where(slot_ref[0, g] == slot, g, held)
        plus, minus, axial = [
            coefs[s][0] * vec[0, s, held] + coefs[s][1] * vec[1, s, held] + coefs[s][2] * vec[2, s, held]
            for s in range(3)
        ]
        results = ((plus + minus) * 0.5, times_unit(minus - plus) * 0.5, axial)
        for s, values in enumerate(results):
            for j in range(PS):
                rows = pl.ds(s * span + j * ER + slot, PS, stride=ER * PS)
                out_ref[rows, :] = values[j * PS : (j + 1) * PS]

    sent = (forward.values(), backward.values(), side_copies, side_returns, copies_a, copies_b)
    for copies in (*sent, *halos):
        for copy in copies:
            copy.wait_send()


def on_device(grid_shape, velocity, element_slot, lid_noslip):
    ny, nz, nc = grid_shape
    slopes, stiff, geometry, to_planes, to_modes = constants()
    vmem = pltpu.VMEM
    dma = pltpu.SemaphoreType.DMA
    flat = velocity.transpose(0, 2, 3, 1, 4).reshape(3 * NODES * ER, LANES)
    result = pl.pallas_call(
        functools.partial(kernel, grid_shape),
        out_shape=jax.ShapeDtypeStruct((3 * NODES * ER, LANES), F32),
        in_specs=[pl.BlockSpec(memory_space=pltpu.HBM)] * 8,
        out_specs=pl.BlockSpec(memory_space=vmem),
        scratch_shapes=[
            pltpu.SMEM((1, ER), jnp.int32),
            vmem((1, LANES // 2), jnp.int32),
            *[vmem((NODES * ER, LANES), F32)] * 3,
            vmem((ER, 3, R, LANES), F32),
            vmem((ER, 3, R, LANES), F32),
            vmem(slopes.shape, BF16),
            vmem(stiff.shape, BF16),
            vmem(geometry.shape, F32),
            vmem(to_planes.shape, BF16),
            vmem(to_modes.shape, BF16),
            vmem((3 * LANES, 3 * LANES), BF16),
            vmem((6 * R, 3 * LANES), BF16),
            vmem((6 * R, Q), F32),
            vmem((3 * BULK, Q), BF16),
            vmem((3 * BULK, Q), BF16),
            vmem((6 * FACE, Q), BF16),
            vmem((6 * FACE, Q), BF16),
            vmem((ER, 3, BULK, LANES), F32),
            vmem((ER, 3, BULK, LANES), F32),
            vmem((2, ER, 3, FACE, LANES), F32),
            vmem((2, ER, 3, FACE, LANES), F32),
            vmem((ER, 3, 2, FACE, LANES), F32),
            vmem((ER, 3, 2, FACE, LANES), F32),
            vmem((3, ER, R, LANES), F32),
            vmem((3, 3, ER, R, LANES), F32),
            vmem((4, 3, ER, R, LANES), F32),
            vmem((ER, 3 * LANES, 3 * LANES), BF16),
            vmem((2, 2, 3, ER, FACE, LANES), F32),
            vmem((2, 16, LANES), F32),
            vmem((ny * nc, 16, LANES), F32),
            vmem((nz, 16, LANES), F32),
            dma((10,)),
            dma((ER, 3)),
            dma((ER, 3)),
            dma((ER,)),
            dma((ER,)),
            dma((2, 2)),
            dma((ER,)),
            dma((ER,)),
            dma((2, 2)),
            dma((2, 2)),
            dma((ny * nc,)),
            dma((ny * nc,)),
            dma((nz,)),
            dma((nz,)),
        ],
        compiler_params=pltpu.CompilerParams(
            collective_id=0, has_side_effects=True, vmem_limit_bytes=62 * 1024 * 1024
        ),
    )(
        element_slot,
        lid_noslip.reshape(1, -1),
        flat,
        jnp.asarray(slopes),
        jnp.asarray(stiff),
        jnp.asarray(geometry),
        jnp.asarray(to_planes),
        jnp.asarray(to_modes),
    )
    return result.reshape(3, PS, PS, ER, LANES).transpose(0, 3, 1, 2, 4)


def solution(mesh):
    n_elem = mesh.shape["elem"]
    nc = 2
    nz = min(8, n_elem // nc)
    ny = n_elem // (nc * nz)
    return jax.shard_map(
        functools.partial(on_device, (ny, nz, nc)),
        mesh=mesh,
        in_specs=(P(None, "elem", None, None, "modes"), P("elem", None), P("modes")),
        out_specs=P(None, "elem", None, None, "modes"),
        check_vma=False,
    )
```

```python
import functools

import jax
import jax.numpy as jnp
import ml_dtypes
import numpy as np
from jax import lax
from jax.experimental import pallas as pl
from jax.experimental.pallas import tpu as pltpu
from jax.sharding import PartitionSpec as P

PS = 10
NODES = PS * PS
R = 112
SENT = 104
TOP = 88
FACE = 16
MID = TOP - FACE
BULK = 80
M = 256
Q = 768
ER = 4
LANES = 128
LAMBDA_COEF = 20.0
INV_NU = 10.0
R_INNER = 1.0
SWIRL_SLOPE = -1.0 / 3.0
SWIRL_CURVE = 4.0 / 3.0
MESH = pl.DeviceIdType.MESH
F32 = jnp.float32
BF16 = jnp.bfloat16


def legendre_rows(abscissa, degree):
    table_rows = [abscissa * 0.0 + 1.0, abscissa.copy()]
    for degree_now in range(2, degree + 1):
        table_rows.append(
            ((2 * degree_now - 1) * abscissa * table_rows[-1] - (degree_now - 1) * table_rows[-2])
            / degree_now
        )
    return table_rows


def gll_tables(points):
    degree = points - 1
    abscissa = -np.cos(np.pi * np.arange(points) / degree)
    for _ in range(60):
        legendre = legendre_rows(abscissa, degree)
        abscissa = abscissa - (abscissa * legendre[degree] - legendre[degree - 1]) / (
            points * legendre[degree]
        )
    legendre = legendre_rows(abscissa, degree)
    last_row = legendre[degree]
    weights = 2.0 / (degree * points * last_row**2)
    identity = np.eye(points)
    distance = abscissa[:, None] - abscissa[None, :] + identity
    derivative = last_row[:, None] / (last_row[None, :] * distance) * (1.0 - identity)
    derivative[0, 0] = -degree * points / 4.0
    derivative[degree, degree] = degree * points / 4.0
    return abscissa, weights, derivative


def halves(values):
    high = values.astype(ml_dtypes.bfloat16)
    low = (values - high.astype(np.float64)).astype(ml_dtypes.bfloat16)
    return high, low


@functools.cache
def constants():
    xi, w, deriv = gll_tables(PS)
    eye = np.eye(PS)
    radius = R_INNER + (np.arange(ER)[:, None] + 0.5 * (xi[None, :] + 1.0)) / ER
    ww = np.outer(w, w)

    def operator(rows):
        padded = np.zeros((R, LANES))
        padded[:NODES, :NODES] = rows
        high, low = halves(padded)
        return np.concatenate([high, high, low], axis=1)

    slope_r = operator(2.0 * ER * np.kron(eye, deriv))
    slope_z = operator(2.0 * ER * np.kron(deriv, eye))
    slopes = np.concatenate([slope_r, slope_z], axis=0)

    stiff, stiff_diag = [], np.zeros((ER, PS, PS))
    for ir in range(ER):
        along_i = deriv.T @ np.diag(w * radius[ir]) @ deriv
        along_j = deriv.T @ np.diag(w) @ deriv
        whole = np.kron(np.diag(w), along_i) + np.kron(along_j, np.diag(w * radius[ir]))
        stiff_diag[ir] = np.diag(whole).reshape(PS, PS).T
        stiff.append(operator(whole - np.diag(np.diag(whole))))
    stiff = np.stack(stiff)

    quarter_h = 0.25 / (ER * ER)
    mass_r = ww[None] * quarter_h * radius[:, :, None]
    mass_over_r = ww[None] * quarter_h / radius[:, :, None]

    def radial_sum(values):
        total = values.copy()
        total[:-1, -1] += values[1:, 0]
        total[1:, 0] += values[:-1, -1]
        return total

    diag_fixed = radial_sum(stiff_diag + LAMBDA_COEF * mass_r)
    diag_square = radial_sum(mass_over_r)
    diag_fixed[0, 0] = 0.0
    diag_fixed[-1, -1] = 0.0

    geometry = np.zeros((3 * ER + 2, R, LANES))
    for part, values in enumerate((mass_r, diag_fixed, diag_square)):
        rows = values.transpose(0, 2, 1).reshape(ER, NODES, 1)
        geometry[part * ER : (part + 1) * ER, :NODES] = rows
    geometry[3 * ER] = 1.0
    geometry[3 * ER, :NODES] = (R_INNER + 0.5 * (np.tile(xi, PS) + 1.0) / ER)[:, None]
    geometry[3 * ER + 1, :PS] = 1.0
    geometry[3 * ER + 1, NODES - PS : NODES] = 2.0

    modes = np.arange(M)
    angles = (modes[:, None] * np.arange(Q)[None, :] % Q) * (2.0 * np.pi / Q)
    weight = np.where(modes == 0, 1.0, 2.0)[:, None]
    inverse = np.stack([weight * np.cos(angles), -weight * np.sin(angles)], axis=1)
    inverse = inverse.reshape(2 * M // LANES, LANES, Q)
    high, low = halves(inverse)
    to_planes = np.concatenate([high, high, low], axis=1)
    forward = np.stack([np.cos(angles), -np.sin(angles)], axis=1) / Q
    forward = forward.reshape(2 * M // LANES, LANES, Q).transpose(0, 2, 1)
    high, low = halves(forward)
    to_modes = np.concatenate([high, low], axis=2)
    return slopes, stiff, geometry.astype(np.float32), to_planes, to_modes


def split(values):
    high = values.astype(BF16)
    low = (values - high.astype(F32)).astype(BF16)
    return high, low


def dot(left, right):
    return jnp.dot(left, right, preferred_element_type=F32)


def kernel(
    grid_shape,
    slot_hbm,
    lid_hbm,
    vel_hbm,
    slopes_hbm,
    stiff_hbm,
    geo_hbm,
    planes_hbm,
    modes_hbm,
    out_ref,
    slot_ref,
    lid_ref,
    vel_r,
    vel_t,
    vel_z,
    cells,
    recv,
    slopes,
    stiff,
    geo,
    to_planes,
    to_modes,
    rhs,
    fields,
    planes,
    push_hi,
    push_lo,
    side_hi,
    side_lo,
    sendb,
    back,
    side_out,
    side_in,
    side_send,
    side_back,
    jac,
    vec,
    img,
    krhs,
    face_in,
    moment,
    red_a,
    red_b,
    local_sem,
    fwd_send,
    fwd_recv,
    bwd_send,
    bwd_recv,
    side_sems,
    fb_send,
    fb_recv,
    halo_send,
    halo_recv,
    a_send,
    a_recv,
    b_send,
    b_recv,
):
    ny, nz, nc = grid_shape
    n_elem = ny * nz * nc
    n_modes = ER
    mi = lax.axis_index("modes")
    e = lax.axis_index("elem")
    core = lax.rem(e, nc)
    zc = lax.rem(e // nc, nz)
    yc = e // (nc * nz)
    size_a = ny * nc
    rank_a = yc * nc + core

    def member_a(t):
        return ((t // nc) * nz + zc) * nc + lax.rem(t, nc)

    def member_b(t):
        return (yc * nz + t) * nc + core

    above = lax.rem(e + 1, n_elem)
    below = lax.rem(e + n_elem - 1, n_elem)

    span = NODES * ER
    vel = (vel_r, vel_t, vel_z)
    local_pairs = [
        *[
            (vel_hbm.at[pl.ds(s * span, span)], vel[s])
            for s in range(3)
        ],
        (slopes_hbm, slopes),
        (planes_hbm, to_planes),
        (geo_hbm, geo),
        (slot_hbm, slot_ref),
        (lid_hbm, lid_ref),
        (modes_hbm, to_modes),
        (stiff_hbm, stiff),
    ]
    local = [
        pltpu.make_async_copy(src, dst, local_sem.at[i]) for i, (src, dst) in enumerate(local_pairs)
    ]
    for copy in local:
        copy.start()

    for g in range(ER):
        for s in range(3):
            cells[g, s, R - 16 :, :] = jnp.zeros((16, LANES), F32)
            recv[g, s, R - 16 :, :] = jnp.zeros((16, LANES), F32)
            img[0, s, g, SENT:, :] = jnp.zeros((R - SENT, LANES), F32)
    no_rows = jnp.zeros((LANES - R, 3 * LANES), BF16)
    for part in range(3):
        rhs[part * LANES + R : (part + 1) * LANES, :] = no_rows
        for g in range(ER):
            krhs[g, part * LANES + R : (part + 1) * LANES, :] = no_rows
    moment[...] = jnp.zeros_like(moment)

    def gather_cell(g, s, target):
        held = slot_ref[0, g]
        for j in range(PS):
            rows = pl.ds(j * ER + held, PS, stride=ER * PS)
            target[g, s, j * PS : (j + 1) * PS, :] = vel[s][rows, :]

    barrier = pltpu.get_barrier_semaphore()
    greeted = [(lax.rem(mi + t, n_modes), e) for t in range(1, n_modes)]
    greeted += [(mi, above), (mi, below)]
    greeted += [(mi, member_a(lax.rem(rank_a + t, size_a))) for t in range(1, size_a)]
    greeted += [(mi, member_b(lax.rem(zc + t, nz))) for t in range(1, nz)]
    for who in greeted:
        pl.semaphore_signal(barrier, inc=1, device_id=who, device_id_type=MESH)
    pl.semaphore_wait(barrier, len(greeted))

    forward = {}
    local[6].wait()
    for off, s in [(off, s) for off in (1, 3, 2) for s in range(3)]:
        if off == 1:
            local[s].wait()
        to = lax.rem(mi + off, n_modes)
        gather_cell(to, s, cells)
        forward[off, s] = pltpu.make_async_remote_copy(
            src_ref=cells.at[to, s, pl.ds(0, SENT)],
            dst_ref=recv.at[mi, s, pl.ds(0, SENT)],
            send_sem=fwd_send.at[off, s],
            recv_sem=fwd_recv.at[off, s],
            device_id=(to, e),
            device_id_type=MESH,
        )
        forward[off, s].start()

    lane = lax.broadcasted_iota(jnp.int32, (1, LANES), 1)
    even = lax.rem(lane, 2) == 0
    pair = (lane // 2).astype(F32)

    def times_unit(values):
        return jnp.where(even, -pltpu.roll(values, LANES - 1, 1), pltpu.roll(values, 1, 1))

    def pair_sum(values):
        return values + jnp.where(even, pltpu.roll(values, LANES - 1, 1), pltpu.roll(values, 1, 1))

    for s in range(3):
        gather_cell(mi, s, recv)
    for copy in (*local[3:6], local[7]):
        copy.wait()

    cell_radius = mi.astype(F32) * (1.0 / ER)
    radius = geo[3 * ER, :, :] + cell_radius
    inv_radius = 1.0 / radius
    swirl_base = SWIRL_SLOPE * radius + SWIRL_CURVE * inv_radius

    def add_modes(block, source, first):
        for s in range(3):
            high, low = split(block[s])
            cols = slice(s * LANES, (s + 1) * LANES)
            rhs[0:R, cols] = high
            rhs[LANES : LANES + R, cols] = low
            rhs[2 * LANES : 2 * LANES + R, cols] = high
        slope = dot(slopes[...], rhs[...])
        d_r = [slope[:R, s * LANES : (s + 1) * LANES] for s in range(3)]
        d_z = [slope[R:, s * LANES : (s + 1) * LANES] for s in range(3)]
        wave = pair + (source * (LANES // 2)).astype(F32)
        u_r, u_t, u_z = block[0], block[1], block[2]
        curl_r = wave * times_unit(u_z) * inv_radius - d_z[1]
        curl_t = d_z[0] - d_r[2]
        curl_z = d_r[1] + (u_t - wave * times_unit(u_r)) * inv_radius
        for f, values in enumerate((u_r, u_t, u_z, curl_r, curl_t, curl_z)):
            high, low = split(values)
            rows = slice(f * R, (f + 1) * R)
            fields[rows, 0:LANES] = high
            fields[rows, LANES : 2 * LANES] = low
            fields[rows, 2 * LANES :] = high
        terms = dot(fields[...], to_planes[source])
        if first:
            planes[...] = terms
        else:
            planes[...] += terms

    add_modes(recv.at[mi], mi, True)

    lid = lid_ref[...].astype(BF16)
    wide = lax.broadcasted_iota(jnp.int32, (LANES // 2, LANES), 1) // 2
    tall = lax.broadcasted_iota(jnp.int32, (LANES // 2, LANES), 0)
    noslip = dot(lid, (wide == tall).astype(BF16))
    side = geo[3 * ER + 1, :, :]
    low_side, high_side = side == 1.0, side == 2.0
    at_low, at_high = (e == 0).astype(F32), (e == n_elem - 1).astype(F32)
    lid_rows = jnp.where(low_side, at_low, 0.0) + jnp.where(high_side, at_high, 0.0)
    sharing = 1.0 + jnp.where(low_side, 1.0 - at_low, 0.0) + jnp.where(high_side, 1.0 - at_high, 0.0)
    wave_own = pair + (mi * (LANES // 2)).astype(F32)
    for s, offset in enumerate((1.0, -1.0, 0.0)):
        square = (wave_own + offset) * (wave_own + offset)
        lid_keep = 1.0 - lid_rows * (noslip if s < 2 else 1.0)
        for g in range(ER):
            fixed = geo[ER + g]
            diag = (fixed + square * geo[2 * ER + g]) * sharing
            jac[s, g] = jnp.where(fixed > 0.0, lid_keep / jnp.where(fixed > 0.0, diag, 1.0), 0.0)

    for off in (1, 3, 2):
        for s in range(3):
            forward[off, s].wait_recv()
        source = lax.rem(mi + n_modes - off, n_modes)
        add_modes(recv.at[source], source, False)

    def push_rows(start, to_hi, to_lo, first, pitch):
        def field(f, cols):
            return planes[pl.ds(pl.multiple_of(f * R + start, 8), FACE), cols]

        rad = geo[3 * ER, pl.ds(start, FACE), :] + cell_radius
        swirl = SWIRL_SLOPE * rad + SWIRL_CURVE / rad
        swirl = jnp.concatenate([swirl] * 3, axis=1)
        spin = 2.0 * SWIRL_SLOPE
        for cols in (slice(0, 3 * LANES), slice(3 * LANES, 6 * LANES)):
            u_r, u_t, u_z, w_r, w_t, w_z = [field(f, cols) for f in range(6)]
            turned = u_t + swirl
            results = (
                turned * w_z - u_z * w_t + spin * u_t,
                u_z * w_r - u_r * w_z - spin * u_r,
                u_r * w_t - turned * w_r,
            )
            for s, values in enumerate(results):
                high, low = split(values)
                rows = pl.ds(pl.multiple_of(first + s * pitch, FACE), FACE)
                to_hi[rows, cols] = high
                to_lo[rows, cols] = low

    def bulk_step(step, _):
        start = pl.multiple_of(step * FACE, FACE)
        push_rows(start + FACE, push_hi, push_lo, start, BULK)
        return 0

    lax.fori_loop(0, BULK // FACE, bulk_step, 0, unroll=True)

    def coefficients(high, low, chunk):
        two = dot(high[...], to_modes[chunk])
        one = dot(low[...], to_modes[chunk, :, 0:LANES])
        return INV_NU * (two[:, :LANES] + (two[:, LANES:] + one))

    backward = {}

    def return_bulk(off):
        to = lax.rem(mi + off, n_modes)
        result = coefficients(push_hi, push_lo, to)
        for s in range(3):
            force = result[s * BULK : (s + 1) * BULK] + LAMBDA_COEF * recv[to, s, FACE : FACE + BULK, :]
            if off == 0:
                back[mi, s] = force
            else:
                sendb[off, s] = force
        if off:
            backward[off] = pltpu.make_async_remote_copy(
                src_ref=sendb.at[off, :, pl.ds(0, MID)],
                dst_ref=back.at[mi, :, pl.ds(0, MID)],
                send_sem=bwd_send.at[off],
                recv_sem=bwd_recv.at[off],
                device_id=(to, e),
                device_id_type=MESH,
            )
            backward[off].start()

    local[8].wait()
    return_bulk(2)
    for side, start in enumerate((0, TOP)):
        push_rows(start, side_hi, side_lo, side * FACE, 2 * FACE)
    for chunk in range(n_modes):
        result = coefficients(side_hi, side_lo, chunk)
        for s in range(3):
            for side, start in enumerate((0, TOP)):
                rows = slice((2 * s + side) * FACE, (2 * s + side + 1) * FACE)
                force = result[rows] + LAMBDA_COEF * recv[chunk, s, start : start + FACE, :]
                side_out[side, chunk, s] = force
    side_copies = []
    for side, who in ((0, below), (1, above)):
        copy = pltpu.make_async_remote_copy(
            src_ref=side_out.at[side],
            dst_ref=side_in.at[1 - side],
            send_sem=side_sems.at[0, side],
            recv_sem=side_sems.at[1, 1 - side],
            device_id=(mi, who),
            device_id_type=MESH,
        )
        copy.start()
        side_copies.append(copy)
    for off in (1, 3, 0):
        return_bulk(off)

    block_row = lax.broadcasted_iota(jnp.int32, (FACE, LANES), 0)
    met = (
        jnp.where(block_row < PS, 1.0 - at_low, 0.0),
        jnp.where((block_row >= 2) & (block_row < 2 + PS), 1.0 - at_high, 0.0),
    )

    def meet(side, other):
        return met[side] * pltpu.roll(other, 2 if side else FACE - 2, 0)

    for copy in side_copies:
        copy.wait_recv()
    side_returns = []
    for off in (2, 1, 3, 0):
        to = lax.rem(mi + off, n_modes)
        for s in range(3):
            for side in range(2):
                total = side_out[side, to, s] + meet(side, side_in[side, to, s])
                if off == 0:
                    side_back[mi, s, side] = total
                else:
                    side_send[off, s, side] = total
        if off:
            copy = pltpu.make_async_remote_copy(
                src_ref=side_send.at[off],
                dst_ref=side_back.at[mi],
                send_sem=fb_send.at[off],
                recv_sem=fb_recv.at[off],
                device_id=(to, e),
                device_id_type=MESH,
            )
            copy.start()
            side_returns.append(copy)
    local[9].wait()
    for off in (1, 3, 2):
        backward[off].wait_recv()
    for copy in side_returns:
        copy.wait_recv()

    for g in range(ER):
        pieces = (
            (slice(0, FACE), [side_back[g, s, 0] for s in range(3)]),
            (slice(FACE, TOP), [back[g, s, 0:MID, :] for s in range(3)]),
            (slice(TOP, SENT), [side_back[g, s, 1] for s in range(3)]),
        )
        for rows, force in pieces:
            turned = times_unit(force[1])
            mass = geo[g, rows, :]
            img[0, 0, g, rows, :] = mass * (force[0] + turned)
            img[0, 1, g, rows, :] = mass * (force[0] - turned)
            img[0, 2, g, rows, :] = mass * force[2]

    halos = []

    def send_faces(k):
        pairs = []
        for side, start, who in ((0, 0, below), (1, TOP, above)):
            copy = pltpu.make_async_remote_copy(
                src_ref=img.at[k, :, :, pl.ds(start, FACE)],
                dst_ref=face_in.at[k - 1, 1 - side],
                send_sem=halo_send.at[k - 1, side],
                recv_sem=halo_recv.at[k - 1, 1 - side],
                device_id=(mi, who),
                device_id_type=MESH,
            )
            copy.start()
            pairs.append(copy)
        halos.append(pairs)

    def inner_part(k):
        for s in range(3):
            for g in range(ER):
                vec[k, s, g] = img[k, s, g]
            for g in range(ER - 1):
                last = pl.ds(2 * PS - 1, PS - 2, stride=PS)
                first = pl.ds(PS, PS - 2, stride=PS)
                shared = img[k, s, g, last, :] + img[k, s, g + 1, first, :]
                vec[k, s, g, last, :] = shared
                vec[k, s, g + 1, first, :] = shared
            for g in range(ER):
                vec[k, s, g, FACE:TOP, :] = vec[k, s, g, FACE:TOP, :] * jac[s, g, FACE:TOP, :]

    def outer_part(k):
        if k > 0:
            for copy in halos[k - 1]:
                copy.wait_recv()
        for side, start, last in ((0, 0, PS - 1), (1, TOP, PS + 1)):
            rows = slice(start, start + FACE)
            for s in range(3):
                block = [vec[k, s, g, rows, :] for g in range(ER)]
                if k > 0:
                    block = [block[g] + meet(side, face_in[k - 1, side, s, g]) for g in range(ER)]
                for g in range(ER):
                    total = block[g]
                    if g + 1 < ER:
                        nearby = pltpu.roll(block[g + 1], PS - 1, 0)
                        total = total + jnp.where(block_row == last, nearby, 0.0)
                    if g > 0:
                        nearby = pltpu.roll(block[g - 1], FACE - PS + 1, 0)
                        total = total + jnp.where(block_row == last - PS + 1, nearby, 0.0)
                    vec[k, s, g, rows, :] = total * jac[s, g, rows, :]

    def apply_stiff(k):
        for g in range(ER):
            for s in range(3):
                high, low = split(vec[k, s, g])
                cols = slice(s * LANES, (s + 1) * LANES)
                krhs[g, 0:R, cols] = high
                krhs[g, LANES : LANES + R, cols] = low
                krhs[g, 2 * LANES : 2 * LANES + R, cols] = high
            image = dot(stiff[g], krhs[g])
            for s in range(3):
                img[k + 1, s, g] = image[:, s * LANES : (s + 1) * LANES]

    share = 1.0 / sharing

    def inner(k, left, right):
        for s in range(3):
            total = jnp.zeros((1, LANES), F32)
            for g in range(ER):
                products = vec[left, s, g] * img[right, s, g]
                if right == 0:
                    products = products * share
                total = total + jnp.sum(products, axis=0, keepdims=True)
            index = k * 3 + s
            moment[index // 9, index % 9 : index % 9 + 1, :] = total

    inner_part(0)
    outer_part(0)
    apply_stiff(0)
    send_faces(1)
    inner(0, 0, 0)
    inner(1, 0, 1)
    inner_part(1)
    outer_part(1)
    apply_stiff(1)
    send_faces(2)
    inner(2, 1, 1)
    inner(3, 1, 2)
    inner_part(2)
    outer_part(2)
    apply_stiff(2)
    inner(4, 2, 2)
    inner(5, 2, 3)

    def exchange(buffer, rank, size, member, send_sems, recv_sems):
        copies = []
        for off in range(1, size):
            copy = pltpu.make_async_remote_copy(
                src_ref=buffer.at[rank],
                dst_ref=buffer.at[rank],
                send_sem=send_sems.at[off],
                recv_sem=recv_sems.at[off],
                device_id=(mi, member(lax.rem(rank + off, size))),
                device_id_type=MESH,
            )
            copy.start()
            copies.append(copy)
        for copy in copies:
            copy.wait_recv()
        total = buffer[0]
        for t in range(1, size):
            total = total + buffer[t]
        return total, copies

    red_a[rank_a] = jnp.where(even, pair_sum(moment[0]), pair_sum(moment[1]))
    total, copies_a = exchange(red_a, rank_a, size_a, member_a, a_send, a_recv)
    red_b[zc] = total
    total, copies_b = exchange(red_b, zc, nz, member_b, b_send, b_recv)
    first = jnp.where(even, total, pltpu.roll(total, 1, 1))
    second = jnp.where(even, pltpu.roll(total, LANES - 1, 1), total)

    coefs = []
    for s in range(3):
        h = [(first if k < 3 else second)[(k % 3) * 3 + s : (k % 3) * 3 + s + 1] for k in range(6)]
        g00, g01, g02, g12, g22 = [h[k] + h[k + 1] for k in range(5)]
        g11 = g02
        ratio1, ratio2 = g01 / g00, g02 / g00
        d1 = g11 - ratio1 * g01
        left = g12 - ratio1 * g02
        ratio = left / d1
        d2 = g22 - ratio2 * g02 - ratio * left
        y1 = h[1] - ratio1 * h[0]
        y2 = h[2] - ratio2 * h[0] - ratio * y1
        c2 = y2 / d2
        c1 = y1 / d1 - ratio * c2
        c0 = h[0] / g00 - ratio1 * c1 - ratio2 * c2
        coefs.append((c0, c1, c2))

    for slot in range(ER):
        held = jnp.int32(0)
        for g in range(ER):
            held = jnp.where(slot_ref[0, g] == slot, g, held)
        plus, minus, axial = [
            coefs[s][0] * vec[0, s, held] + coefs[s][1] * vec[1, s, held] + coefs[s][2] * vec[2, s, held]
            for s in range(3)
        ]
        results = ((plus + minus) * 0.5, times_unit(minus - plus) * 0.5, axial)
        for s, values in enumerate(results):
            for j in range(PS):
                rows = pl.ds(s * span + j * ER + slot, PS, stride=ER * PS)
                out_ref[rows, :] = values[j * PS : (j + 1) * PS]

    sent = (forward.values(), backward.values(), side_copies, side_returns, copies_a, copies_b)
    for copies in (*sent, *halos):
        for copy in copies:
            copy.wait_send()


def on_device(grid_shape, velocity, element_slot, lid_noslip):
    ny, nz, nc = grid_shape
    slopes, stiff, geometry, to_planes, to_modes = constants()
    vmem = pltpu.VMEM
    dma = pltpu.SemaphoreType.DMA
    flat = velocity.transpose(0, 2, 3, 1, 4).reshape(3 * NODES * ER, LANES)
    result = pl.pallas_call(
        functools.partial(kernel, grid_shape),
        out_shape=vmem((3 * NODES * ER, LANES), F32),
        in_specs=[pl.BlockSpec(memory_space=pltpu.HBM)] * 8,
        out_specs=pl.BlockSpec(memory_space=vmem),
        scratch_shapes=[
            pltpu.SMEM((1, ER), jnp.int32),
            vmem((1, LANES // 2), jnp.int32),
            *[vmem((NODES * ER, LANES), F32)] * 3,
            vmem((ER, 3, R, LANES), F32),
            vmem((ER, 3, R, LANES), F32),
            vmem(slopes.shape, BF16),
            vmem(stiff.shape, BF16),
            vmem(geometry.shape, F32),
            vmem(to_planes.shape, BF16),
            vmem(to_modes.shape, BF16),
            vmem((3 * LANES, 3 * LANES), BF16),
            vmem((6 * R, 3 * LANES), BF16),
            vmem((6 * R, Q), F32),
            vmem((3 * BULK, Q), BF16),
            vmem((3 * BULK, Q), BF16),
            vmem((6 * FACE, Q), BF16),
            vmem((6 * FACE, Q), BF16),
            vmem((ER, 3, BULK, LANES), F32),
            vmem((ER, 3, BULK, LANES), F32),
            vmem((2, ER, 3, FACE, LANES), F32),
            vmem((2, ER, 3, FACE, LANES), F32),
            vmem((ER, 3, 2, FACE, LANES), F32),
            vmem((ER, 3, 2, FACE, LANES), F32),
            vmem((3, ER, R, LANES), F32),
            vmem((3, 3, ER, R, LANES), F32),
            vmem((4, 3, ER, R, LANES), F32),
            vmem((ER, 3 * LANES, 3 * LANES), BF16),
            vmem((2, 2, 3, ER, FACE, LANES), F32),
            vmem((2, 16, LANES), F32),
            vmem((ny * nc, 16, LANES), F32),
            vmem((nz, 16, LANES), F32),
            dma((10,)),
            dma((ER, 3)),
            dma((ER, 3)),
            dma((ER,)),
            dma((ER,)),
            dma((2, 2)),
            dma((ER,)),
            dma((ER,)),
            dma((2, 2)),
            dma((2, 2)),
            dma((ny * nc,)),
            dma((ny * nc,)),
            dma((nz,)),
            dma((nz,)),
        ],
        compiler_params=pltpu.CompilerParams(
            collective_id=0, has_side_effects=True, vmem_limit_bytes=48 * 1024 * 1024
        ),
    )(
        *[
            pltpu.with_memory_space_constraint(operand, pltpu.HBM)
            for operand in (
                element_slot,
                lid_noslip.reshape(1, -1),
                flat,
                *[jnp.asarray(table) for table in (slopes, stiff, geometry, to_planes, to_modes)],
            )
        ]
    )
    return result.reshape(3, PS, PS, ER, LANES).transpose(0, 3, 1, 2, 4)


def solution(mesh):
    n_elem = mesh.shape["elem"]
    nc = 2
    nz = min(8, n_elem // nc)
    ny = n_elem // (nc * nz)
    return jax.shard_map(
        functools.partial(on_device, (ny, nz, nc)),
        mesh=mesh,
        in_specs=(P(None, "elem", None, None, "modes"), P("elem", None), P("modes")),
        out_specs=P(None, "elem", None, None, "modes"),
        check_vma=False,
    )
```

```python
import functools

import jax
import jax.numpy as jnp
import ml_dtypes
import numpy as np
from jax import lax
from jax.experimental import pallas as pl
from jax.experimental.pallas import tpu as pltpu
from jax.sharding import PartitionSpec as P

PS = 10
NODES = PS * PS
R = 112
TOP = 88
FACE = 16
FACE_AT = (0, NODES - PS - TOP)
MID = TOP - FACE
ENDS = NODES - MID
MOMENTS = 9
BULK = 80
M = 256
Q = 768
ER = 4
LANES = 128
LAMBDA_COEF = 20.0
INV_NU = 10.0
R_INNER = 1.0
SWIRL_SLOPE = -1.0 / 3.0
SWIRL_CURVE = 4.0 / 3.0
MESH = pl.DeviceIdType.MESH
F32 = jnp.float32
BF16 = jnp.bfloat16


def legendre_rows(abscissa, degree):
    table_rows = [abscissa * 0.0 + 1.0, abscissa.copy()]
    for degree_now in range(2, degree + 1):
        table_rows.append(
            ((2 * degree_now - 1) * abscissa * table_rows[-1] - (degree_now - 1) * table_rows[-2])
            / degree_now
        )
    return table_rows


def gll_tables(points):
    degree = points - 1
    abscissa = -np.cos(np.pi * np.arange(points) / degree)
    for _ in range(60):
        legendre = legendre_rows(abscissa, degree)
        abscissa = abscissa - (abscissa * legendre[degree] - legendre[degree - 1]) / (
            points * legendre[degree]
        )
    legendre = legendre_rows(abscissa, degree)
    last_row = legendre[degree]
    weights = 2.0 / (degree * points * last_row**2)
    identity = np.eye(points)
    distance = abscissa[:, None] - abscissa[None, :] + identity
    derivative = last_row[:, None] / (last_row[None, :] * distance) * (1.0 - identity)
    derivative[0, 0] = -degree * points / 4.0
    derivative[degree, degree] = degree * points / 4.0
    return abscissa, weights, derivative


def halves(values):
    high = values.astype(ml_dtypes.bfloat16)
    low = (values - high.astype(np.float64)).astype(ml_dtypes.bfloat16)
    return high, low


@functools.cache
def constants():
    xi, w, deriv = gll_tables(PS)
    eye = np.eye(PS)
    radius = R_INNER + (np.arange(ER)[:, None] + 0.5 * (xi[None, :] + 1.0)) / ER
    ww = np.outer(w, w)

    def operator(rows):
        padded = np.zeros((R, LANES))
        padded[:NODES, :NODES] = rows
        high, low = halves(padded)
        return np.concatenate([high, high, low], axis=1)

    slope_r = operator(2.0 * ER * np.kron(eye, deriv))
    slope_z = operator(2.0 * ER * np.kron(deriv, eye))
    slopes = np.concatenate([slope_r, slope_z], axis=0)

    stiff, stiff_diag = [], np.zeros((ER, PS, PS))
    for ir in range(ER):
        along_i = deriv.T @ np.diag(w * radius[ir]) @ deriv
        along_j = deriv.T @ np.diag(w) @ deriv
        whole = np.kron(np.diag(w), along_i) + np.kron(along_j, np.diag(w * radius[ir]))
        stiff_diag[ir] = np.diag(whole).reshape(PS, PS).T
        stiff.append(operator(whole - np.diag(np.diag(whole))))
    stiff = np.stack(stiff)

    quarter_h = 0.25 / (ER * ER)
    mass_r = ww[None] * quarter_h * radius[:, :, None]
    mass_over_r = ww[None] * quarter_h / radius[:, :, None]

    def radial_sum(values):
        total = values.copy()
        total[:-1, -1] += values[1:, 0]
        total[1:, 0] += values[:-1, -1]
        return total

    diag_fixed = radial_sum(stiff_diag + LAMBDA_COEF * mass_r)
    diag_square = radial_sum(mass_over_r)
    diag_fixed[0, 0] = 0.0
    diag_fixed[-1, -1] = 0.0

    geometry = np.zeros((3 * ER + 2, R, LANES))
    for part, values in enumerate((mass_r, diag_fixed, diag_square)):
        rows = values.transpose(0, 2, 1).reshape(ER, NODES, 1)
        geometry[part * ER : (part + 1) * ER, :NODES] = rows
    geometry[3 * ER] = 1.0
    geometry[3 * ER, :NODES] = (R_INNER + 0.5 * (np.tile(xi, PS) + 1.0) / ER)[:, None]
    geometry[3 * ER + 1, :PS] = 1.0
    geometry[3 * ER + 1, NODES - PS : NODES] = 2.0

    modes = np.arange(M)
    angles = (modes[:, None] * np.arange(Q)[None, :] % Q) * (2.0 * np.pi / Q)
    weight = np.where(modes == 0, 1.0, 2.0)[:, None]
    inverse = np.stack([weight * np.cos(angles), -weight * np.sin(angles)], axis=1)
    inverse = inverse.reshape(2 * M // LANES, LANES, Q)
    high, low = halves(inverse)
    to_planes = np.concatenate([high, high, low], axis=1)
    forward = np.stack([np.cos(angles), -np.sin(angles)], axis=1) / Q
    forward = forward.reshape(2 * M // LANES, LANES, Q).transpose(0, 2, 1)
    high, low = halves(forward)
    to_modes = np.concatenate([high, low], axis=2)
    return slopes, stiff, geometry.astype(np.float32), to_planes, to_modes


def split(values):
    high = values.astype(BF16)
    low = (values - high.astype(F32)).astype(BF16)
    return high, low


def dot(left, right):
    return jnp.dot(left, right, preferred_element_type=F32)


def kernel(
    grid_shape,
    slot_hbm,
    lid_hbm,
    vel_hbm,
    slopes_hbm,
    stiff_hbm,
    geo_hbm,
    planes_hbm,
    modes_hbm,
    out_ref,
    slot_ref,
    lid_ref,
    vel_r,
    vel_t,
    vel_z,
    cells,
    recv,
    slopes,
    stiff,
    geo,
    to_planes,
    to_modes,
    rhs,
    fields,
    planes,
    push_hi,
    push_lo,
    side_hi,
    side_lo,
    sendb,
    back,
    side_out,
    side_in,
    side_send,
    side_back,
    jac,
    vec,
    img,
    krhs,
    face_in,
    moment,
    red_a,
    red_b,
    local_sem,
    fwd_send,
    fwd_recv,
    bwd_send,
    bwd_recv,
    side_sems,
    fb_send,
    fb_recv,
    halo_send,
    halo_recv,
    a_send,
    a_recv,
    b_send,
    b_recv,
):
    ny, nz, nc = grid_shape
    n_elem = ny * nz * nc
    n_modes = ER
    mi = lax.axis_index("modes")
    e = lax.axis_index("elem")
    core = lax.rem(e, nc)
    zc = lax.rem(e // nc, nz)
    yc = e // (nc * nz)
    size_a = ny * nc
    rank_a = yc * nc + core

    def member_a(t):
        return ((t // nc) * nz + zc) * nc + lax.rem(t, nc)

    def member_b(t):
        return (yc * nz + t) * nc + core

    above = lax.rem(e + 1, n_elem)
    below = lax.rem(e + n_elem - 1, n_elem)

    span = NODES * ER
    vel = (vel_r, vel_t, vel_z)
    local_pairs = [
        *[
            (vel_hbm.at[pl.ds(s * span, span)], vel[s])
            for s in range(3)
        ],
        (slopes_hbm, slopes),
        (planes_hbm, to_planes),
        (geo_hbm, geo),
        (slot_hbm, slot_ref),
        (lid_hbm, lid_ref),
        (modes_hbm, to_modes),
        (stiff_hbm, stiff),
    ]
    local = [
        pltpu.make_async_copy(src, dst, local_sem.at[i]) for i, (src, dst) in enumerate(local_pairs)
    ]
    for copy in local:
        copy.start()

    for g in range(ER):
        for s in range(3):
            recv[g, s, R - 16 :, :] = jnp.zeros((16, LANES), F32)
            img[0, s, g, TOP + FACE :, :] = jnp.zeros((R - TOP - FACE, LANES), F32)
            side_back[g, s, 2 * FACE - 8 :, :] = jnp.zeros((8, LANES), F32)
    no_rows = jnp.zeros((LANES - R, 3 * LANES), BF16)
    for part in range(3):
        rhs[part * LANES + R : (part + 1) * LANES, :] = no_rows
        for g in range(ER):
            krhs[g, part * LANES + R : (part + 1) * LANES, :] = no_rows
    moment[...] = jnp.zeros_like(moment)

    def gather_cell(g, s, target):
        held = slot_ref[0, g]
        for j in range(PS):
            rows = pl.ds(j * ER + held, PS, stride=ER * PS)
            target[g, s, j * PS : (j + 1) * PS, :] = vel[s][rows, :]

    barrier = pltpu.get_barrier_semaphore()
    greeted = [(lax.rem(mi + t, n_modes), e) for t in range(1, n_modes)]
    greeted += [(mi, above), (mi, below)]
    greeted += [(mi, member_a(lax.rem(rank_a + t, size_a))) for t in range(1, size_a)]
    greeted += [(mi, member_b(lax.rem(zc + t, nz))) for t in range(1, nz)]
    for who in greeted:
        pl.semaphore_signal(barrier, inc=1, device_id=who, device_id_type=MESH)
    pl.semaphore_wait(barrier, len(greeted))

    forward = {}
    local[6].wait()
    for off, s in [(off, s) for off in (1, 3, 2) for s in range(3)]:
        if off == 1:
            local[s].wait()
        to = lax.rem(mi + off, n_modes)
        gather_cell(to, s, cells)
        forward[off, s] = pltpu.make_async_remote_copy(
            src_ref=cells.at[to, s, pl.ds(0, NODES)],
            dst_ref=recv.at[mi, s, pl.ds(0, NODES)],
            send_sem=fwd_send.at[off, s],
            recv_sem=fwd_recv.at[off, s],
            device_id=(to, e),
            device_id_type=MESH,
        )
        forward[off, s].start()

    lane = lax.broadcasted_iota(jnp.int32, (1, LANES), 1)
    even = lax.rem(lane, 2) == 0
    pair = (lane // 2).astype(F32)

    def times_unit(values):
        return jnp.where(even, -pltpu.roll(values, LANES - 1, 1), pltpu.roll(values, 1, 1))

    def pair_sum(values):
        return values + jnp.where(even, pltpu.roll(values, LANES - 1, 1), pltpu.roll(values, 1, 1))

    for s in range(3):
        gather_cell(mi, s, recv)
    for copy in (*local[3:6], local[7]):
        copy.wait()

    cell_radius = mi.astype(F32) * (1.0 / ER)
    radius = geo[3 * ER, :, :] + cell_radius
    inv_radius = 1.0 / radius
    swirl_base = SWIRL_SLOPE * radius + SWIRL_CURVE * inv_radius

    def add_modes(block, source, first):
        for s in range(3):
            high, low = split(block[s])
            cols = slice(s * LANES, (s + 1) * LANES)
            rhs[0:R, cols] = high
            rhs[LANES : LANES + R, cols] = low
            rhs[2 * LANES : 2 * LANES + R, cols] = high
        slope = dot(slopes[...], rhs[...])
        d_r = [slope[:R, s * LANES : (s + 1) * LANES] for s in range(3)]
        d_z = [slope[R:, s * LANES : (s + 1) * LANES] for s in range(3)]
        wave = pair + (source * (LANES // 2)).astype(F32)
        u_r, u_t, u_z = block[0], block[1], block[2]
        curl_r = wave * times_unit(u_z) * inv_radius - d_z[1]
        curl_t = d_z[0] - d_r[2]
        curl_z = d_r[1] + (u_t - wave * times_unit(u_r)) * inv_radius
        for f, values in enumerate((u_r, u_t, u_z, curl_r, curl_t, curl_z)):
            high, low = split(values)
            rows = slice(f * R, (f + 1) * R)
            fields[rows, 0:LANES] = high
            fields[rows, LANES : 2 * LANES] = low
            fields[rows, 2 * LANES :] = high
        terms = dot(fields[...], to_planes[source])
        if first:
            planes[...] = terms
        else:
            planes[...] += terms

    add_modes(recv.at[mi], mi, True)

    lid = lid_ref[...].astype(BF16)
    wide = lax.broadcasted_iota(jnp.int32, (LANES // 2, LANES), 1) // 2
    tall = lax.broadcasted_iota(jnp.int32, (LANES // 2, LANES), 0)
    noslip = dot(lid, (wide == tall).astype(BF16))
    side = geo[3 * ER + 1, :, :]
    low_side, high_side = side == 1.0, side == 2.0
    at_low, at_high = (e == 0).astype(F32), (e == n_elem - 1).astype(F32)
    lid_rows = jnp.where(low_side, at_low, 0.0) + jnp.where(high_side, at_high, 0.0)
    sharing = 1.0 + jnp.where(low_side, 1.0 - at_low, 0.0) + jnp.where(high_side, 1.0 - at_high, 0.0)
    wave_own = pair + (mi * (LANES // 2)).astype(F32)
    for s, offset in enumerate((1.0, -1.0, 0.0)):
        square = (wave_own + offset) * (wave_own + offset)
        lid_keep = 1.0 - lid_rows * (noslip if s < 2 else 1.0)
        for g in range(ER):
            fixed = geo[ER + g]
            diag = (fixed + square * geo[2 * ER + g]) * sharing
            jac[s, g] = jnp.where(fixed > 0.0, lid_keep / jnp.where(fixed > 0.0, diag, 1.0), 0.0)

    for off in (1, 3, 2):
        for s in range(3):
            forward[off, s].wait_recv()
        source = lax.rem(mi + n_modes - off, n_modes)
        add_modes(recv.at[source], source, False)

    def push_rows(start, to_hi, to_lo, first, pitch):
        def field(f, cols):
            return planes[pl.ds(pl.multiple_of(f * R + start, 8), FACE), cols]

        rad = geo[3 * ER, pl.ds(start, FACE), :] + cell_radius
        swirl = SWIRL_SLOPE * rad + SWIRL_CURVE / rad
        swirl = jnp.concatenate([swirl] * 3, axis=1)
        spin = 2.0 * SWIRL_SLOPE
        for cols in (slice(0, 3 * LANES), slice(3 * LANES, 6 * LANES)):
            u_r, u_t, u_z, w_r, w_t, w_z = [field(f, cols) for f in range(6)]
            turned = u_t + swirl
            results = (
                turned * w_z - u_z * w_t + spin * u_t,
                u_z * w_r - u_r * w_z - spin * u_r,
                u_r * w_t - turned * w_r,
            )
            for s, values in enumerate(results):
                high, low = split(values)
                rows = pl.ds(pl.multiple_of(first + s * pitch, FACE), FACE)
                to_hi[rows, cols] = high
                to_lo[rows, cols] = low

    def bulk_step(step, _):
        start = pl.multiple_of(step * FACE, FACE)
        push_rows(start + FACE, push_hi, push_lo, start, BULK)
        return 0

    lax.fori_loop(0, BULK // FACE, bulk_step, 0, unroll=True)

    def coefficients(high, low, chunk):
        two = dot(high[...], to_modes[chunk])
        one = dot(low[...], to_modes[chunk, :, 0:LANES])
        return INV_NU * (two[:, :LANES] + (two[:, LANES:] + one))

    backward = {}

    def return_bulk(off):
        to = lax.rem(mi + off, n_modes)
        result = coefficients(push_hi, push_lo, to)
        for s in range(3):
            force = result[s * BULK : (s + 1) * BULK] + LAMBDA_COEF * recv[to, s, FACE : FACE + BULK, :]
            if off == 0:
                back[mi, s] = force
            else:
                sendb[off, s] = force
        if off:
            backward[off] = pltpu.make_async_remote_copy(
                src_ref=sendb.at[off, :, pl.ds(0, MID)],
                dst_ref=back.at[mi, :, pl.ds(0, MID)],
                send_sem=bwd_send.at[off],
                recv_sem=bwd_recv.at[off],
                device_id=(to, e),
                device_id_type=MESH,
            )
            backward[off].start()

    local[8].wait()
    return_bulk(2)
    for side, start in enumerate((0, TOP)):
        push_rows(start, side_hi, side_lo, side * FACE, 2 * FACE)
    for chunk in range(n_modes):
        result = coefficients(side_hi, side_lo, chunk)
        for s in range(3):
            for side, start in enumerate((0, TOP)):
                rows = slice((2 * s + side) * FACE, (2 * s + side + 1) * FACE)
                force = result[rows] + LAMBDA_COEF * recv[chunk, s, start : start + FACE, :]
                side_out[side, chunk, s] = force
    side_copies = []
    for side, who in ((0, below), (1, above)):
        copy = pltpu.make_async_remote_copy(
            src_ref=side_out.at[side, :, :, pl.ds(FACE_AT[side], PS)],
            dst_ref=side_in.at[1 - side, :, :, pl.ds(FACE_AT[1 - side], PS)],
            send_sem=side_sems.at[0, side],
            recv_sem=side_sems.at[1, 1 - side],
            device_id=(mi, who),
            device_id_type=MESH,
        )
        copy.start()
        side_copies.append(copy)
    for off in (1, 3, 0):
        return_bulk(off)

    block_row = lax.broadcasted_iota(jnp.int32, (FACE, LANES), 0)
    met = (
        (block_row < PS) & (e > 0),
        (block_row >= FACE_AT[1]) & (block_row < FACE_AT[1] + PS) & (e < n_elem - 1),
    )

    def meet(side, other):
        return jnp.where(met[side], other, 0.0)

    for copy in side_copies:
        copy.wait_recv()
    side_returns = []
    for off in (2, 1, 3, 0):
        to = lax.rem(mi + off, n_modes)
        for s in range(3):
            for side in range(2):
                total = side_out[side, to, s] + meet(side, side_in[side, to, s])
                rows = slice(side * FACE, (side + 1) * FACE)
                if off == 0:
                    side_back[mi, s, rows, :] = total
                else:
                    side_send[off, s, rows, :] = total
        if off:
            copy = pltpu.make_async_remote_copy(
                src_ref=side_send.at[off, :, pl.ds(0, ENDS)],
                dst_ref=side_back.at[mi, :, pl.ds(0, ENDS)],
                send_sem=fb_send.at[off],
                recv_sem=fb_recv.at[off],
                device_id=(to, e),
                device_id_type=MESH,
            )
            copy.start()
            side_returns.append(copy)
    local[9].wait()
    for off in (1, 3, 2):
        backward[off].wait_recv()
    for copy in side_returns:
        copy.wait_recv()

    for g in range(ER):
        pieces = (
            (slice(0, FACE), [side_back[g, s, 0:FACE, :] for s in range(3)]),
            (slice(FACE, TOP), [back[g, s, 0:MID, :] for s in range(3)]),
            (slice(TOP, TOP + FACE), [side_back[g, s, FACE:, :] for s in range(3)]),
        )
        for rows, force in pieces:
            turned = times_unit(force[1])
            mass = geo[g, rows, :]
            img[0, 0, g, rows, :] = mass * (force[0] + turned)
            img[0, 1, g, rows, :] = mass * (force[0] - turned)
            img[0, 2, g, rows, :] = mass * force[2]

    halos = []

    def send_faces(k):
        pairs = []
        for side, start, who in ((0, 0, below), (1, NODES - PS, above)):
            copy = pltpu.make_async_remote_copy(
                src_ref=img.at[k, :, :, pl.ds(start, PS)],
                dst_ref=face_in.at[k - 1, 1 - side, :, :, pl.ds(FACE_AT[1 - side], PS)],
                send_sem=halo_send.at[k - 1, side],
                recv_sem=halo_recv.at[k - 1, 1 - side],
                device_id=(mi, who),
                device_id_type=MESH,
            )
            copy.start()
            pairs.append(copy)
        halos.append(pairs)

    def inner_part(k):
        for s in range(3):
            for g in range(ER):
                vec[k, s, g] = img[k, s, g]
            for g in range(ER - 1):
                last = pl.ds(2 * PS - 1, PS - 2, stride=PS)
                first = pl.ds(PS, PS - 2, stride=PS)
                shared = img[k, s, g, last, :] + img[k, s, g + 1, first, :]
                vec[k, s, g, last, :] = shared
                vec[k, s, g + 1, first, :] = shared
            for g in range(ER):
                vec[k, s, g, FACE:TOP, :] = vec[k, s, g, FACE:TOP, :] * jac[s, g, FACE:TOP, :]

    def outer_part(k):
        if k > 0:
            for copy in halos[k - 1]:
                copy.wait_recv()
        for side, start, last in ((0, 0, PS - 1), (1, TOP, PS + 1)):
            rows = slice(start, start + FACE)
            for s in range(3):
                block = [vec[k, s, g, rows, :] for g in range(ER)]
                if k > 0:
                    block = [block[g] + meet(side, face_in[k - 1, side, s, g]) for g in range(ER)]
                for g in range(ER):
                    total = block[g]
                    if g + 1 < ER:
                        nearby = pltpu.roll(block[g + 1], PS - 1, 0)
                        total = total + jnp.where(block_row == last, nearby, 0.0)
                    if g > 0:
                        nearby = pltpu.roll(block[g - 1], FACE - PS + 1, 0)
                        total = total + jnp.where(block_row == last - PS + 1, nearby, 0.0)
                    vec[k, s, g, rows, :] = total * jac[s, g, rows, :]

    def apply_stiff(k):
        for g in range(ER):
            for s in range(3):
                high, low = split(vec[k, s, g])
                cols = slice(s * LANES, (s + 1) * LANES)
                krhs[g, 0:R, cols] = high
                krhs[g, LANES : LANES + R, cols] = low
                krhs[g, 2 * LANES : 2 * LANES + R, cols] = high
            image = dot(stiff[g], krhs[g])
            for s in range(3):
                img[k + 1, s, g] = image[:, s * LANES : (s + 1) * LANES]

    share = 1.0 / sharing

    def inner(k, left, right):
        for s in range(3):
            total = jnp.zeros((1, LANES), F32)
            for g in range(ER):
                products = vec[left, s, g] * img[right, s, g]
                if right == 0:
                    products = products * share
                total = total + jnp.sum(products, axis=0, keepdims=True)
            index = k * 3 + s
            at = index % MOMENTS
            moment[index // MOMENTS, at : at + 1, :] = total

    inner_part(0)
    outer_part(0)
    apply_stiff(0)
    send_faces(1)
    inner(0, 0, 0)
    inner(1, 0, 1)
    inner_part(1)
    outer_part(1)
    apply_stiff(1)
    send_faces(2)
    inner(2, 1, 1)
    inner(3, 1, 2)
    inner_part(2)
    outer_part(2)
    apply_stiff(2)
    inner(4, 2, 2)
    inner(5, 2, 3)

    def exchange(buffer, rank, size, member, send_sems, recv_sems):
        copies = []
        for off in range(1, size):
            copy = pltpu.make_async_remote_copy(
                src_ref=buffer.at[rank, pl.ds(0, MOMENTS)],
                dst_ref=buffer.at[rank, pl.ds(0, MOMENTS)],
                send_sem=send_sems.at[off],
                recv_sem=recv_sems.at[off],
                device_id=(mi, member(lax.rem(rank + off, size))),
                device_id_type=MESH,
            )
            copy.start()
            copies.append(copy)
        for copy in copies:
            copy.wait_recv()
        total = buffer[0, 0:MOMENTS, :]
        for t in range(1, size):
            total = total + buffer[t, 0:MOMENTS, :]
        return total, copies

    red_a[rank_a] = jnp.where(even, pair_sum(moment[0]), pair_sum(moment[1]))
    total, copies_a = exchange(red_a, rank_a, size_a, member_a, a_send, a_recv)
    red_b[zc, 0:MOMENTS, :] = total
    total, copies_b = exchange(red_b, zc, nz, member_b, b_send, b_recv)
    first = jnp.where(even, total, pltpu.roll(total, 1, 1))
    second = jnp.where(even, pltpu.roll(total, LANES - 1, 1), total)

    coefs = []
    for s in range(3):
        h = [(first if k < 3 else second)[(k % 3) * 3 + s : (k % 3) * 3 + s + 1] for k in range(6)]
        g00, g01, g02, g12, g22 = [h[k] + h[k + 1] for k in range(5)]
        g11 = g02
        ratio1, ratio2 = g01 / g00, g02 / g00
        d1 = g11 - ratio1 * g01
        left = g12 - ratio1 * g02
        ratio = left / d1
        d2 = g22 - ratio2 * g02 - ratio * left
        y1 = h[1] - ratio1 * h[0]
        y2 = h[2] - ratio2 * h[0] - ratio * y1
        c2 = y2 / d2
        c1 = y1 / d1 - ratio * c2
        c0 = h[0] / g00 - ratio1 * c1 - ratio2 * c2
        coefs.append((c0, c1, c2))

    for slot in range(ER):
        held = jnp.int32(0)
        for g in range(ER):
            held = jnp.where(slot_ref[0, g] == slot, g, held)
        plus, minus, axial = [
            coefs[s][0] * vec[0, s, held] + coefs[s][1] * vec[1, s, held] + coefs[s][2] * vec[2, s, held]
            for s in range(3)
        ]
        results = ((plus + minus) * 0.5, times_unit(minus - plus) * 0.5, axial)
        for s, values in enumerate(results):
            for j in range(PS):
                rows = pl.ds(s * span + j * ER + slot, PS, stride=ER * PS)
                out_ref[rows, :] = values[j * PS : (j + 1) * PS]

    sent = (forward.values(), backward.values(), side_copies, side_returns, copies_a, copies_b)
    for copies in (*sent, *halos):
        for copy in copies:
            copy.wait_send()


def on_device(grid_shape, velocity, element_slot, lid_noslip):
    ny, nz, nc = grid_shape
    slopes, stiff, geometry, to_planes, to_modes = constants()
    vmem = pltpu.VMEM
    dma = pltpu.SemaphoreType.DMA
    flat = velocity.transpose(0, 2, 3, 1, 4).reshape(3 * NODES * ER, LANES)
    result = pl.pallas_call(
        functools.partial(kernel, grid_shape),
        out_shape=vmem((3 * NODES * ER, LANES), F32),
        in_specs=[pl.BlockSpec(memory_space=pltpu.HBM)] * 8,
        out_specs=pl.BlockSpec(memory_space=vmem),
        scratch_shapes=[
            pltpu.SMEM((1, ER), jnp.int32),
            vmem((1, LANES // 2), jnp.int32),
            *[vmem((NODES * ER, LANES), F32)] * 3,
            vmem((ER, 3, R, LANES), F32),
            vmem((ER, 3, R, LANES), F32),
            vmem(slopes.shape, BF16),
            vmem(stiff.shape, BF16),
            vmem(geometry.shape, F32),
            vmem(to_planes.shape, BF16),
            vmem(to_modes.shape, BF16),
            vmem((3 * LANES, 3 * LANES), BF16),
            vmem((6 * R, 3 * LANES), BF16),
            vmem((6 * R, Q), F32),
            vmem((3 * BULK, Q), BF16),
            vmem((3 * BULK, Q), BF16),
            vmem((6 * FACE, Q), BF16),
            vmem((6 * FACE, Q), BF16),
            vmem((ER, 3, BULK, LANES), F32),
            vmem((ER, 3, BULK, LANES), F32),
            vmem((2, ER, 3, FACE, LANES), F32),
            vmem((2, ER, 3, FACE, LANES), F32),
            vmem((ER, 3, 2 * FACE, LANES), F32),
            vmem((ER, 3, 2 * FACE, LANES), F32),
            vmem((3, ER, R, LANES), F32),
            vmem((3, 3, ER, R, LANES), F32),
            vmem((4, 3, ER, R, LANES), F32),
            vmem((ER, 3 * LANES, 3 * LANES), BF16),
            vmem((2, 2, 3, ER, FACE, LANES), F32),
            vmem((2, 16, LANES), F32),
            vmem((ny * nc, 16, LANES), F32),
            vmem((nz, 16, LANES), F32),
            dma((10,)),
            dma((ER, 3)),
            dma((ER, 3)),
            dma((ER,)),
            dma((ER,)),
            dma((2, 2)),
            dma((ER,)),
            dma((ER,)),
            dma((2, 2)),
            dma((2, 2)),
            dma((ny * nc,)),
            dma((ny * nc,)),
            dma((nz,)),
            dma((nz,)),
        ],
        compiler_params=pltpu.CompilerParams(
            collective_id=0, has_side_effects=True, vmem_limit_bytes=48 * 1024 * 1024
        ),
    )(
        *[
            pltpu.with_memory_space_constraint(operand, pltpu.HBM)
            for operand in (
                element_slot,
                lid_noslip.reshape(1, -1),
                flat,
                *[jnp.asarray(table) for table in (slopes, stiff, geometry, to_planes, to_modes)],
            )
        ]
    )
    return result.reshape(3, PS, PS, ER, LANES).transpose(0, 3, 1, 2, 4)


def solution(mesh):
    n_elem = mesh.shape["elem"]
    nc = 2
    nz = min(8, n_elem // nc)
    ny = n_elem // (nc * nz)
    return jax.shard_map(
        functools.partial(on_device, (ny, nz, nc)),
        mesh=mesh,
        in_specs=(P(None, "elem", None, None, "modes"), P("elem", None), P("modes")),
        out_specs=P(None, "elem", None, None, "modes"),
        check_vma=False,
    )
```

```python
import functools

import jax
import jax.numpy as jnp
import ml_dtypes
import numpy as np
from jax import lax
from jax.experimental import pallas as pl
from jax.experimental.pallas import tpu as pltpu
from jax.sharding import PartitionSpec as P

PS = 10
NODES = PS * PS
R = 112
TOP = 88
FACE = 16
FACE_AT = (0, NODES - PS - TOP)
MID = TOP - FACE
ENDS = NODES - MID
MOMENTS = 9
BULK = 80
M = 256
Q = 768
ER = 4
LANES = 128
LAMBDA_COEF = 20.0
INV_NU = 10.0
R_INNER = 1.0
SWIRL_SLOPE = -1.0 / 3.0
SWIRL_CURVE = 4.0 / 3.0
MESH = pl.DeviceIdType.MESH
F32 = jnp.float32
BF16 = jnp.bfloat16


def legendre_rows(abscissa, degree):
    table_rows = [abscissa * 0.0 + 1.0, abscissa.copy()]
    for degree_now in range(2, degree + 1):
        table_rows.append(
            ((2 * degree_now - 1) * abscissa * table_rows[-1] - (degree_now - 1) * table_rows[-2])
            / degree_now
        )
    return table_rows


def gll_tables(points):
    degree = points - 1
    abscissa = -np.cos(np.pi * np.arange(points) / degree)
    for _ in range(60):
        legendre = legendre_rows(abscissa, degree)
        abscissa = abscissa - (abscissa * legendre[degree] - legendre[degree - 1]) / (
            points * legendre[degree]
        )
    legendre = legendre_rows(abscissa, degree)
    last_row = legendre[degree]
    weights = 2.0 / (degree * points * last_row**2)
    identity = np.eye(points)
    distance = abscissa[:, None] - abscissa[None, :] + identity
    derivative = last_row[:, None] / (last_row[None, :] * distance) * (1.0 - identity)
    derivative[0, 0] = -degree * points / 4.0
    derivative[degree, degree] = degree * points / 4.0
    return abscissa, weights, derivative


def halves(values):
    high = values.astype(ml_dtypes.bfloat16)
    low = (values - high.astype(np.float64)).astype(ml_dtypes.bfloat16)
    return high, low


@functools.cache
def constants():
    xi, w, deriv = gll_tables(PS)
    eye = np.eye(PS)
    radius = R_INNER + (np.arange(ER)[:, None] + 0.5 * (xi[None, :] + 1.0)) / ER
    ww = np.outer(w, w)

    def operator(rows):
        padded = np.zeros((R, LANES))
        padded[:NODES, :NODES] = rows
        high, low = halves(padded)
        return np.concatenate([high, high, low], axis=1)

    slope_r = operator(2.0 * ER * np.kron(eye, deriv))
    slope_z = operator(2.0 * ER * np.kron(deriv, eye))
    slopes = np.concatenate([slope_r, slope_z], axis=0)

    stiff, stiff_diag = [], np.zeros((ER, PS, PS))
    for ir in range(ER):
        along_i = deriv.T @ np.diag(w * radius[ir]) @ deriv
        along_j = deriv.T @ np.diag(w) @ deriv
        whole = np.kron(np.diag(w), along_i) + np.kron(along_j, np.diag(w * radius[ir]))
        stiff_diag[ir] = np.diag(whole).reshape(PS, PS).T
        stiff.append(operator(whole - np.diag(np.diag(whole))))
    stiff = np.stack(stiff)

    quarter_h = 0.25 / (ER * ER)
    mass_r = ww[None] * quarter_h * radius[:, :, None]
    mass_over_r = ww[None] * quarter_h / radius[:, :, None]

    def radial_sum(values):
        total = values.copy()
        total[:-1, -1] += values[1:, 0]
        total[1:, 0] += values[:-1, -1]
        return total

    diag_fixed = radial_sum(stiff_diag + LAMBDA_COEF * mass_r)
    diag_square = radial_sum(mass_over_r)
    diag_fixed[0, 0] = 0.0
    diag_fixed[-1, -1] = 0.0

    geometry = np.zeros((3 * ER + 2, R, LANES))
    for part, values in enumerate((mass_r, diag_fixed, diag_square)):
        rows = values.transpose(0, 2, 1).reshape(ER, NODES, 1)
        geometry[part * ER : (part + 1) * ER, :NODES] = rows
    geometry[3 * ER] = 1.0
    geometry[3 * ER, :NODES] = (R_INNER + 0.5 * (np.tile(xi, PS) + 1.0) / ER)[:, None]
    geometry[3 * ER + 1, :PS] = 1.0
    geometry[3 * ER + 1, NODES - PS : NODES] = 2.0

    modes = np.arange(M)
    angles = (modes[:, None] * np.arange(Q)[None, :] % Q) * (2.0 * np.pi / Q)
    weight = np.where(modes == 0, 1.0, 2.0)[:, None]
    inverse = np.stack([weight * np.cos(angles), -weight * np.sin(angles)], axis=1)
    inverse = inverse.reshape(2 * M // LANES, LANES, Q)
    high, low = halves(inverse)
    to_planes = np.concatenate([high, high, low], axis=1)
    forward = np.stack([np.cos(angles), -np.sin(angles)], axis=1) / Q
    forward = forward.reshape(2 * M // LANES, LANES, Q).transpose(0, 2, 1)
    high, low = halves(forward)
    to_modes = np.concatenate([high, low], axis=2)
    return slopes, stiff, geometry.astype(np.float32), to_planes, to_modes


def split(values):
    high = values.astype(BF16)
    low = (values - high.astype(F32)).astype(BF16)
    return high, low


def dot(left, right):
    return jnp.dot(left, right, preferred_element_type=F32)


def kernel(
    grid_shape,
    slot_hbm,
    lid_hbm,
    vel_hbm,
    slopes_hbm,
    stiff_hbm,
    geo_hbm,
    planes_hbm,
    modes_hbm,
    out_ref,
    slot_ref,
    lid_ref,
    vel_r,
    vel_t,
    vel_z,
    cells,
    recv,
    slopes,
    stiff,
    geo,
    to_planes,
    to_modes,
    rhs,
    fields,
    planes,
    push_hi,
    push_lo,
    side_hi,
    side_lo,
    sendb,
    back,
    side_out,
    side_in,
    side_send,
    side_back,
    jac,
    vec,
    img,
    ordered,
    krhs,
    face_in,
    moment,
    red_a,
    red_b,
    local_sem,
    fwd_send,
    fwd_recv,
    bwd_send,
    bwd_recv,
    side_sems,
    fb_send,
    fb_recv,
    halo_send,
    halo_recv,
    a_send,
    a_recv,
    b_send,
    b_recv,
):
    ny, nz, nc = grid_shape
    n_elem = ny * nz * nc
    n_modes = ER
    mi = lax.axis_index("modes")
    e = lax.axis_index("elem")
    core = lax.rem(e, nc)
    zc = lax.rem(e // nc, nz)
    yc = e // (nc * nz)
    size_a = ny * nc
    rank_a = yc * nc + core

    def member_a(t):
        return ((t // nc) * nz + zc) * nc + lax.rem(t, nc)

    def member_b(t):
        return (yc * nz + t) * nc + core

    above = lax.rem(e + 1, n_elem)
    below = lax.rem(e + n_elem - 1, n_elem)

    span = NODES * ER
    vel = (vel_r, vel_t, vel_z)
    local_pairs = [
        *[
            (vel_hbm.at[pl.ds(s * span, span)], vel[s])
            for s in range(3)
        ],
        (slopes_hbm, slopes),
        (planes_hbm, to_planes),
        (geo_hbm, geo),
        (slot_hbm, slot_ref),
        (lid_hbm, lid_ref),
        (modes_hbm, to_modes),
        (stiff_hbm, stiff),
    ]
    local = [
        pltpu.make_async_copy(src, dst, local_sem.at[i]) for i, (src, dst) in enumerate(local_pairs)
    ]
    for copy in local:
        copy.start()

    for g in range(ER):
        for s in range(3):
            recv[g, s, R - 16 :, :] = jnp.zeros((16, LANES), F32)
            img[0, s, g, TOP + FACE :, :] = jnp.zeros((R - TOP - FACE, LANES), F32)
            side_back[g, s, 2 * FACE - 8 :, :] = jnp.zeros((8, LANES), F32)
    no_rows = jnp.zeros((LANES - R, 3 * LANES), BF16)
    for part in range(3):
        rhs[part * LANES + R : (part + 1) * LANES, :] = no_rows
        for g in range(ER):
            krhs[g, part * LANES + R : (part + 1) * LANES, :] = no_rows
    moment[...] = jnp.zeros_like(moment)

    def gather_cell(g, s, target):
        held = slot_ref[0, g]
        for j in range(PS):
            rows = pl.ds(j * ER + held, PS, stride=ER * PS)
            target[g, s, j * PS : (j + 1) * PS, :] = vel[s][rows, :]

    barrier = pltpu.get_barrier_semaphore()
    greeted = [(lax.rem(mi + t, n_modes), e) for t in range(1, n_modes)]
    greeted += [(mi, above), (mi, below)]
    greeted += [(mi, member_a(lax.rem(rank_a + t, size_a))) for t in range(1, size_a)]
    greeted += [(mi, member_b(lax.rem(zc + t, nz))) for t in range(1, nz)]
    for who in greeted:
        pl.semaphore_signal(barrier, inc=1, device_id=who, device_id_type=MESH)
    pl.semaphore_wait(barrier, len(greeted))

    forward = {}
    local[6].wait()
    for off, s in [(off, s) for off in (1, 3, 2) for s in range(3)]:
        if off == 1:
            local[s].wait()
        to = lax.rem(mi + off, n_modes)
        gather_cell(to, s, cells)
        forward[off, s] = pltpu.make_async_remote_copy(
            src_ref=cells.at[to, s, pl.ds(0, NODES)],
            dst_ref=recv.at[mi, s, pl.ds(0, NODES)],
            send_sem=fwd_send.at[off, s],
            recv_sem=fwd_recv.at[off, s],
            device_id=(to, e),
            device_id_type=MESH,
        )
        forward[off, s].start()

    lane = lax.broadcasted_iota(jnp.int32, (1, LANES), 1)
    even = lax.rem(lane, 2) == 0
    pair = (lane // 2).astype(F32)

    def times_unit(values):
        return jnp.where(even, -pltpu.roll(values, LANES - 1, 1), pltpu.roll(values, 1, 1))

    def pair_sum(values):
        return values + jnp.where(even, pltpu.roll(values, LANES - 1, 1), pltpu.roll(values, 1, 1))

    for s in range(3):
        gather_cell(mi, s, recv)
    for copy in (*local[3:6], local[7]):
        copy.wait()

    cell_radius = mi.astype(F32) * (1.0 / ER)
    radius = geo[3 * ER, :, :] + cell_radius
    inv_radius = 1.0 / radius
    swirl_base = SWIRL_SLOPE * radius + SWIRL_CURVE * inv_radius

    def slope_of(block, comps, rows):
        for s in comps:
            high, low = split(block[s])
            cols = slice(s * LANES, (s + 1) * LANES)
            rhs[0:R, cols] = high
            rhs[LANES : LANES + R, cols] = low
            rhs[2 * LANES : 2 * LANES + R, cols] = high
        return dot(slopes[0:rows, :], rhs[:, comps[0] * LANES : (comps[-1] + 1) * LANES])

    def add_fields(values, source, half, first):
        for f, field in enumerate(values):
            high, low = split(field)
            rows = slice((3 * half + f) * R, (3 * half + f + 1) * R)
            fields[rows, 0:LANES] = high
            fields[rows, LANES : 2 * LANES] = low
            fields[rows, 2 * LANES :] = high
        rows = slice(3 * half * R, 3 * (half + 1) * R)
        terms = dot(fields[rows, :], to_planes[source])
        if first:
            planes[rows, :] = terms
        else:
            planes[rows, :] += terms

    def add_modes(block, source, first, arrived):
        wave = pair + (source * (LANES // 2)).astype(F32)
        arrived(0)
        arrived(1)
        slope = slope_of(block, (0, 1), 2 * R)
        u_r, u_t = block[0], block[1]
        d_z = [slope[R:, s * LANES : (s + 1) * LANES] for s in range(2)]
        curl_z = slope[:R, LANES:] + (u_t - wave * times_unit(u_r)) * inv_radius
        add_fields((u_r, u_t, curl_z), source, 0, first)
        arrived(2)
        slope = slope_of(block, (2,), R)
        u_z = block[2]
        curl_r = wave * times_unit(u_z) * inv_radius - d_z[1]
        add_fields((u_z, curl_r, d_z[0] - slope), source, 1, first)

    add_modes(recv.at[mi], mi, True, lambda s: None)

    lid = lid_ref[...].astype(BF16)
    wide = lax.broadcasted_iota(jnp.int32, (LANES // 2, LANES), 1) // 2
    tall = lax.broadcasted_iota(jnp.int32, (LANES // 2, LANES), 0)
    noslip = dot(lid, (wide == tall).astype(BF16))
    side = geo[3 * ER + 1, :, :]
    low_side, high_side = side == 1.0, side == 2.0
    at_low, at_high = (e == 0).astype(F32), (e == n_elem - 1).astype(F32)
    lid_rows = jnp.where(low_side, at_low, 0.0) + jnp.where(high_side, at_high, 0.0)
    sharing = 1.0 + jnp.where(low_side, 1.0 - at_low, 0.0) + jnp.where(high_side, 1.0 - at_high, 0.0)
    wave_own = pair + (mi * (LANES // 2)).astype(F32)
    for s, offset in enumerate((1.0, -1.0, 0.0)):
        square = (wave_own + offset) * (wave_own + offset)
        lid_keep = 1.0 - lid_rows * (noslip if s < 2 else 1.0)
        for g in range(ER):
            fixed = geo[ER + g]
            diag = (fixed + square * geo[2 * ER + g]) * sharing
            jac[s, g] = jnp.where(fixed > 0.0, lid_keep / jnp.where(fixed > 0.0, diag, 1.0), 0.0)

    for off in (1, 3, 2):
        source = lax.rem(mi + n_modes - off, n_modes)
        add_modes(recv.at[source], source, False, lambda s: forward[off, s].wait_recv())

    def push_rows(start, to_hi, to_lo, first, pitch):
        def field(f, cols):
            return planes[pl.ds(pl.multiple_of(f * R + start, 8), FACE), cols]

        rad = geo[3 * ER, pl.ds(start, FACE), :] + cell_radius
        swirl = SWIRL_SLOPE * rad + SWIRL_CURVE / rad
        swirl = jnp.concatenate([swirl] * 3, axis=1)
        spin = 2.0 * SWIRL_SLOPE
        for cols in (slice(0, 3 * LANES), slice(3 * LANES, 6 * LANES)):
            u_r, u_t, w_z, u_z, w_r, w_t = [field(f, cols) for f in range(6)]
            turned = u_t + swirl
            results = (
                turned * w_z - u_z * w_t + spin * u_t,
                u_z * w_r - u_r * w_z - spin * u_r,
                u_r * w_t - turned * w_r,
            )
            for s, values in enumerate(results):
                high, low = split(values)
                rows = pl.ds(pl.multiple_of(first + s * pitch, FACE), FACE)
                to_hi[rows, cols] = high
                to_lo[rows, cols] = low

    def bulk_step(step, _):
        start = pl.multiple_of(step * FACE, FACE)
        push_rows(start + FACE, push_hi, push_lo, start, BULK)
        return 0

    lax.fori_loop(0, BULK // FACE, bulk_step, 0, unroll=True)

    def coefficients(high, low, chunk):
        two = dot(high[...], to_modes[chunk])
        one = dot(low[...], to_modes[chunk, :, 0:LANES])
        return INV_NU * (two[:, :LANES] + (two[:, LANES:] + one))

    backward = {}

    def return_bulk(off):
        to = lax.rem(mi + off, n_modes)
        result = coefficients(push_hi, push_lo, to)
        for s in range(3):
            force = result[s * BULK : (s + 1) * BULK] + LAMBDA_COEF * recv[to, s, FACE : FACE + BULK, :]
            if off == 0:
                back[mi, s] = force
            else:
                sendb[off, s] = force
        if off:
            backward[off] = pltpu.make_async_remote_copy(
                src_ref=sendb.at[off, :, pl.ds(0, MID)],
                dst_ref=back.at[mi, :, pl.ds(0, MID)],
                send_sem=bwd_send.at[off],
                recv_sem=bwd_recv.at[off],
                device_id=(to, e),
                device_id_type=MESH,
            )
            backward[off].start()

    local[8].wait()
    return_bulk(2)
    for side, start in enumerate((0, TOP)):
        push_rows(start, side_hi, side_lo, side * FACE, 2 * FACE)
    for chunk in range(n_modes):
        result = coefficients(side_hi, side_lo, chunk)
        for s in range(3):
            for side, start in enumerate((0, TOP)):
                rows = slice((2 * s + side) * FACE, (2 * s + side + 1) * FACE)
                force = result[rows] + LAMBDA_COEF * recv[chunk, s, start : start + FACE, :]
                side_out[side, chunk, s] = force
    side_copies = []
    for side, who in ((0, below), (1, above)):
        copy = pltpu.make_async_remote_copy(
            src_ref=side_out.at[side, :, :, pl.ds(FACE_AT[side], PS)],
            dst_ref=side_in.at[1 - side, :, :, pl.ds(FACE_AT[1 - side], PS)],
            send_sem=side_sems.at[0, side],
            recv_sem=side_sems.at[1, 1 - side],
            device_id=(mi, who),
            device_id_type=MESH,
        )
        copy.start()
        side_copies.append(copy)
    for off in (1, 3, 0):
        return_bulk(off)

    block_row = lax.broadcasted_iota(jnp.int32, (FACE, LANES), 0)
    met = (
        (block_row < PS) & (e > 0),
        (block_row >= FACE_AT[1]) & (block_row < FACE_AT[1] + PS) & (e < n_elem - 1),
    )

    def meet(side, other):
        return jnp.where(met[side], other, 0.0)

    for copy in side_copies:
        copy.wait_recv()
    side_returns = []
    for off in (2, 1, 3, 0):
        to = lax.rem(mi + off, n_modes)
        for s in range(3):
            for side in range(2):
                total = side_out[side, to, s] + meet(side, side_in[side, to, s])
                rows = slice(side * FACE, (side + 1) * FACE)
                if off == 0:
                    side_back[mi, s, rows, :] = total
                else:
                    side_send[off, s, rows, :] = total
        if off:
            copy = pltpu.make_async_remote_copy(
                src_ref=side_send.at[off, :, pl.ds(0, ENDS)],
                dst_ref=side_back.at[mi, :, pl.ds(0, ENDS)],
                send_sem=fb_send.at[off],
                recv_sem=fb_recv.at[off],
                device_id=(to, e),
                device_id_type=MESH,
            )
            copy.start()
            side_returns.append(copy)
    local[9].wait()
    for off in (1, 3, 2):
        backward[off].wait_recv()
    for copy in side_returns:
        copy.wait_recv()

    for g in range(ER):
        pieces = (
            (slice(0, FACE), [side_back[g, s, 0:FACE, :] for s in range(3)]),
            (slice(FACE, TOP), [back[g, s, 0:MID, :] for s in range(3)]),
            (slice(TOP, TOP + FACE), [side_back[g, s, FACE:, :] for s in range(3)]),
        )
        for rows, force in pieces:
            turned = times_unit(force[1])
            mass = geo[g, rows, :]
            img[0, 0, g, rows, :] = mass * (force[0] + turned)
            img[0, 1, g, rows, :] = mass * (force[0] - turned)
            img[0, 2, g, rows, :] = mass * force[2]

    halos = []

    def send_faces(k):
        pairs = []
        for side, start, who in ((0, 0, below), (1, NODES - PS, above)):
            copy = pltpu.make_async_remote_copy(
                src_ref=img.at[k, :, :, pl.ds(start, PS)],
                dst_ref=face_in.at[k - 1, 1 - side, :, :, pl.ds(FACE_AT[1 - side], PS)],
                send_sem=halo_send.at[k - 1, side],
                recv_sem=halo_recv.at[k - 1, 1 - side],
                device_id=(mi, who),
                device_id_type=MESH,
            )
            copy.start()
            pairs.append(copy)
        halos.append(pairs)

    def inner_part(k):
        for s in range(3):
            for g in range(ER):
                vec[k, s, g] = img[k, s, g]
            for g in range(ER - 1):
                last = pl.ds(2 * PS - 1, PS - 2, stride=PS)
                first = pl.ds(PS, PS - 2, stride=PS)
                shared = img[k, s, g, last, :] + img[k, s, g + 1, first, :]
                vec[k, s, g, last, :] = shared
                vec[k, s, g + 1, first, :] = shared
            for g in range(ER):
                vec[k, s, g, FACE:TOP, :] = vec[k, s, g, FACE:TOP, :] * jac[s, g, FACE:TOP, :]
                split_rows(k, g, s, FACE, BULK)

    def outer_part(k):
        if k > 0:
            for copy in halos[k - 1]:
                copy.wait_recv()
        for side, start, last in ((0, 0, PS - 1), (1, TOP, PS + 1)):
            rows = slice(start, start + FACE)
            for s in range(3):
                block = [vec[k, s, g, rows, :] for g in range(ER)]
                if k > 0:
                    block = [block[g] + meet(side, face_in[k - 1, side, s, g]) for g in range(ER)]
                for g in range(ER):
                    total = block[g]
                    if g + 1 < ER:
                        nearby = pltpu.roll(block[g + 1], PS - 1, 0)
                        total = total + jnp.where(block_row == last, nearby, 0.0)
                    if g > 0:
                        nearby = pltpu.roll(block[g - 1], FACE - PS + 1, 0)
                        total = total + jnp.where(block_row == last - PS + 1, nearby, 0.0)
                    vec[k, s, g, rows, :] = total * jac[s, g, rows, :]

    def split_rows(k, g, s, start, stop):
        high, low = split(vec[k, s, g, start:stop, :])
        cols = slice(s * LANES, (s + 1) * LANES)
        krhs[g, start:stop, cols] = high
        krhs[g, LANES + start : LANES + stop, cols] = low
        krhs[g, 2 * LANES + start : 2 * LANES + stop, cols] = high

    def apply_stiff(k):
        for g in range(ER):
            for s in range(3):
                split_rows(k, g, s, 0, FACE)
                split_rows(k, g, s, BULK, R)
            image = dot(stiff[g], krhs[g])
            for s in range(3):
                img[k + 1, s, g] = image[:, s * LANES : (s + 1) * LANES]

    share = 1.0 / sharing

    def inner(k, left, right):
        for s in range(3):
            products = vec[left, s, 0] * img[right, s, 0]
            for g in range(1, ER):
                products = products + vec[left, s, g] * img[right, s, g]
            if right == 0:
                products = products * share
            total = jnp.sum(products, axis=0, keepdims=True)
            index = k * 3 + s
            at = index % MOMENTS
            moment[index // MOMENTS, at : at + 1, :] = total

    inner_part(0)
    outer_part(0)
    apply_stiff(0)
    send_faces(1)
    inner(0, 0, 0)
    inner(1, 0, 1)
    inner_part(1)
    outer_part(1)
    apply_stiff(1)
    send_faces(2)
    inner(2, 1, 1)
    inner(3, 1, 2)
    inner_part(2)
    outer_part(2)
    apply_stiff(2)
    inner(4, 2, 2)
    inner(5, 2, 3)

    def arrange():
        for slot in range(ER):
            held = jnp.int32(0)
            for g in range(ER):
                held = jnp.where(slot_ref[0, g] == slot, g, held)
            for k in range(3):
                for s in range(3):
                    for j in range(PS):
                        rows = pl.ds(j * ER + slot, PS, stride=ER * PS)
                        ordered[k, s, rows, :] = vec[k, s, held, j * PS : (j + 1) * PS, :]

    def exchange(buffer, rank, size, member, send_sems, recv_sems, meanwhile):
        copies = []
        for off in range(1, size):
            copy = pltpu.make_async_remote_copy(
                src_ref=buffer.at[rank, pl.ds(0, MOMENTS)],
                dst_ref=buffer.at[rank, pl.ds(0, MOMENTS)],
                send_sem=send_sems.at[off],
                recv_sem=recv_sems.at[off],
                device_id=(mi, member(lax.rem(rank + off, size))),
                device_id_type=MESH,
            )
            copy.start()
            copies.append(copy)
        meanwhile()
        for copy in copies:
            copy.wait_recv()
        total = buffer[0, 0:MOMENTS, :]
        for t in range(1, size):
            total = total + buffer[t, 0:MOMENTS, :]
        return total, copies

    red_a[rank_a] = jnp.where(even, pair_sum(moment[0]), pair_sum(moment[1]))
    total, copies_a = exchange(red_a, rank_a, size_a, member_a, a_send, a_recv, arrange)
    red_b[zc, 0:MOMENTS, :] = total
    total, copies_b = exchange(red_b, zc, nz, member_b, b_send, b_recv, lambda: None)
    first = jnp.where(even, total, pltpu.roll(total, 1, 1))
    second = jnp.where(even, pltpu.roll(total, LANES - 1, 1), total)

    coefs = []
    for s in range(3):
        h = [(first if k < 3 else second)[(k % 3) * 3 + s : (k % 3) * 3 + s + 1] for k in range(6)]
        g00, g01, g02, g12, g22 = [h[k] + h[k + 1] for k in range(5)]
        g11 = g02
        ratio1, ratio2 = g01 / g00, g02 / g00
        d1 = g11 - ratio1 * g01
        left = g12 - ratio1 * g02
        ratio = left / d1
        d2 = g22 - ratio2 * g02 - ratio * left
        y1 = h[1] - ratio1 * h[0]
        y2 = h[2] - ratio2 * h[0] - ratio * y1
        c2 = y2 / d2
        c1 = y1 / d1 - ratio * c2
        c0 = h[0] / g00 - ratio1 * c1 - ratio2 * c2
        coefs.append((c0, c1, c2))

    block = 2 * ER * PS
    for start in range(0, span, block):
        rows = slice(start, start + block)
        plus, minus, axial = [
            coefs[s][0] * ordered[0, s, rows, :]
            + coefs[s][1] * ordered[1, s, rows, :]
            + coefs[s][2] * ordered[2, s, rows, :]
            for s in range(3)
        ]
        results = ((plus + minus) * 0.5, times_unit(minus - plus) * 0.5, axial)
        for s, values in enumerate(results):
            out_ref[s * span + start : s * span + start + block, :] = values

    sent = (forward.values(), backward.values(), side_copies, side_returns, copies_a, copies_b)
    for copies in (*sent, *halos):
        for copy in copies:
            copy.wait_send()


def on_device(grid_shape, velocity, element_slot, lid_noslip):
    ny, nz, nc = grid_shape
    slopes, stiff, geometry, to_planes, to_modes = constants()
    vmem = pltpu.VMEM
    dma = pltpu.SemaphoreType.DMA
    flat = velocity.transpose(0, 2, 3, 1, 4).reshape(3 * NODES * ER, LANES)
    result = pl.pallas_call(
        functools.partial(kernel, grid_shape),
        out_shape=vmem((3 * NODES * ER, LANES), F32),
        in_specs=[pl.BlockSpec(memory_space=pltpu.HBM)] * 8,
        out_specs=pl.BlockSpec(memory_space=vmem),
        scratch_shapes=[
            pltpu.SMEM((1, ER), jnp.int32),
            vmem((1, LANES // 2), jnp.int32),
            *[vmem((NODES * ER, LANES), F32)] * 3,
            vmem((ER, 3, R, LANES), F32),
            vmem((ER, 3, R, LANES), F32),
            vmem(slopes.shape, BF16),
            vmem(stiff.shape, BF16),
            vmem(geometry.shape, F32),
            vmem(to_planes.shape, BF16),
            vmem(to_modes.shape, BF16),
            vmem((3 * LANES, 3 * LANES), BF16),
            vmem((6 * R, 3 * LANES), BF16),
            vmem((6 * R, Q), F32),
            vmem((3 * BULK, Q), BF16),
            vmem((3 * BULK, Q), BF16),
            vmem((6 * FACE, Q), BF16),
            vmem((6 * FACE, Q), BF16),
            vmem((ER, 3, BULK, LANES), F32),
            vmem((ER, 3, BULK, LANES), F32),
            vmem((2, ER, 3, FACE, LANES), F32),
            vmem((2, ER, 3, FACE, LANES), F32),
            vmem((ER, 3, 2 * FACE, LANES), F32),
            vmem((ER, 3, 2 * FACE, LANES), F32),
            vmem((3, ER, R, LANES), F32),
            vmem((3, 3, ER, R, LANES), F32),
            vmem((4, 3, ER, R, LANES), F32),
            vmem((3, 3, NODES * ER, LANES), F32),
            vmem((ER, 3 * LANES, 3 * LANES), BF16),
            vmem((2, 2, 3, ER, FACE, LANES), F32),
            vmem((2, 16, LANES), F32),
            vmem((ny * nc, 16, LANES), F32),
            vmem((nz, 16, LANES), F32),
            dma((10,)),
            dma((ER, 3)),
            dma((ER, 3)),
            dma((ER,)),
            dma((ER,)),
            dma((2, 2)),
            dma((ER,)),
            dma((ER,)),
            dma((2, 2)),
            dma((2, 2)),
            dma((ny * nc,)),
            dma((ny * nc,)),
            dma((nz,)),
            dma((nz,)),
        ],
        compiler_params=pltpu.CompilerParams(
            collective_id=0, has_side_effects=True, vmem_limit_bytes=48 * 1024 * 1024
        ),
    )(
        *[
            pltpu.with_memory_space_constraint(operand, pltpu.HBM)
            for operand in (
                element_slot,
                lid_noslip.reshape(1, -1),
                flat,
                *[jnp.asarray(table) for table in (slopes, stiff, geometry, to_planes, to_modes)],
            )
        ]
    )
    return result.reshape(3, PS, PS, ER, LANES).transpose(0, 3, 1, 2, 4)


def solution(mesh):
    n_elem = mesh.shape["elem"]
    nc = 2
    nz = min(8, n_elem // nc)
    ny = n_elem // (nc * nz)
    return jax.shard_map(
        functools.partial(on_device, (ny, nz, nc)),
        mesh=mesh,
        in_specs=(P(None, "elem", None, None, "modes"), P("elem", None), P("modes")),
        out_specs=P(None, "elem", None, None, "modes"),
        check_vma=False,
    )
```

```python
import functools

import jax
import jax.numpy as jnp
import ml_dtypes
import numpy as np
from jax import lax
from jax.experimental import pallas as pl
from jax.experimental.pallas import tpu as pltpu
from jax.sharding import PartitionSpec as P

PS = 10
NODES = PS * PS
R = 112
TOP = 88
FACE = 16
FACE_AT = (0, NODES - PS - TOP)
MID = TOP - FACE
ENDS = NODES - MID
MOMENTS = 9
BULK = 80
M = 256
Q = 768
ER = 4
LANES = 128
LAMBDA_COEF = 20.0
INV_NU = 10.0
R_INNER = 1.0
SWIRL_SLOPE = -1.0 / 3.0
SWIRL_CURVE = 4.0 / 3.0
MESH = pl.DeviceIdType.MESH
F32 = jnp.float32
BF16 = jnp.bfloat16


def legendre_rows(abscissa, degree):
    table_rows = [abscissa * 0.0 + 1.0, abscissa.copy()]
    for degree_now in range(2, degree + 1):
        table_rows.append(
            ((2 * degree_now - 1) * abscissa * table_rows[-1] - (degree_now - 1) * table_rows[-2])
            / degree_now
        )
    return table_rows


def gll_tables(points):
    degree = points - 1
    abscissa = -np.cos(np.pi * np.arange(points) / degree)
    for _ in range(60):
        legendre = legendre_rows(abscissa, degree)
        abscissa = abscissa - (abscissa * legendre[degree] - legendre[degree - 1]) / (
            points * legendre[degree]
        )
    legendre = legendre_rows(abscissa, degree)
    last_row = legendre[degree]
    weights = 2.0 / (degree * points * last_row**2)
    identity = np.eye(points)
    distance = abscissa[:, None] - abscissa[None, :] + identity
    derivative = last_row[:, None] / (last_row[None, :] * distance) * (1.0 - identity)
    derivative[0, 0] = -degree * points / 4.0
    derivative[degree, degree] = degree * points / 4.0
    return abscissa, weights, derivative


def halves(values):
    high = values.astype(ml_dtypes.bfloat16)
    low = (values - high.astype(np.float64)).astype(ml_dtypes.bfloat16)
    return high, low


@functools.cache
def constants():
    xi, w, deriv = gll_tables(PS)
    eye = np.eye(PS)
    radius = R_INNER + (np.arange(ER)[:, None] + 0.5 * (xi[None, :] + 1.0)) / ER
    ww = np.outer(w, w)

    def operator(rows):
        padded = np.zeros((R, LANES))
        padded[:NODES, :NODES] = rows
        high, low = halves(padded)
        return np.concatenate([high, high, low], axis=1)

    slope_r = operator(2.0 * ER * np.kron(eye, deriv))
    slope_z = operator(2.0 * ER * np.kron(deriv, eye))
    slopes = np.concatenate([slope_r, slope_z], axis=0)

    stiff, stiff_diag = [], np.zeros((ER, PS, PS))
    for ir in range(ER):
        along_i = deriv.T @ np.diag(w * radius[ir]) @ deriv
        along_j = deriv.T @ np.diag(w) @ deriv
        whole = np.kron(np.diag(w), along_i) + np.kron(along_j, np.diag(w * radius[ir]))
        stiff_diag[ir] = np.diag(whole).reshape(PS, PS).T
        stiff.append(operator(whole - np.diag(np.diag(whole))))
    stiff = np.stack(stiff)

    quarter_h = 0.25 / (ER * ER)
    mass_r = ww[None] * quarter_h * radius[:, :, None]
    mass_over_r = ww[None] * quarter_h / radius[:, :, None]

    def radial_sum(values):
        total = values.copy()
        total[:-1, -1] += values[1:, 0]
        total[1:, 0] += values[:-1, -1]
        return total

    diag_fixed = radial_sum(stiff_diag + LAMBDA_COEF * mass_r)
    diag_square = radial_sum(mass_over_r)
    diag_fixed[0, 0] = 0.0
    diag_fixed[-1, -1] = 0.0

    geometry = np.zeros((3 * ER + 2, R, LANES))
    for part, values in enumerate((mass_r, diag_fixed, diag_square)):
        rows = values.transpose(0, 2, 1).reshape(ER, NODES, 1)
        geometry[part * ER : (part + 1) * ER, :NODES] = rows
    geometry[3 * ER] = 1.0
    geometry[3 * ER, :NODES] = (R_INNER + 0.5 * (np.tile(xi, PS) + 1.0) / ER)[:, None]
    geometry[3 * ER + 1, :PS] = 1.0
    geometry[3 * ER + 1, NODES - PS : NODES] = 2.0

    modes = np.arange(M)
    angles = (modes[:, None] * np.arange(Q)[None, :] % Q) * (2.0 * np.pi / Q)
    weight = np.where(modes == 0, 1.0, 2.0)[:, None]
    inverse = np.stack([weight * np.cos(angles), -weight * np.sin(angles)], axis=1)
    inverse = inverse.reshape(2 * M // LANES, LANES, Q)
    high, low = halves(inverse)
    to_planes = np.concatenate([high, high, low], axis=1)
    forward = np.stack([np.cos(angles), -np.sin(angles)], axis=1) / Q
    forward = forward.reshape(2 * M // LANES, LANES, Q).transpose(0, 2, 1)
    high, low = halves(forward)
    to_modes = np.concatenate([high, low], axis=2)
    return slopes, stiff, geometry.astype(np.float32), to_planes, to_modes


def split(values):
    high = values.astype(BF16)
    low = (values - high.astype(F32)).astype(BF16)
    return high, low


def dot(left, right):
    return jnp.dot(left, right, preferred_element_type=F32)


def kernel(
    grid_shape,
    slot_hbm,
    lid_hbm,
    vel_hbm,
    slopes_hbm,
    stiff_hbm,
    geo_hbm,
    planes_hbm,
    modes_hbm,
    ordered,
    total_ref,
    slot_ref,
    lid_ref,
    vel_r,
    vel_t,
    vel_z,
    cells,
    recv,
    slopes,
    stiff,
    geo,
    to_planes,
    to_modes,
    rhs,
    fields,
    planes,
    push_hi,
    push_lo,
    side_hi,
    side_lo,
    sendb,
    back,
    side_out,
    side_in,
    side_send,
    side_back,
    jac,
    vec,
    img,
    krhs,
    face_in,
    moment,
    red_a,
    red_b,
    local_sem,
    fwd_send,
    fwd_recv,
    bwd_send,
    bwd_recv,
    side_sems,
    fb_send,
    fb_recv,
    halo_send,
    halo_recv,
    a_send,
    a_recv,
    b_send,
    b_recv,
):
    ny, nz, nc = grid_shape
    n_elem = ny * nz * nc
    n_modes = ER
    mi = lax.axis_index("modes")
    e = lax.axis_index("elem")
    core = lax.rem(e, nc)
    zc = lax.rem(e // nc, nz)
    yc = e // (nc * nz)
    size_a = ny * nc
    rank_a = yc * nc + core

    def member_a(t):
        return ((t // nc) * nz + zc) * nc + lax.rem(t, nc)

    def member_b(t):
        return (yc * nz + t) * nc + core

    above = lax.rem(e + 1, n_elem)
    below = lax.rem(e + n_elem - 1, n_elem)

    barrier = pltpu.get_barrier_semaphore()
    greeted = [(lax.rem(mi + t, n_modes), e) for t in range(1, n_modes)]
    greeted += [(mi, above), (mi, below)]
    greeted += [(mi, member_a(lax.rem(rank_a + t, size_a))) for t in range(1, size_a)]
    greeted += [(mi, member_b(lax.rem(zc + t, nz))) for t in range(1, nz)]
    for who in greeted:
        pl.semaphore_signal(barrier, inc=1, device_id=who, device_id_type=MESH)

    span = NODES * ER
    vel = (vel_r, vel_t, vel_z)
    local_pairs = [
        *[
            (vel_hbm.at[pl.ds(s * span, span)], vel[s])
            for s in range(3)
        ],
        (slopes_hbm, slopes),
        (planes_hbm, to_planes),
        (geo_hbm, geo),
        (slot_hbm, slot_ref),
        (lid_hbm, lid_ref),
        (modes_hbm, to_modes),
        (stiff_hbm, stiff),
    ]
    local = [
        pltpu.make_async_copy(src, dst, local_sem.at[i]) for i, (src, dst) in enumerate(local_pairs)
    ]
    for i in (6, 0, 1, 2, 3, 4, 5, 7, 8, 9):
        local[i].start()

    for g in range(ER):
        for s in range(3):
            recv[g, s, NODES:, :] = jnp.zeros((R - NODES, LANES), F32)
            img[0, s, g, TOP + FACE :, :] = jnp.zeros((R - TOP - FACE, LANES), F32)
            side_back[g, s, 2 * FACE - 8 :, :] = jnp.zeros((8, LANES), F32)
    no_rows = jnp.zeros((LANES - R, 3 * LANES), BF16)
    for part in range(3):
        rhs[part * LANES + R : (part + 1) * LANES, :] = no_rows
        for g in range(ER):
            krhs[g, part * LANES + R : (part + 1) * LANES, :] = no_rows
    moment[...] = jnp.zeros_like(moment)

    def gather_cell(g, s, target):
        held = slot_ref[0, g]
        for j in range(PS):
            rows = pl.ds(j * ER + held, PS, stride=ER * PS)
            target[g, s, j * PS : (j + 1) * PS, :] = vel[s][rows, :]

    local[6].wait()
    local[0].wait()
    for off in (1, 3, 2):
        gather_cell(lax.rem(mi + off, n_modes), 0, cells)
    pl.semaphore_wait(barrier, len(greeted))

    forward = {}
    for off, s in [(off, s) for off in (1, 3, 2) for s in range(3)]:
        if off == 1 and s > 0:
            local[s].wait()
        to = lax.rem(mi + off, n_modes)
        if s > 0:
            gather_cell(to, s, cells)
        forward[off, s] = pltpu.make_async_remote_copy(
            src_ref=cells.at[to, s, pl.ds(0, NODES)],
            dst_ref=recv.at[mi, s, pl.ds(0, NODES)],
            send_sem=fwd_send.at[off, s],
            recv_sem=fwd_recv.at[off, s],
            device_id=(to, e),
            device_id_type=MESH,
        )
        forward[off, s].start()

    lane = lax.broadcasted_iota(jnp.int32, (1, LANES), 1)
    even = lax.rem(lane, 2) == 0
    pair = (lane // 2).astype(F32)

    def times_unit(values):
        return jnp.where(even, -pltpu.roll(values, LANES - 1, 1), pltpu.roll(values, 1, 1))

    def pair_sum(values):
        return values + jnp.where(even, pltpu.roll(values, LANES - 1, 1), pltpu.roll(values, 1, 1))

    for s in range(3):
        gather_cell(mi, s, recv)
    for copy in (*local[3:6], local[7]):
        copy.wait()

    cell_radius = mi.astype(F32) * (1.0 / ER)
    radius = geo[3 * ER, :, :] + cell_radius
    inv_radius = 1.0 / radius
    swirl_base = SWIRL_SLOPE * radius + SWIRL_CURVE * inv_radius

    def slope_of(block, comps, rows):
        for s in comps:
            high, low = split(block[s])
            cols = slice(s * LANES, (s + 1) * LANES)
            rhs[0:R, cols] = high
            rhs[LANES : LANES + R, cols] = low
            rhs[2 * LANES : 2 * LANES + R, cols] = high
        return dot(slopes[0:rows, :], rhs[:, comps[0] * LANES : (comps[-1] + 1) * LANES])

    def add_fields(values, source, half, first):
        for f, field in enumerate(values):
            high, low = split(field)
            rows = slice((3 * half + f) * R, (3 * half + f + 1) * R)
            fields[rows, 0:LANES] = high
            fields[rows, LANES : 2 * LANES] = low
            fields[rows, 2 * LANES :] = high
        rows = slice(3 * half * R, 3 * (half + 1) * R)
        terms = dot(fields[rows, :], to_planes[source])
        if first:
            planes[rows, :] = terms
        else:
            planes[rows, :] += terms

    def add_modes(block, source, first, arrived):
        wave = pair + (source * (LANES // 2)).astype(F32)
        arrived(0)
        arrived(1)
        slope = slope_of(block, (0, 1), 2 * R)
        u_r, u_t = block[0], block[1]
        d_z = [slope[R:, s * LANES : (s + 1) * LANES] for s in range(2)]
        curl_z = slope[:R, LANES:] + (u_t - wave * times_unit(u_r)) * inv_radius
        add_fields((u_r, u_t, curl_z), source, 0, first)
        arrived(2)
        slope = slope_of(block, (2,), R)
        u_z = block[2]
        curl_r = wave * times_unit(u_z) * inv_radius - d_z[1]
        add_fields((u_z, curl_r, d_z[0] - slope), source, 1, first)

    add_modes(recv.at[mi], mi, True, lambda s: None)

    lid = lid_ref[...].astype(BF16)
    wide = lax.broadcasted_iota(jnp.int32, (LANES // 2, LANES), 1) // 2
    tall = lax.broadcasted_iota(jnp.int32, (LANES // 2, LANES), 0)
    noslip = dot(lid, (wide == tall).astype(BF16))
    side = geo[3 * ER + 1, :, :]
    low_side, high_side = side == 1.0, side == 2.0
    at_low, at_high = (e == 0).astype(F32), (e == n_elem - 1).astype(F32)
    lid_rows = jnp.where(low_side, at_low, 0.0) + jnp.where(high_side, at_high, 0.0)
    sharing = 1.0 + jnp.where(low_side, 1.0 - at_low, 0.0) + jnp.where(high_side, 1.0 - at_high, 0.0)
    wave_own = pair + (mi * (LANES // 2)).astype(F32)
    for s, offset in enumerate((1.0, -1.0, 0.0)):
        square = (wave_own + offset) * (wave_own + offset)
        lid_keep = 1.0 - lid_rows * (noslip if s < 2 else 1.0)
        for g in range(ER):
            fixed = geo[ER + g]
            diag = (fixed + square * geo[2 * ER + g]) * sharing
            jac[s, g] = jnp.where(fixed > 0.0, lid_keep / jnp.where(fixed > 0.0, diag, 1.0), 0.0)

    for off in (1, 3, 2):
        source = lax.rem(mi + n_modes - off, n_modes)
        add_modes(recv.at[source], source, False, lambda s: forward[off, s].wait_recv())

    def push_rows(start, to_hi, to_lo, first, pitch):
        def field(f, cols):
            return planes[pl.ds(pl.multiple_of(f * R + start, 8), FACE), cols]

        rad = geo[3 * ER, pl.ds(start, FACE), :] + cell_radius
        swirl = SWIRL_SLOPE * rad + SWIRL_CURVE / rad
        swirl = jnp.concatenate([swirl] * 3, axis=1)
        spin = 2.0 * SWIRL_SLOPE
        for cols in (slice(0, 3 * LANES), slice(3 * LANES, 6 * LANES)):
            u_r, u_t, w_z, u_z, w_r, w_t = [field(f, cols) for f in range(6)]
            turned = u_t + swirl
            results = (
                turned * w_z - u_z * w_t + spin * u_t,
                u_z * w_r - u_r * w_z - spin * u_r,
                u_r * w_t - turned * w_r,
            )
            for s, values in enumerate(results):
                high, low = split(values)
                rows = pl.ds(pl.multiple_of(first + s * pitch, FACE), FACE)
                to_hi[rows, cols] = high
                to_lo[rows, cols] = low

    def bulk_step(step, _):
        start = pl.multiple_of(step * FACE, FACE)
        push_rows(start + FACE, push_hi, push_lo, start, BULK)
        return 0

    lax.fori_loop(0, BULK // FACE, bulk_step, 0, unroll=True)

    def coefficients(high, low, chunk):
        two = dot(high[...], to_modes[chunk])
        one = dot(low[...], to_modes[chunk, :, 0:LANES])
        return INV_NU * (two[:, :LANES] + (two[:, LANES:] + one))

    backward = {}

    def return_bulk(off):
        to = lax.rem(mi + off, n_modes)
        result = coefficients(push_hi, push_lo, to)
        for s in range(3):
            force = result[s * BULK : (s + 1) * BULK] + LAMBDA_COEF * recv[to, s, FACE : FACE + BULK, :]
            if off == 0:
                back[mi, s] = force
            else:
                sendb[off, s] = force
        if off:
            backward[off] = pltpu.make_async_remote_copy(
                src_ref=sendb.at[off, :, pl.ds(0, MID)],
                dst_ref=back.at[mi, :, pl.ds(0, MID)],
                send_sem=bwd_send.at[off],
                recv_sem=bwd_recv.at[off],
                device_id=(to, e),
                device_id_type=MESH,
            )
            backward[off].start()

    local[8].wait()
    return_bulk(2)
    for side, start in enumerate((0, TOP)):
        push_rows(start, side_hi, side_lo, side * FACE, 2 * FACE)
    for chunk in range(n_modes):
        result = coefficients(side_hi, side_lo, chunk)
        for s in range(3):
            for side, start in enumerate((0, TOP)):
                rows = slice((2 * s + side) * FACE, (2 * s + side + 1) * FACE)
                force = result[rows] + LAMBDA_COEF * recv[chunk, s, start : start + FACE, :]
                side_out[side, chunk, s] = force
    side_copies = []
    for side, who in ((0, below), (1, above)):
        copy = pltpu.make_async_remote_copy(
            src_ref=side_out.at[side, :, :, pl.ds(FACE_AT[side], PS)],
            dst_ref=side_in.at[1 - side, :, :, pl.ds(FACE_AT[1 - side], PS)],
            send_sem=side_sems.at[0, side],
            recv_sem=side_sems.at[1, 1 - side],
            device_id=(mi, who),
            device_id_type=MESH,
        )
        copy.start()
        side_copies.append(copy)
    for off in (1, 3, 0):
        return_bulk(off)

    block_row = lax.broadcasted_iota(jnp.int32, (FACE, LANES), 0)
    met = (
        (block_row < PS) & (e > 0),
        (block_row >= FACE_AT[1]) & (block_row < FACE_AT[1] + PS) & (e < n_elem - 1),
    )

    def meet(side, other):
        return jnp.where(met[side], other, 0.0)

    for copy in side_copies:
        copy.wait_recv()
    side_returns = []
    for off in (2, 1, 3, 0):
        to = lax.rem(mi + off, n_modes)
        for s in range(3):
            for side in range(2):
                total = side_out[side, to, s] + meet(side, side_in[side, to, s])
                rows = slice(side * FACE, (side + 1) * FACE)
                if off == 0:
                    side_back[mi, s, rows, :] = total
                else:
                    side_send[off, s, rows, :] = total
        if off:
            copy = pltpu.make_async_remote_copy(
                src_ref=side_send.at[off, :, pl.ds(0, ENDS)],
                dst_ref=side_back.at[mi, :, pl.ds(0, ENDS)],
                send_sem=fb_send.at[off],
                recv_sem=fb_recv.at[off],
                device_id=(to, e),
                device_id_type=MESH,
            )
            copy.start()
            side_returns.append(copy)
    local[9].wait()
    for off in (1, 3, 2):
        backward[off].wait_recv()
    for copy in side_returns:
        copy.wait_recv()

    for g in range(ER):
        pieces = (
            (slice(0, FACE), [side_back[g, s, 0:FACE, :] for s in range(3)]),
            (slice(FACE, TOP), [back[g, s, 0:MID, :] for s in range(3)]),
            (slice(TOP, TOP + FACE), [side_back[g, s, FACE:, :] for s in range(3)]),
        )
        for rows, force in pieces:
            turned = times_unit(force[1])
            mass = geo[g, rows, :]
            img[0, 0, g, rows, :] = mass * (force[0] + turned)
            img[0, 1, g, rows, :] = mass * (force[0] - turned)
            img[0, 2, g, rows, :] = mass * force[2]

    halos = []

    def send_faces(k):
        pairs = []
        for side, start, who in ((0, 0, below), (1, NODES - PS, above)):
            copy = pltpu.make_async_remote_copy(
                src_ref=img.at[k, :, :, pl.ds(start, PS)],
                dst_ref=face_in.at[k - 1, 1 - side, :, :, pl.ds(FACE_AT[1 - side], PS)],
                send_sem=halo_send.at[k - 1, side],
                recv_sem=halo_recv.at[k - 1, 1 - side],
                device_id=(mi, who),
                device_id_type=MESH,
            )
            copy.start()
            pairs.append(copy)
        halos.append(pairs)

    def inner_part(k):
        for s in range(3):
            for g in range(ER):
                vec[k, s, g] = img[k, s, g]
            for g in range(ER - 1):
                last = pl.ds(2 * PS - 1, PS - 2, stride=PS)
                first = pl.ds(PS, PS - 2, stride=PS)
                shared = img[k, s, g, last, :] + img[k, s, g + 1, first, :]
                vec[k, s, g, last, :] = shared
                vec[k, s, g + 1, first, :] = shared
            for g in range(ER):
                vec[k, s, g, FACE:TOP, :] = vec[k, s, g, FACE:TOP, :] * jac[s, g, FACE:TOP, :]
                split_rows(k, g, s, FACE, BULK)

    def outer_part(k):
        if k > 0:
            for copy in halos[k - 1]:
                copy.wait_recv()
        for side, start, last in ((0, 0, PS - 1), (1, TOP, PS + 1)):
            rows = slice(start, start + FACE)
            for s in range(3):
                block = [vec[k, s, g, rows, :] for g in range(ER)]
                if k > 0:
                    block = [block[g] + meet(side, face_in[k - 1, side, s, g]) for g in range(ER)]
                for g in range(ER):
                    total = block[g]
                    if g + 1 < ER:
                        nearby = pltpu.roll(block[g + 1], PS - 1, 0)
                        total = total + jnp.where(block_row == last, nearby, 0.0)
                    if g > 0:
                        nearby = pltpu.roll(block[g - 1], FACE - PS + 1, 0)
                        total = total + jnp.where(block_row == last - PS + 1, nearby, 0.0)
                    vec[k, s, g, rows, :] = total * jac[s, g, rows, :]

    def split_rows(k, g, s, start, stop):
        high, low = split(vec[k, s, g, start:stop, :])
        cols = slice(s * LANES, (s + 1) * LANES)
        krhs[g, start:stop, cols] = high
        krhs[g, LANES + start : LANES + stop, cols] = low
        krhs[g, 2 * LANES + start : 2 * LANES + stop, cols] = high

    def apply_stiff(k):
        for g in range(ER):
            for s in range(3):
                split_rows(k, g, s, 0, FACE)
                split_rows(k, g, s, BULK, R)
            image = dot(stiff[g], krhs[g])
            for s in range(3):
                img[k + 1, s, g] = image[:, s * LANES : (s + 1) * LANES]

    share = 1.0 / sharing

    def inner(k, left, right):
        for s in range(3):
            products = vec[left, s, 0] * img[right, s, 0]
            for g in range(1, ER):
                products = products + vec[left, s, g] * img[right, s, g]
            if right == 0:
                products = products * share
            total = jnp.sum(products, axis=0, keepdims=True)
            index = k * 3 + s
            at = index % MOMENTS
            moment[index // MOMENTS, at : at + 1, :] = total

    inner_part(0)
    outer_part(0)
    apply_stiff(0)
    send_faces(1)
    inner(0, 0, 0)
    inner(1, 0, 1)
    inner_part(1)
    outer_part(1)
    apply_stiff(1)
    send_faces(2)
    inner(2, 1, 1)
    inner(3, 1, 2)
    inner_part(2)
    outer_part(2)
    apply_stiff(2)
    inner(4, 2, 2)
    inner(5, 2, 3)

    def arrange():
        for slot in range(ER):
            held = jnp.int32(0)
            for g in range(ER):
                held = jnp.where(slot_ref[0, g] == slot, g, held)
            for k in range(3):
                for s in range(3):
                    for j in range(PS):
                        rows = pl.ds(j * ER + slot, PS, stride=ER * PS)
                        ordered[k, s, rows, :] = vec[k, s, held, j * PS : (j + 1) * PS, :]

    def exchange(buffer, rank, size, member, send_sems, recv_sems, meanwhile):
        copies = []
        for off in range(1, size):
            copy = pltpu.make_async_remote_copy(
                src_ref=buffer.at[rank, pl.ds(0, MOMENTS)],
                dst_ref=buffer.at[rank, pl.ds(0, MOMENTS)],
                send_sem=send_sems.at[off],
                recv_sem=recv_sems.at[off],
                device_id=(mi, member(lax.rem(rank + off, size))),
                device_id_type=MESH,
            )
            copy.start()
            copies.append(copy)
        meanwhile()
        for copy in copies:
            copy.wait_recv()
        total = buffer[0, 0:MOMENTS, :]
        for t in range(1, size):
            total = total + buffer[t, 0:MOMENTS, :]
        return total, copies

    red_a[rank_a] = jnp.where(even, pair_sum(moment[0]), pair_sum(moment[1]))
    total, copies_a = exchange(red_a, rank_a, size_a, member_a, a_send, a_recv, arrange)
    red_b[zc, 0:MOMENTS, :] = total
    total, copies_b = exchange(red_b, zc, nz, member_b, b_send, b_recv, lambda: None)
    total_ref[...] = total

    sent = (forward.values(), backward.values(), side_copies, side_returns, copies_a, copies_b)
    for copies in (*sent, *halos):
        for copy in copies:
            copy.wait_send()


def combine(ordered, total_ref, out_hbm, out_ref, sems):
    span = NODES * ER
    lane = lax.broadcasted_iota(jnp.int32, (1, LANES), 1)
    even = lax.rem(lane, 2) == 0

    def times_unit(values):
        return jnp.where(even, -pltpu.roll(values, LANES - 1, 1), pltpu.roll(values, 1, 1))

    total = total_ref[...]
    first = jnp.where(even, total, pltpu.roll(total, 1, 1))
    second = jnp.where(even, pltpu.roll(total, LANES - 1, 1), total)

    coefs = []
    for s in range(3):
        h = [(first if k < 3 else second)[(k % 3) * 3 + s : (k % 3) * 3 + s + 1] for k in range(6)]
        g00, g01, g02, g12, g22 = [h[k] + h[k + 1] for k in range(5)]
        g11 = g02
        ratio1, ratio2 = g01 / g00, g02 / g00
        d1 = g11 - ratio1 * g01
        left = g12 - ratio1 * g02
        ratio = left / d1
        d2 = g22 - ratio2 * g02 - ratio * left
        y1 = h[1] - ratio1 * h[0]
        y2 = h[2] - ratio2 * h[0] - ratio * y1
        c2 = y2 / d2
        c1 = y1 / d1 - ratio * c2
        c0 = h[0] / g00 - ratio1 * c1 - ratio2 * c2
        coefs.append((c0, c1, c2))

    block = 2 * ER * PS
    copies = []
    for start in range(0, span, block):
        rows = slice(start, start + block)
        plus, minus, axial = [
            coefs[s][0] * ordered[0, s, rows, :]
            + coefs[s][1] * ordered[1, s, rows, :]
            + coefs[s][2] * ordered[2, s, rows, :]
            for s in range(3)
        ]
        results = ((plus + minus) * 0.5, times_unit(minus - plus) * 0.5, axial)
        for s, values in enumerate(results):
            out_ref[s * span + start : s * span + start + block, :] = values
            rows = pl.ds(s * span + start, block)
            copy = pltpu.make_async_copy(
                out_ref.at[rows], out_hbm.at[rows], sems.at[s, start // block]
            )
            copy.start()
            copies.append(copy)

    for copy in copies:
        copy.wait()


def on_device(grid_shape, velocity, element_slot, lid_noslip):
    ny, nz, nc = grid_shape
    slopes, stiff, geometry, to_planes, to_modes = constants()
    vmem = pltpu.VMEM
    dma = pltpu.SemaphoreType.DMA
    flat = velocity.transpose(0, 2, 3, 1, 4).reshape(3 * NODES * ER, LANES)
    ordered, total = pl.pallas_call(
        functools.partial(kernel, grid_shape),
        out_shape=(vmem((3, 3, NODES * ER, LANES), F32), vmem((MOMENTS, LANES), F32)),
        in_specs=[pl.BlockSpec(memory_space=pltpu.HBM)] * 8,
        out_specs=(pl.BlockSpec(memory_space=vmem),) * 2,
        scratch_shapes=[
            pltpu.SMEM((1, ER), jnp.int32),
            vmem((1, LANES // 2), jnp.int32),
            *[vmem((NODES * ER, LANES), F32)] * 3,
            vmem((ER, 3, R, LANES), F32),
            vmem((ER, 3, R, LANES), F32),
            vmem(slopes.shape, BF16),
            vmem(stiff.shape, BF16),
            vmem(geometry.shape, F32),
            vmem(to_planes.shape, BF16),
            vmem(to_modes.shape, BF16),
            vmem((3 * LANES, 3 * LANES), BF16),
            vmem((6 * R, 3 * LANES), BF16),
            vmem((6 * R, Q), F32),
            vmem((3 * BULK, Q), BF16),
            vmem((3 * BULK, Q), BF16),
            vmem((6 * FACE, Q), BF16),
            vmem((6 * FACE, Q), BF16),
            vmem((ER, 3, BULK, LANES), F32),
            vmem((ER, 3, BULK, LANES), F32),
            vmem((2, ER, 3, FACE, LANES), F32),
            vmem((2, ER, 3, FACE, LANES), F32),
            vmem((ER, 3, 2 * FACE, LANES), F32),
            vmem((ER, 3, 2 * FACE, LANES), F32),
            vmem((3, ER, R, LANES), F32),
            vmem((3, 3, ER, R, LANES), F32),
            vmem((4, 3, ER, R, LANES), F32),
            vmem((ER, 3 * LANES, 3 * LANES), BF16),
            vmem((2, 2, 3, ER, FACE, LANES), F32),
            vmem((2, 16, LANES), F32),
            vmem((ny * nc, 16, LANES), F32),
            vmem((nz, 16, LANES), F32),
            dma((10,)),
            dma((ER, 3)),
            dma((ER, 3)),
            dma((ER,)),
            dma((ER,)),
            dma((2, 2)),
            dma((ER,)),
            dma((ER,)),
            dma((2, 2)),
            dma((2, 2)),
            dma((ny * nc,)),
            dma((ny * nc,)),
            dma((nz,)),
            dma((nz,)),
        ],
        compiler_params=pltpu.CompilerParams(
            collective_id=0, has_side_effects=True, vmem_limit_bytes=48 * 1024 * 1024
        ),
    )(
        *[
            pltpu.with_memory_space_constraint(operand, pltpu.HBM)
            for operand in (
                element_slot,
                lid_noslip.reshape(1, -1),
                flat,
                *[jnp.asarray(table) for table in (slopes, stiff, geometry, to_planes, to_modes)],
            )
        ]
    )
    result = pl.pallas_call(
        combine,
        out_shape=jax.ShapeDtypeStruct((3 * NODES * ER, LANES), F32),
        in_specs=[pl.BlockSpec(memory_space=vmem)] * 2,
        out_specs=pl.BlockSpec(memory_space=pl.ANY),
        scratch_shapes=[vmem((3 * NODES * ER, LANES), F32), dma((3, 5))],
    )(*[pltpu.with_memory_space_constraint(held, pltpu.VMEM) for held in (ordered, total)])
    return result.reshape(3, PS, PS, ER, LANES).transpose(0, 3, 1, 2, 4)


def solution(mesh):
    n_elem = mesh.shape["elem"]
    nc = 2
    nz = min(8, n_elem // nc)
    ny = n_elem // (nc * nz)
    return jax.shard_map(
        functools.partial(on_device, (ny, nz, nc)),
        mesh=mesh,
        in_specs=(P(None, "elem", None, None, "modes"), P("elem", None), P("modes")),
        out_specs=P(None, "elem", None, None, "modes"),
        check_vma=False,
    )
```

```python
import functools

import jax
import jax.numpy as jnp
import ml_dtypes
import numpy as np
from jax import lax
from jax.experimental import pallas as pl
from jax.experimental.pallas import tpu as pltpu
from jax.sharding import PartitionSpec as P

PS = 10
NODES = PS * PS
R = 112
TOP = 88
FACE = 16
FACE_AT = (0, NODES - PS - TOP)
MID = TOP - FACE
ENDS = NODES - MID
MOMENTS = 9
BULK = 80
M = 256
Q = 768
ER = 4
LANES = 128
LAMBDA_COEF = 20.0
INV_NU = 10.0
R_INNER = 1.0
SWIRL_SLOPE = -1.0 / 3.0
SWIRL_CURVE = 4.0 / 3.0
MESH = pl.DeviceIdType.MESH
F32 = jnp.float32
BF16 = jnp.bfloat16


def legendre_rows(abscissa, degree):
    table_rows = [abscissa * 0.0 + 1.0, abscissa.copy()]
    for degree_now in range(2, degree + 1):
        table_rows.append(
            ((2 * degree_now - 1) * abscissa * table_rows[-1] - (degree_now - 1) * table_rows[-2])
            / degree_now
        )
    return table_rows


def gll_tables(points):
    degree = points - 1
    abscissa = -np.cos(np.pi * np.arange(points) / degree)
    for _ in range(60):
        legendre = legendre_rows(abscissa, degree)
        abscissa = abscissa - (abscissa * legendre[degree] - legendre[degree - 1]) / (
            points * legendre[degree]
        )
    legendre = legendre_rows(abscissa, degree)
    last_row = legendre[degree]
    weights = 2.0 / (degree * points * last_row**2)
    identity = np.eye(points)
    distance = abscissa[:, None] - abscissa[None, :] + identity
    derivative = last_row[:, None] / (last_row[None, :] * distance) * (1.0 - identity)
    derivative[0, 0] = -degree * points / 4.0
    derivative[degree, degree] = degree * points / 4.0
    return abscissa, weights, derivative


def halves(values):
    high = values.astype(ml_dtypes.bfloat16)
    low = (values - high.astype(np.float64)).astype(ml_dtypes.bfloat16)
    return high, low


@functools.cache
def constants():
    xi, w, deriv = gll_tables(PS)
    eye = np.eye(PS)
    radius = R_INNER + (np.arange(ER)[:, None] + 0.5 * (xi[None, :] + 1.0)) / ER
    ww = np.outer(w, w)

    def operator(rows):
        padded = np.zeros((R, LANES))
        padded[:NODES, :NODES] = rows
        high, low = halves(padded)
        return np.concatenate([high, high, low], axis=1)

    slope_r = operator(2.0 * ER * np.kron(eye, deriv))
    slope_z = operator(2.0 * ER * np.kron(deriv, eye))
    slopes = np.concatenate([slope_r, slope_z], axis=0)

    stiff, stiff_diag = [], np.zeros((ER, PS, PS))
    for ir in range(ER):
        along_i = deriv.T @ np.diag(w * radius[ir]) @ deriv
        along_j = deriv.T @ np.diag(w) @ deriv
        whole = np.kron(np.diag(w), along_i) + np.kron(along_j, np.diag(w * radius[ir]))
        stiff_diag[ir] = np.diag(whole).reshape(PS, PS).T
        stiff.append(operator(whole - np.diag(np.diag(whole))))
    stiff = np.stack(stiff)

    quarter_h = 0.25 / (ER * ER)
    mass_r = ww[None] * quarter_h * radius[:, :, None]
    mass_over_r = ww[None] * quarter_h / radius[:, :, None]

    def radial_sum(values):
        total = values.copy()
        total[:-1, -1] += values[1:, 0]
        total[1:, 0] += values[:-1, -1]
        return total

    diag_fixed = radial_sum(stiff_diag + LAMBDA_COEF * mass_r)
    diag_square = radial_sum(mass_over_r)
    diag_fixed[0, 0] = 0.0
    diag_fixed[-1, -1] = 0.0

    geometry = np.zeros((3 * ER + 2, R, LANES))
    for part, values in enumerate((mass_r, diag_fixed, diag_square)):
        rows = values.transpose(0, 2, 1).reshape(ER, NODES, 1)
        geometry[part * ER : (part + 1) * ER, :NODES] = rows
    geometry[3 * ER] = 1.0
    geometry[3 * ER, :NODES] = (R_INNER + 0.5 * (np.tile(xi, PS) + 1.0) / ER)[:, None]
    geometry[3 * ER + 1, :PS] = 1.0
    geometry[3 * ER + 1, NODES - PS : NODES] = 2.0

    modes = np.arange(M)
    angles = (modes[:, None] * np.arange(Q)[None, :] % Q) * (2.0 * np.pi / Q)
    weight = np.where(modes == 0, 1.0, 2.0)[:, None]
    inverse = np.stack([weight * np.cos(angles), -weight * np.sin(angles)], axis=1)
    inverse = inverse.reshape(2 * M // LANES, LANES, Q)
    high, low = halves(inverse)
    to_planes = np.concatenate([high, high, low], axis=1)
    forward = np.stack([np.cos(angles), -np.sin(angles)], axis=1) / Q
    forward = forward.reshape(2 * M // LANES, LANES, Q).transpose(0, 2, 1)
    high, low = halves(forward)
    to_modes = np.concatenate([high, low], axis=2)
    return slopes, stiff, geometry.astype(np.float32), to_planes, to_modes


def split(values):
    high = values.astype(BF16)
    low = (values - high.astype(F32)).astype(BF16)
    return high, low


def dot(left, right):
    return jnp.dot(left, right, preferred_element_type=F32)


def kernel(
    grid_shape,
    slot_hbm,
    lid_hbm,
    vel_hbm,
    slopes_hbm,
    stiff_hbm,
    geo_hbm,
    planes_hbm,
    modes_hbm,
    ordered,
    total_ref,
    slot_ref,
    lid_ref,
    vel_r,
    vel_t,
    vel_z,
    cells,
    recv,
    slopes,
    stiff,
    geo,
    to_planes,
    to_modes,
    rhs,
    fields,
    planes,
    push_hi,
    push_lo,
    side_hi,
    side_lo,
    sendb,
    back,
    side_out,
    side_in,
    side_send,
    side_back,
    jac,
    vec,
    img,
    krhs,
    face_in,
    moment,
    red_a,
    red_b,
    local_sem,
    fwd_send,
    fwd_recv,
    bwd_send,
    bwd_recv,
    side_sems,
    fb_send,
    fb_recv,
    halo_send,
    halo_recv,
    a_send,
    a_recv,
    b_send,
    b_recv,
):
    ny, nz, nc = grid_shape
    n_elem = ny * nz * nc
    n_modes = ER
    mi = lax.axis_index("modes")
    e = lax.axis_index("elem")
    core = lax.rem(e, nc)
    zc = lax.rem(e // nc, nz)
    yc = e // (nc * nz)
    size_a = ny * nc
    rank_a = yc * nc + core

    def member_a(t):
        return ((t // nc) * nz + zc) * nc + lax.rem(t, nc)

    def member_b(t):
        return (yc * nz + t) * nc + core

    above = lax.rem(e + 1, n_elem)
    below = lax.rem(e + n_elem - 1, n_elem)

    barrier = pltpu.get_barrier_semaphore()
    greeted = [(lax.rem(mi + t, n_modes), e) for t in range(1, n_modes)]
    greeted += [(mi, above), (mi, below)]
    greeted += [(mi, member_a(lax.rem(rank_a + t, size_a))) for t in range(1, size_a)]
    greeted += [(mi, member_b(lax.rem(zc + t, nz))) for t in range(1, nz)]
    for who in greeted:
        pl.semaphore_signal(barrier, inc=1, device_id=who, device_id_type=MESH)

    span = NODES * ER
    vel = (vel_r, vel_t, vel_z)
    local_pairs = [
        *[
            (vel_hbm.at[pl.ds(s * span, span)], vel[s])
            for s in range(3)
        ],
        (slopes_hbm, slopes),
        (planes_hbm, to_planes),
        (geo_hbm, geo),
        (slot_hbm, slot_ref),
        (lid_hbm, lid_ref),
        (modes_hbm, to_modes),
        (stiff_hbm, stiff),
    ]
    local = [
        pltpu.make_async_copy(src, dst, local_sem.at[i]) for i, (src, dst) in enumerate(local_pairs)
    ]
    for i in (6, 0, 1, 2, 3, 4, 5, 7, 8, 9):
        local[i].start()

    for g in range(ER):
        for s in range(3):
            recv[g, s, NODES:, :] = jnp.zeros((R - NODES, LANES), F32)
            img[0, s, g, TOP + FACE :, :] = jnp.zeros((R - TOP - FACE, LANES), F32)
            side_back[g, s, 2 * FACE - 8 :, :] = jnp.zeros((8, LANES), F32)
    no_rows = jnp.zeros((LANES - R, 3 * LANES), BF16)
    for part in range(3):
        rhs[part * LANES + R : (part + 1) * LANES, :] = no_rows
        for g in range(ER):
            krhs[g, part * LANES + R : (part + 1) * LANES, :] = no_rows
    moment[...] = jnp.zeros_like(moment)

    def gather_cell(g, s, target):
        held = slot_ref[0, g]
        for j in range(PS):
            rows = pl.ds(j * ER + held, PS, stride=ER * PS)
            target[g, s, j * PS : (j + 1) * PS, :] = vel[s][rows, :]

    local[6].wait()
    local[0].wait()
    for off in (1, 3, 2):
        gather_cell(lax.rem(mi + off, n_modes), 0, cells)
    pl.semaphore_wait(barrier, len(greeted))

    forward = {}
    for off, s in [(off, s) for group in ((1, 3), (2,)) for s in range(3) for off in group]:
        if off == 1 and s > 0:
            local[s].wait()
        to = lax.rem(mi + off, n_modes)
        if s > 0:
            gather_cell(to, s, cells)
        forward[off, s] = pltpu.make_async_remote_copy(
            src_ref=cells.at[to, s, pl.ds(0, NODES)],
            dst_ref=recv.at[mi, s, pl.ds(0, NODES)],
            send_sem=fwd_send.at[off, s],
            recv_sem=fwd_recv.at[off, s],
            device_id=(to, e),
            device_id_type=MESH,
        )
        forward[off, s].start()

    lane = lax.broadcasted_iota(jnp.int32, (1, LANES), 1)
    even = lax.rem(lane, 2) == 0
    pair = (lane // 2).astype(F32)

    def times_unit(values):
        return jnp.where(even, -pltpu.roll(values, LANES - 1, 1), pltpu.roll(values, 1, 1))

    def pair_sum(values):
        return values + jnp.where(even, pltpu.roll(values, LANES - 1, 1), pltpu.roll(values, 1, 1))

    for s in range(3):
        gather_cell(mi, s, recv)
    for copy in (*local[3:6], local[7]):
        copy.wait()

    cell_radius = mi.astype(F32) * (1.0 / ER)
    radius = geo[3 * ER, :, :] + cell_radius
    inv_radius = 1.0 / radius
    swirl_base = SWIRL_SLOPE * radius + SWIRL_CURVE * inv_radius

    def slope_of(block, comps, rows):
        for s in comps:
            high, low = split(block[s])
            cols = slice(s * LANES, (s + 1) * LANES)
            rhs[0:R, cols] = high
            rhs[LANES : LANES + R, cols] = low
            rhs[2 * LANES : 2 * LANES + R, cols] = high
        return dot(slopes[0:rows, :], rhs[:, comps[0] * LANES : (comps[-1] + 1) * LANES])

    def add_fields(values, source, half, first):
        for f, field in enumerate(values):
            high, low = split(field)
            rows = slice((3 * half + f) * R, (3 * half + f + 1) * R)
            fields[rows, 0:LANES] = high
            fields[rows, LANES : 2 * LANES] = low
            fields[rows, 2 * LANES :] = high
        rows = slice(3 * half * R, 3 * (half + 1) * R)
        terms = dot(fields[rows, :], to_planes[source])
        if first:
            planes[rows, :] = terms
        else:
            planes[rows, :] += terms

    def add_modes(block, source, first, arrived):
        wave = pair + (source * (LANES // 2)).astype(F32)
        arrived(0)
        arrived(1)
        slope = slope_of(block, (0, 1), 2 * R)
        u_r, u_t = block[0], block[1]
        d_z = [slope[R:, s * LANES : (s + 1) * LANES] for s in range(2)]
        curl_z = slope[:R, LANES:] + (u_t - wave * times_unit(u_r)) * inv_radius
        add_fields((u_r, u_t, curl_z), source, 0, first)
        arrived(2)
        slope = slope_of(block, (2,), R)
        u_z = block[2]
        curl_r = wave * times_unit(u_z) * inv_radius - d_z[1]
        add_fields((u_z, curl_r, d_z[0] - slope), source, 1, first)

    add_modes(recv.at[mi], mi, True, lambda s: None)

    lid = lid_ref[...].astype(BF16)
    wide = lax.broadcasted_iota(jnp.int32, (LANES // 2, LANES), 1) // 2
    tall = lax.broadcasted_iota(jnp.int32, (LANES // 2, LANES), 0)
    noslip = dot(lid, (wide == tall).astype(BF16))
    side = geo[3 * ER + 1, :, :]
    low_side, high_side = side == 1.0, side == 2.0
    at_low, at_high = (e == 0).astype(F32), (e == n_elem - 1).astype(F32)
    lid_rows = jnp.where(low_side, at_low, 0.0) + jnp.where(high_side, at_high, 0.0)
    sharing = 1.0 + jnp.where(low_side, 1.0 - at_low, 0.0) + jnp.where(high_side, 1.0 - at_high, 0.0)
    wave_own = pair + (mi * (LANES // 2)).astype(F32)
    for s, offset in enumerate((1.0, -1.0, 0.0)):
        square = (wave_own + offset) * (wave_own + offset)
        lid_keep = 1.0 - lid_rows * (noslip if s < 2 else 1.0)
        for g in range(ER):
            fixed = geo[ER + g]
            diag = (fixed + square * geo[2 * ER + g]) * sharing
            jac[s, g] = jnp.where(fixed > 0.0, lid_keep / jnp.where(fixed > 0.0, diag, 1.0), 0.0)

    for off in (1, 3, 2):
        source = lax.rem(mi + n_modes - off, n_modes)
        add_modes(recv.at[source], source, False, lambda s: forward[off, s].wait_recv())

    def push_rows(start, to_hi, to_lo, first, pitch):
        def field(f, cols):
            return planes[pl.ds(pl.multiple_of(f * R + start, 8), FACE), cols]

        rad = geo[3 * ER, pl.ds(start, FACE), :] + cell_radius
        swirl = SWIRL_SLOPE * rad + SWIRL_CURVE / rad
        swirl = jnp.concatenate([swirl] * 3, axis=1)
        spin = 2.0 * SWIRL_SLOPE
        for cols in (slice(0, 3 * LANES), slice(3 * LANES, 6 * LANES)):
            u_r, u_t, w_z, u_z, w_r, w_t = [field(f, cols) for f in range(6)]
            turned = u_t + swirl
            results = (
                turned * w_z - u_z * w_t + spin * u_t,
                u_z * w_r - u_r * w_z - spin * u_r,
                u_r * w_t - turned * w_r,
            )
            for s, values in enumerate(results):
                high, low = split(values)
                rows = pl.ds(pl.multiple_of(first + s * pitch, FACE), FACE)
                to_hi[rows, cols] = high
                to_lo[rows, cols] = low

    def bulk_step(step, _):
        start = pl.multiple_of(step * FACE, FACE)
        push_rows(start + FACE, push_hi, push_lo, start, BULK)
        return 0

    lax.fori_loop(0, BULK // FACE, bulk_step, 0, unroll=True)

    def coefficients(high, low, chunk):
        two = dot(high[...], to_modes[chunk])
        one = dot(low[...], to_modes[chunk, :, 0:LANES])
        return INV_NU * (two[:, :LANES] + (two[:, LANES:] + one))

    backward = {}

    def return_bulk(off):
        to = lax.rem(mi + off, n_modes)
        result = coefficients(push_hi, push_lo, to)
        for s in range(3):
            force = result[s * BULK : (s + 1) * BULK] + LAMBDA_COEF * recv[to, s, FACE : FACE + BULK, :]
            if off == 0:
                back[mi, s] = force
            else:
                sendb[off, s] = force
        if off:
            backward[off] = pltpu.make_async_remote_copy(
                src_ref=sendb.at[off, :, pl.ds(0, MID)],
                dst_ref=back.at[mi, :, pl.ds(0, MID)],
                send_sem=bwd_send.at[off],
                recv_sem=bwd_recv.at[off],
                device_id=(to, e),
                device_id_type=MESH,
            )
            backward[off].start()

    local[8].wait()
    return_bulk(2)
    for side, start in enumerate((0, TOP)):
        push_rows(start, side_hi, side_lo, side * FACE, 2 * FACE)
    for chunk in range(n_modes):
        result = coefficients(side_hi, side_lo, chunk)
        for s in range(3):
            for side, start in enumerate((0, TOP)):
                rows = slice((2 * s + side) * FACE, (2 * s + side + 1) * FACE)
                force = result[rows] + LAMBDA_COEF * recv[chunk, s, start : start + FACE, :]
                side_out[side, chunk, s] = force
    side_copies = []
    for side, who in ((0, below), (1, above)):
        copy = pltpu.make_async_remote_copy(
            src_ref=side_out.at[side, :, :, pl.ds(FACE_AT[side], PS)],
            dst_ref=side_in.at[1 - side, :, :, pl.ds(FACE_AT[1 - side], PS)],
            send_sem=side_sems.at[0, side],
            recv_sem=side_sems.at[1, 1 - side],
            device_id=(mi, who),
            device_id_type=MESH,
        )
        copy.start()
        side_copies.append(copy)
    for off in (1, 3, 0):
        return_bulk(off)

    block_row = lax.broadcasted_iota(jnp.int32, (FACE, LANES), 0)
    met = (
        (block_row < PS) & (e > 0),
        (block_row >= FACE_AT[1]) & (block_row < FACE_AT[1] + PS) & (e < n_elem - 1),
    )

    def meet(side, other):
        return jnp.where(met[side], other, 0.0)

    for copy in side_copies:
        copy.wait_recv()
    side_returns = []
    for off in (2, 1, 3, 0):
        to = lax.rem(mi + off, n_modes)
        for s in range(3):
            for side in range(2):
                total = side_out[side, to, s] + meet(side, side_in[side, to, s])
                rows = slice(side * FACE, (side + 1) * FACE)
                if off == 0:
                    side_back[mi, s, rows, :] = total
                else:
                    side_send[off, s, rows, :] = total
        if off:
            copy = pltpu.make_async_remote_copy(
                src_ref=side_send.at[off, :, pl.ds(0, ENDS)],
                dst_ref=side_back.at[mi, :, pl.ds(0, ENDS)],
                send_sem=fb_send.at[off],
                recv_sem=fb_recv.at[off],
                device_id=(to, e),
                device_id_type=MESH,
            )
            copy.start()
            side_returns.append(copy)
    local[9].wait()
    for off in (1, 3, 2):
        backward[off].wait_recv()
    for copy in side_returns:
        copy.wait_recv()

    for g in range(ER):
        pieces = (
            (slice(0, FACE), [side_back[g, s, 0:FACE, :] for s in range(3)]),
            (slice(FACE, TOP), [back[g, s, 0:MID, :] for s in range(3)]),
            (slice(TOP, TOP + FACE), [side_back[g, s, FACE:, :] for s in range(3)]),
        )
        for rows, force in pieces:
            turned = times_unit(force[1])
            mass = geo[g, rows, :]
            img[0, 0, g, rows, :] = mass * (force[0] + turned)
            img[0, 1, g, rows, :] = mass * (force[0] - turned)
            img[0, 2, g, rows, :] = mass * force[2]

    halos = []

    def send_faces(k):
        pairs = []
        for side, start, who in ((0, 0, below), (1, NODES - PS, above)):
            copy = pltpu.make_async_remote_copy(
                src_ref=img.at[k, :, :, pl.ds(start, PS)],
                dst_ref=face_in.at[k - 1, 1 - side, :, :, pl.ds(FACE_AT[1 - side], PS)],
                send_sem=halo_send.at[k - 1, side],
                recv_sem=halo_recv.at[k - 1, 1 - side],
                device_id=(mi, who),
                device_id_type=MESH,
            )
            copy.start()
            pairs.append(copy)
        halos.append(pairs)

    def inner_part(k):
        for s in range(3):
            for g in range(ER):
                vec[k, s, g] = img[k, s, g]
            for g in range(ER - 1):
                last = pl.ds(2 * PS - 1, PS - 2, stride=PS)
                first = pl.ds(PS, PS - 2, stride=PS)
                shared = img[k, s, g, last, :] + img[k, s, g + 1, first, :]
                vec[k, s, g, last, :] = shared
                vec[k, s, g + 1, first, :] = shared
            for g in range(ER):
                vec[k, s, g, FACE:TOP, :] = vec[k, s, g, FACE:TOP, :] * jac[s, g, FACE:TOP, :]
                split_rows(k, g, s, FACE, BULK)

    def outer_part(k):
        if k > 0:
            for copy in halos[k - 1]:
                copy.wait_recv()
        for side, start, last in ((0, 0, PS - 1), (1, TOP, PS + 1)):
            rows = slice(start, start + FACE)
            for s in range(3):
                block = [vec[k, s, g, rows, :] for g in range(ER)]
                if k > 0:
                    block = [block[g] + meet(side, face_in[k - 1, side, s, g]) for g in range(ER)]
                for g in range(ER):
                    total = block[g]
                    if g + 1 < ER:
                        nearby = pltpu.roll(block[g + 1], PS - 1, 0)
                        total = total + jnp.where(block_row == last, nearby, 0.0)
                    if g > 0:
                        nearby = pltpu.roll(block[g - 1], FACE - PS + 1, 0)
                        total = total + jnp.where(block_row == last - PS + 1, nearby, 0.0)
                    vec[k, s, g, rows, :] = total * jac[s, g, rows, :]

    def split_rows(k, g, s, start, stop):
        high, low = split(vec[k, s, g, start:stop, :])
        cols = slice(s * LANES, (s + 1) * LANES)
        krhs[g, start:stop, cols] = high
        krhs[g, LANES + start : LANES + stop, cols] = low
        krhs[g, 2 * LANES + start : 2 * LANES + stop, cols] = high

    def apply_stiff(k):
        for g in range(ER):
            for s in range(3):
                split_rows(k, g, s, 0, FACE)
                split_rows(k, g, s, BULK, R)
            image = dot(stiff[g], krhs[g])
            for s in range(3):
                img[k + 1, s, g] = image[:, s * LANES : (s + 1) * LANES]

    share = 1.0 / sharing

    def inner(k, left, right):
        for s in range(3):
            products = vec[left, s, 0] * img[right, s, 0]
            for g in range(1, ER):
                products = products + vec[left, s, g] * img[right, s, g]
            if right == 0:
                products = products * share
            total = jnp.sum(products, axis=0, keepdims=True)
            index = k * 3 + s
            at = index % MOMENTS
            moment[index // MOMENTS, at : at + 1, :] = total

    inner_part(0)
    outer_part(0)
    apply_stiff(0)
    send_faces(1)
    inner(0, 0, 0)
    inner(1, 0, 1)
    inner_part(1)
    outer_part(1)
    apply_stiff(1)
    send_faces(2)
    inner(2, 1, 1)
    inner(3, 1, 2)
    inner_part(2)
    outer_part(2)
    apply_stiff(2)
    inner(4, 2, 2)
    inner(5, 2, 3)

    def arrange():
        for slot in range(ER):
            held = jnp.int32(0)
            for g in range(ER):
                held = jnp.where(slot_ref[0, g] == slot, g, held)
            for k in range(3):
                for s in range(3):
                    for j in range(PS):
                        rows = pl.ds(j * ER + slot, PS, stride=ER * PS)
                        ordered[k, s, rows, :] = vec[k, s, held, j * PS : (j + 1) * PS, :]

    def exchange(buffer, rank, size, member, send_sems, recv_sems, meanwhile):
        copies = []
        for off in range(1, size):
            copy = pltpu.make_async_remote_copy(
                src_ref=buffer.at[rank, pl.ds(0, MOMENTS)],
                dst_ref=buffer.at[rank, pl.ds(0, MOMENTS)],
                send_sem=send_sems.at[off],
                recv_sem=recv_sems.at[off],
                device_id=(mi, member(lax.rem(rank + off, size))),
                device_id_type=MESH,
            )
            copy.start()
            copies.append(copy)
        meanwhile()
        for copy in copies:
            copy.wait_recv()
        total = buffer[0, 0:MOMENTS, :]
        for t in range(1, size):
            total = total + buffer[t, 0:MOMENTS, :]
        return total, copies

    red_a[rank_a] = jnp.where(even, pair_sum(moment[0]), pair_sum(moment[1]))
    total, copies_a = exchange(red_a, rank_a, size_a, member_a, a_send, a_recv, arrange)
    red_b[zc, 0:MOMENTS, :] = total
    total, copies_b = exchange(red_b, zc, nz, member_b, b_send, b_recv, lambda: None)
    total_ref[...] = total

    sent = (forward.values(), backward.values(), side_copies, side_returns, copies_a, copies_b)
    for copies in (*sent, *halos):
        for copy in copies:
            copy.wait_send()


def combine(ordered, total_ref, out_hbm, out_ref, sems):
    span = NODES * ER
    lane = lax.broadcasted_iota(jnp.int32, (1, LANES), 1)
    even = lax.rem(lane, 2) == 0

    def times_unit(values):
        return jnp.where(even, -pltpu.roll(values, LANES - 1, 1), pltpu.roll(values, 1, 1))

    total = total_ref[...]
    first = jnp.where(even, total, pltpu.roll(total, 1, 1))
    second = jnp.where(even, pltpu.roll(total, LANES - 1, 1), total)

    coefs = []
    for s in range(3):
        h = [(first if k < 3 else second)[(k % 3) * 3 + s : (k % 3) * 3 + s + 1] for k in range(6)]
        g00, g01, g02, g12, g22 = [h[k] + h[k + 1] for k in range(5)]
        g11 = g02
        ratio1, ratio2 = g01 / g00, g02 / g00
        d1 = g11 - ratio1 * g01
        left = g12 - ratio1 * g02
        ratio = left / d1
        d2 = g22 - ratio2 * g02 - ratio * left
        y1 = h[1] - ratio1 * h[0]
        y2 = h[2] - ratio2 * h[0] - ratio * y1
        c2 = y2 / d2
        c1 = y1 / d1 - ratio * c2
        c0 = h[0] / g00 - ratio1 * c1 - ratio2 * c2
        coefs.append((c0, c1, c2))

    block = 2 * ER * PS
    copies = []
    for start in range(0, span, block):
        rows = slice(start, start + block)
        plus, minus, axial = [
            coefs[s][0] * ordered[0, s, rows, :]
            + coefs[s][1] * ordered[1, s, rows, :]
            + coefs[s][2] * ordered[2, s, rows, :]
            for s in range(3)
        ]
        results = ((plus + minus) * 0.5, times_unit(minus - plus) * 0.5, axial)
        for s, values in enumerate(results):
            out_ref[s * span + start : s * span + start + block, :] = values
            rows = pl.ds(s * span + start, block)
            copy = pltpu.make_async_copy(
                out_ref.at[rows], out_hbm.at[rows], sems.at[s, start // block]
            )
            copy.start()
            copies.append(copy)

    for copy in copies:
        copy.wait()


def on_device(grid_shape, velocity, element_slot, lid_noslip):
    ny, nz, nc = grid_shape
    slopes, stiff, geometry, to_planes, to_modes = constants()
    vmem = pltpu.VMEM
    dma = pltpu.SemaphoreType.DMA
    flat = velocity.transpose(0, 2, 3, 1, 4).reshape(3 * NODES * ER, LANES)
    ordered, total = pl.pallas_call(
        functools.partial(kernel, grid_shape),
        out_shape=(vmem((3, 3, NODES * ER, LANES), F32), vmem((MOMENTS, LANES), F32)),
        in_specs=[pl.BlockSpec(memory_space=pltpu.HBM)] * 8,
        out_specs=(pl.BlockSpec(memory_space=vmem),) * 2,
        scratch_shapes=[
            pltpu.SMEM((1, ER), jnp.int32),
            vmem((1, LANES // 2), jnp.int32),
            *[vmem((NODES * ER, LANES), F32)] * 3,
            vmem((ER, 3, R, LANES), F32),
            vmem((ER, 3, R, LANES), F32),
            vmem(slopes.shape, BF16),
            vmem(stiff.shape, BF16),
            vmem(geometry.shape, F32),
            vmem(to_planes.shape, BF16),
            vmem(to_modes.shape, BF16),
            vmem((3 * LANES, 3 * LANES), BF16),
            vmem((6 * R, 3 * LANES), BF16),
            vmem((6 * R, Q), F32),
            vmem((3 * BULK, Q), BF16),
            vmem((3 * BULK, Q), BF16),
            vmem((6 * FACE, Q), BF16),
            vmem((6 * FACE, Q), BF16),
            vmem((ER, 3, BULK, LANES), F32),
            vmem((ER, 3, BULK, LANES), F32),
            vmem((2, ER, 3, FACE, LANES), F32),
            vmem((2, ER, 3, FACE, LANES), F32),
            vmem((ER, 3, 2 * FACE, LANES), F32),
            vmem((ER, 3, 2 * FACE, LANES), F32),
            vmem((3, ER, R, LANES), F32),
            vmem((3, 3, ER, R, LANES), F32),
            vmem((4, 3, ER, R, LANES), F32),
            vmem((ER, 3 * LANES, 3 * LANES), BF16),
            vmem((2, 2, 3, ER, FACE, LANES), F32),
            vmem((2, 16, LANES), F32),
            vmem((ny * nc, 16, LANES), F32),
            vmem((nz, 16, LANES), F32),
            dma((10,)),
            dma((ER, 3)),
            dma((ER, 3)),
            dma((ER,)),
            dma((ER,)),
            dma((2, 2)),
            dma((ER,)),
            dma((ER,)),
            dma((2, 2)),
            dma((2, 2)),
            dma((ny * nc,)),
            dma((ny * nc,)),
            dma((nz,)),
            dma((nz,)),
        ],
        compiler_params=pltpu.CompilerParams(
            collective_id=0, has_side_effects=True, vmem_limit_bytes=48 * 1024 * 1024
        ),
    )(
        *[
            pltpu.with_memory_space_constraint(operand, pltpu.HBM)
            for operand in (
                element_slot,
                lid_noslip.reshape(1, -1),
                flat,
                *[jnp.asarray(table) for table in (slopes, stiff, geometry, to_planes, to_modes)],
            )
        ]
    )
    result = pl.pallas_call(
        combine,
        out_shape=jax.ShapeDtypeStruct((3 * NODES * ER, LANES), F32),
        in_specs=[pl.BlockSpec(memory_space=vmem)] * 2,
        out_specs=pl.BlockSpec(memory_space=pl.ANY),
        scratch_shapes=[vmem((3 * NODES * ER, LANES), F32), dma((3, 5))],
    )(*[pltpu.with_memory_space_constraint(held, pltpu.VMEM) for held in (ordered, total)])
    return result.reshape(3, PS, PS, ER, LANES).transpose(0, 3, 1, 2, 4)


def solution(mesh):
    n_elem = mesh.shape["elem"]
    nc = 2
    nz = min(8, n_elem // nc)
    ny = n_elem // (nc * nz)
    return jax.shard_map(
        functools.partial(on_device, (ny, nz, nc)),
        mesh=mesh,
        in_specs=(P(None, "elem", None, None, "modes"), P("elem", None), P("modes")),
        out_specs=P(None, "elem", None, None, "modes"),
        check_vma=False,
    )
```

```python
import functools

import jax
import jax.numpy as jnp
import ml_dtypes
import numpy as np
from jax import lax
from jax.experimental import pallas as pl
from jax.experimental.pallas import tpu as pltpu
from jax.sharding import PartitionSpec as P

PS = 10
NODES = PS * PS
R = 112
TOP = 88
FACE = 16
FACE_AT = (0, NODES - PS - TOP)
MID = TOP - FACE
ENDS = NODES - MID
MOMENTS = 9
BULK = 80
M = 256
Q = 768
ER = 4
LANES = 128
LAMBDA_COEF = 20.0
INV_NU = 10.0
R_INNER = 1.0
SWIRL_SLOPE = -1.0 / 3.0
SWIRL_CURVE = 4.0 / 3.0
MESH = pl.DeviceIdType.MESH
F32 = jnp.float32
BF16 = jnp.bfloat16


def legendre_rows(abscissa, degree):
    table_rows = [abscissa * 0.0 + 1.0, abscissa.copy()]
    for degree_now in range(2, degree + 1):
        table_rows.append(
            ((2 * degree_now - 1) * abscissa * table_rows[-1] - (degree_now - 1) * table_rows[-2])
            / degree_now
        )
    return table_rows


def gll_tables(points):
    degree = points - 1
    abscissa = -np.cos(np.pi * np.arange(points) / degree)
    for _ in range(60):
        legendre = legendre_rows(abscissa, degree)
        abscissa = abscissa - (abscissa * legendre[degree] - legendre[degree - 1]) / (
            points * legendre[degree]
        )
    legendre = legendre_rows(abscissa, degree)
    last_row = legendre[degree]
    weights = 2.0 / (degree * points * last_row**2)
    identity = np.eye(points)
    distance = abscissa[:, None] - abscissa[None, :] + identity
    derivative = last_row[:, None] / (last_row[None, :] * distance) * (1.0 - identity)
    derivative[0, 0] = -degree * points / 4.0
    derivative[degree, degree] = degree * points / 4.0
    return abscissa, weights, derivative


def halves(values):
    high = values.astype(ml_dtypes.bfloat16)
    low = (values - high.astype(np.float64)).astype(ml_dtypes.bfloat16)
    return high, low


@functools.cache
def constants():
    xi, w, deriv = gll_tables(PS)
    eye = np.eye(PS)
    radius = R_INNER + (np.arange(ER)[:, None] + 0.5 * (xi[None, :] + 1.0)) / ER
    ww = np.outer(w, w)

    def operator(rows):
        padded = np.zeros((R, LANES))
        padded[:NODES, :NODES] = rows
        high, low = halves(padded)
        return np.concatenate([high, high, low], axis=1)

    slope_r = operator(2.0 * ER * np.kron(eye, deriv))
    slope_z = operator(2.0 * ER * np.kron(deriv, eye))
    slopes = np.concatenate([slope_r, slope_z], axis=0)

    stiff, stiff_diag = [], np.zeros((ER, PS, PS))
    for ir in range(ER):
        along_i = deriv.T @ np.diag(w * radius[ir]) @ deriv
        along_j = deriv.T @ np.diag(w) @ deriv
        whole = np.kron(np.diag(w), along_i) + np.kron(along_j, np.diag(w * radius[ir]))
        stiff_diag[ir] = np.diag(whole).reshape(PS, PS).T
        stiff.append(operator(whole - np.diag(np.diag(whole))))
    stiff = np.stack(stiff)

    quarter_h = 0.25 / (ER * ER)
    mass_r = ww[None] * quarter_h * radius[:, :, None]
    mass_over_r = ww[None] * quarter_h / radius[:, :, None]

    def radial_sum(values):
        total = values.copy()
        total[:-1, -1] += values[1:, 0]
        total[1:, 0] += values[:-1, -1]
        return total

    diag_fixed = radial_sum(stiff_diag + LAMBDA_COEF * mass_r)
    diag_square = radial_sum(mass_over_r)
    diag_fixed[0, 0] = 0.0
    diag_fixed[-1, -1] = 0.0

    geometry = np.zeros((3 * ER + 2, R, LANES))
    for part, values in enumerate((mass_r, diag_fixed, diag_square)):
        rows = values.transpose(0, 2, 1).reshape(ER, NODES, 1)
        geometry[part * ER : (part + 1) * ER, :NODES] = rows
    geometry[3 * ER] = 1.0
    geometry[3 * ER, :NODES] = (R_INNER + 0.5 * (np.tile(xi, PS) + 1.0) / ER)[:, None]
    geometry[3 * ER + 1, :PS] = 1.0
    geometry[3 * ER + 1, NODES - PS : NODES] = 2.0

    modes = np.arange(M)
    angles = (modes[:, None] * np.arange(Q)[None, :] % Q) * (2.0 * np.pi / Q)
    weight = np.where(modes == 0, 1.0, 2.0)[:, None]
    inverse = np.stack([weight * np.cos(angles), -weight * np.sin(angles)], axis=1)
    inverse = inverse.reshape(2 * M // LANES, LANES, Q)
    high, low = halves(inverse)
    to_planes = np.concatenate([high, high, low], axis=1)
    forward = np.stack([np.cos(angles), -np.sin(angles)], axis=1) / Q
    forward = forward.reshape(2 * M // LANES, LANES, Q).transpose(0, 2, 1)
    high, low = halves(forward)
    to_modes = np.concatenate([high, low], axis=2)
    return slopes, stiff, geometry.astype(np.float32), to_planes, to_modes


def split(values):
    high = values.astype(BF16)
    low = (values - high.astype(F32)).astype(BF16)
    return high, low


def dot(left, right):
    return jnp.dot(left, right, preferred_element_type=F32)


def kernel(
    grid_shape,
    slot_hbm,
    lid_hbm,
    vel_hbm,
    slopes_hbm,
    stiff_hbm,
    geo_hbm,
    planes_hbm,
    modes_hbm,
    ordered,
    total_ref,
    slot_ref,
    lid_ref,
    vel_r,
    vel_t,
    vel_z,
    cells,
    recv,
    slopes,
    stiff,
    geo,
    to_planes,
    to_modes,
    rhs,
    fields,
    planes,
    push_hi,
    push_lo,
    side_hi,
    side_lo,
    sendb,
    back,
    side_out,
    side_in,
    side_send,
    side_back,
    jac,
    vec,
    img,
    krhs,
    face_in,
    moment,
    red_a,
    red_b,
    local_sem,
    fwd_send,
    fwd_recv,
    bwd_send,
    bwd_recv,
    side_sems,
    fb_send,
    fb_recv,
    halo_send,
    halo_recv,
    a_send,
    a_recv,
    b_send,
    b_recv,
):
    ny, nz, nc = grid_shape
    n_elem = ny * nz * nc
    n_modes = ER
    mi = lax.axis_index("modes")
    e = lax.axis_index("elem")
    core = lax.rem(e, nc)
    zc = lax.rem(e // nc, nz)
    yc = e // (nc * nz)
    size_a = ny * nc
    rank_a = yc * nc + core

    def member_a(t):
        return ((t // nc) * nz + zc) * nc + lax.rem(t, nc)

    def member_b(t):
        return (yc * nz + t) * nc + core

    above = lax.rem(e + 1, n_elem)
    below = lax.rem(e + n_elem - 1, n_elem)

    barrier = pltpu.get_barrier_semaphore()
    greeted = [(lax.rem(mi + t, n_modes), e) for t in range(1, n_modes)]
    greeted += [(mi, above), (mi, below)]
    greeted += [(mi, member_a(lax.rem(rank_a + t, size_a))) for t in range(1, size_a)]
    greeted += [(mi, member_b(lax.rem(zc + t, nz))) for t in range(1, nz)]
    for who in greeted:
        pl.semaphore_signal(barrier, inc=1, device_id=who, device_id_type=MESH)

    span = NODES * ER
    vel = (vel_r, vel_t, vel_z)
    local_pairs = [
        *[
            (vel_hbm.at[pl.ds(s * span, span)], vel[s])
            for s in range(3)
        ],
        (slopes_hbm, slopes),
        (planes_hbm, to_planes),
        (geo_hbm, geo),
        (slot_hbm, slot_ref),
        (lid_hbm, lid_ref),
        (modes_hbm, to_modes),
        (stiff_hbm, stiff),
    ]
    local = [
        pltpu.make_async_copy(src, dst, local_sem.at[i]) for i, (src, dst) in enumerate(local_pairs)
    ]
    for i in (6, 0, 1, 2, 3, 4, 5, 7, 8, 9):
        local[i].start()

    for g in range(ER):
        for s in range(3):
            recv[g, s, NODES:, :] = jnp.zeros((R - NODES, LANES), F32)
            img[0, s, g, TOP + FACE :, :] = jnp.zeros((R - TOP - FACE, LANES), F32)
            side_back[g, s, 2 * FACE - 8 :, :] = jnp.zeros((8, LANES), F32)
    no_rows = jnp.zeros((LANES - R, 3 * LANES), BF16)
    for part in range(3):
        rhs[part * LANES + R : (part + 1) * LANES, :] = no_rows
        for g in range(ER):
            krhs[g, part * LANES + R : (part + 1) * LANES, :] = no_rows
    moment[...] = jnp.zeros_like(moment)

    def gather_cell(g, s, target):
        held = slot_ref[0, g]
        for j in range(PS):
            rows = pl.ds(j * ER + held, PS, stride=ER * PS)
            target[g, s, j * PS : (j + 1) * PS, :] = vel[s][rows, :]

    local[6].wait()
    local[0].wait()
    for off in (1, 3, 2):
        gather_cell(lax.rem(mi + off, n_modes), 0, cells)
    pl.semaphore_wait(barrier, len(greeted))

    forward = {}
    for off, s in [(off, s) for group in ((1, 3), (2,)) for s in range(3) for off in group]:
        if off == 1 and s > 0:
            local[s].wait()
        to = lax.rem(mi + off, n_modes)
        if s > 0:
            gather_cell(to, s, cells)
        forward[off, s] = pltpu.make_async_remote_copy(
            src_ref=cells.at[to, s, pl.ds(0, NODES)],
            dst_ref=recv.at[mi, s, pl.ds(0, NODES)],
            send_sem=fwd_send.at[off, s],
            recv_sem=fwd_recv.at[off, s],
            device_id=(to, e),
            device_id_type=MESH,
        )
        forward[off, s].start()

    lane = lax.broadcasted_iota(jnp.int32, (1, LANES), 1)
    even = lax.rem(lane, 2) == 0
    pair = (lane // 2).astype(F32)

    def times_unit(values):
        return jnp.where(even, -pltpu.roll(values, LANES - 1, 1), pltpu.roll(values, 1, 1))

    def pair_sum(values):
        return values + jnp.where(even, pltpu.roll(values, LANES - 1, 1), pltpu.roll(values, 1, 1))

    for s in range(3):
        gather_cell(mi, s, recv)
    for copy in (*local[3:6], local[7]):
        copy.wait()

    cell_radius = mi.astype(F32) * (1.0 / ER)
    radius = geo[3 * ER, :, :] + cell_radius
    inv_radius = 1.0 / radius
    swirl_base = SWIRL_SLOPE * radius + SWIRL_CURVE * inv_radius

    def slope_of(block, comps, rows):
        for s in comps:
            high, low = split(block[s])
            cols = slice(s * LANES, (s + 1) * LANES)
            rhs[0:R, cols] = high
            rhs[LANES : LANES + R, cols] = low
            rhs[2 * LANES : 2 * LANES + R, cols] = high
        return dot(slopes[0:rows, :], rhs[:, comps[0] * LANES : (comps[-1] + 1) * LANES])

    def add_fields(values, source, half, first):
        for f, field in enumerate(values):
            high, low = split(field)
            rows = slice((3 * half + f) * R, (3 * half + f + 1) * R)
            fields[rows, 0:LANES] = high
            fields[rows, LANES : 2 * LANES] = low
            fields[rows, 2 * LANES :] = high
        rows = slice(3 * half * R, 3 * (half + 1) * R)
        terms = dot(fields[rows, :], to_planes[source])
        if first:
            planes[rows, :] = terms
        else:
            planes[rows, :] += terms

    def add_modes(block, source, first, arrived):
        wave = pair + (source * (LANES // 2)).astype(F32)
        arrived(0)
        arrived(1)
        slope = slope_of(block, (0, 1), 2 * R)
        u_r, u_t = block[0], block[1]
        d_z = [slope[R:, s * LANES : (s + 1) * LANES] for s in range(2)]
        curl_z = slope[:R, LANES:] + (u_t - wave * times_unit(u_r)) * inv_radius
        add_fields((u_r, u_t, curl_z), source, 0, first)
        arrived(2)
        slope = slope_of(block, (2,), R)
        u_z = block[2]
        curl_r = wave * times_unit(u_z) * inv_radius - d_z[1]
        add_fields((u_z, curl_r, d_z[0] - slope), source, 1, first)

    add_modes(recv.at[mi], mi, True, lambda s: None)

    lid = lid_ref[...].astype(BF16)
    wide = lax.broadcasted_iota(jnp.int32, (LANES // 2, LANES), 1) // 2
    tall = lax.broadcasted_iota(jnp.int32, (LANES // 2, LANES), 0)
    noslip = dot(lid, (wide == tall).astype(BF16))
    side = geo[3 * ER + 1, :, :]
    low_side, high_side = side == 1.0, side == 2.0
    at_low, at_high = (e == 0).astype(F32), (e == n_elem - 1).astype(F32)
    lid_rows = jnp.where(low_side, at_low, 0.0) + jnp.where(high_side, at_high, 0.0)
    sharing = 1.0 + jnp.where(low_side, 1.0 - at_low, 0.0) + jnp.where(high_side, 1.0 - at_high, 0.0)
    wave_own = pair + (mi * (LANES // 2)).astype(F32)
    for s, offset in enumerate((1.0, -1.0, 0.0)):
        square = (wave_own + offset) * (wave_own + offset)
        lid_keep = 1.0 - lid_rows * (noslip if s < 2 else 1.0)
        for g in range(ER):
            fixed = geo[ER + g]
            diag = (fixed + square * geo[2 * ER + g]) * sharing
            jac[s, g] = jnp.where(fixed > 0.0, lid_keep / jnp.where(fixed > 0.0, diag, 1.0), 0.0)

    for off in (1, 3, 2):
        source = lax.rem(mi + n_modes - off, n_modes)
        add_modes(recv.at[source], source, False, lambda s: forward[off, s].wait_recv())

    def push_rows(start, to_hi, to_lo, first, pitch):
        def field(f, cols):
            return planes[pl.ds(pl.multiple_of(f * R + start, 8), FACE), cols]

        rad = geo[3 * ER, pl.ds(start, FACE), :] + cell_radius
        swirl = SWIRL_SLOPE * rad + SWIRL_CURVE / rad
        swirl = jnp.concatenate([swirl] * 3, axis=1)
        spin = 2.0 * SWIRL_SLOPE
        for cols in (slice(0, 3 * LANES), slice(3 * LANES, 6 * LANES)):
            u_r, u_t, w_z, u_z, w_r, w_t = [field(f, cols) for f in range(6)]
            turned = u_t + swirl
            results = (
                turned * w_z - u_z * w_t + spin * u_t,
                u_z * w_r - u_r * w_z - spin * u_r,
                u_r * w_t - turned * w_r,
            )
            for s, values in enumerate(results):
                high, low = split(values)
                rows = pl.ds(pl.multiple_of(first + s * pitch, FACE), FACE)
                to_hi[rows, cols] = high
                to_lo[rows, cols] = low

    def bulk_step(step, _):
        start = pl.multiple_of(step * FACE, FACE)
        push_rows(start + FACE, push_hi, push_lo, start, BULK)
        return 0

    lax.fori_loop(0, BULK // FACE, bulk_step, 0, unroll=True)

    def coefficients(high, low, chunk):
        two = dot(high[...], to_modes[chunk])
        one = dot(low[...], to_modes[chunk, :, 0:LANES])
        return INV_NU * (two[:, :LANES] + (two[:, LANES:] + one))

    backward = {}

    def send_bulk(off, comps, sem):
        to = lax.rem(mi + off, n_modes)
        rows = pl.ds(0, MID)
        copy = pltpu.make_async_remote_copy(
            src_ref=sendb.at[off, comps, rows],
            dst_ref=back.at[mi, comps, rows],
            send_sem=bwd_send.at[sem],
            recv_sem=bwd_recv.at[sem],
            device_id=(to, e),
            device_id_type=MESH,
        )
        copy.start()
        backward[sem] = copy

    def return_bulk(off):
        to = lax.rem(mi + off, n_modes)
        count = 1 if off == 2 else 3
        for first in range(0, 3, count):
            part = pl.ds(first * BULK, count * BULK)
            result = coefficients(push_hi.at[part], push_lo.at[part], to)
            for s in range(first, first + count):
                held = recv[to, s, FACE : FACE + BULK, :]
                at = (s - first) * BULK
                force = result[at : at + BULK] + LAMBDA_COEF * held
                if off == 0:
                    back[mi, s] = force
                else:
                    sendb[off, s] = force
            if off:
                send_bulk(off, pl.ds(first, count), 2 * first if off == 2 else off)

    local[8].wait()
    return_bulk(2)
    for side, start in enumerate((0, TOP)):
        push_rows(start, side_hi, side_lo, side * FACE, 2 * FACE)
    for chunk in range(n_modes):
        result = coefficients(side_hi, side_lo, chunk)
        for s in range(3):
            for side, start in enumerate((0, TOP)):
                rows = slice((2 * s + side) * FACE, (2 * s + side + 1) * FACE)
                force = result[rows] + LAMBDA_COEF * recv[chunk, s, start : start + FACE, :]
                side_out[side, chunk, s] = force
    side_copies = []
    for side, who in ((0, below), (1, above)):
        copy = pltpu.make_async_remote_copy(
            src_ref=side_out.at[side, :, :, pl.ds(FACE_AT[side], PS)],
            dst_ref=side_in.at[1 - side, :, :, pl.ds(FACE_AT[1 - side], PS)],
            send_sem=side_sems.at[0, side],
            recv_sem=side_sems.at[1, 1 - side],
            device_id=(mi, who),
            device_id_type=MESH,
        )
        copy.start()
        side_copies.append(copy)
    for off in (1, 3, 0):
        return_bulk(off)

    block_row = lax.broadcasted_iota(jnp.int32, (FACE, LANES), 0)
    met = (
        (block_row < PS) & (e > 0),
        (block_row >= FACE_AT[1]) & (block_row < FACE_AT[1] + PS) & (e < n_elem - 1),
    )

    def meet(side, other):
        return jnp.where(met[side], other, 0.0)

    for copy in side_copies:
        copy.wait_recv()
    side_returns = []
    for off in (2, 1, 3, 0):
        to = lax.rem(mi + off, n_modes)
        for s in range(3):
            for side in range(2):
                total = side_out[side, to, s] + meet(side, side_in[side, to, s])
                rows = slice(side * FACE, (side + 1) * FACE)
                if off == 0:
                    side_back[mi, s, rows, :] = total
                else:
                    side_send[off, s, rows, :] = total
        if off:
            copy = pltpu.make_async_remote_copy(
                src_ref=side_send.at[off, :, pl.ds(0, ENDS)],
                dst_ref=side_back.at[mi, :, pl.ds(0, ENDS)],
                send_sem=fb_send.at[off],
                recv_sem=fb_recv.at[off],
                device_id=(to, e),
                device_id_type=MESH,
            )
            copy.start()
            side_returns.append(copy)
    local[9].wait()
    for sem in (1, 3, 0, 2, 4):
        backward[sem].wait_recv()
    for copy in side_returns:
        copy.wait_recv()

    for g in range(ER):
        pieces = (
            (slice(0, FACE), [side_back[g, s, 0:FACE, :] for s in range(3)]),
            (slice(FACE, TOP), [back[g, s, 0:MID, :] for s in range(3)]),
            (slice(TOP, TOP + FACE), [side_back[g, s, FACE:, :] for s in range(3)]),
        )
        for rows, force in pieces:
            turned = times_unit(force[1])
            mass = geo[g, rows, :]
            img[0, 0, g, rows, :] = mass * (force[0] + turned)
            img[0, 1, g, rows, :] = mass * (force[0] - turned)
            img[0, 2, g, rows, :] = mass * force[2]

    halos = []

    def send_faces(k):
        pairs = []
        for side, start, who in ((0, 0, below), (1, NODES - PS, above)):
            copy = pltpu.make_async_remote_copy(
                src_ref=img.at[k, :, :, pl.ds(start, PS)],
                dst_ref=face_in.at[k - 1, 1 - side, :, :, pl.ds(FACE_AT[1 - side], PS)],
                send_sem=halo_send.at[k - 1, side],
                recv_sem=halo_recv.at[k - 1, 1 - side],
                device_id=(mi, who),
                device_id_type=MESH,
            )
            copy.start()
            pairs.append(copy)
        halos.append(pairs)

    def inner_part(k):
        for s in range(3):
            for g in range(ER):
                vec[k, s, g] = img[k, s, g]
            for g in range(ER - 1):
                last = pl.ds(2 * PS - 1, PS - 2, stride=PS)
                first = pl.ds(PS, PS - 2, stride=PS)
                shared = img[k, s, g, last, :] + img[k, s, g + 1, first, :]
                vec[k, s, g, last, :] = shared
                vec[k, s, g + 1, first, :] = shared
            for g in range(ER):
                vec[k, s, g, FACE:TOP, :] = vec[k, s, g, FACE:TOP, :] * jac[s, g, FACE:TOP, :]
                split_rows(k, g, s, FACE, BULK)

    def outer_part(k):
        if k > 0:
            for copy in halos[k - 1]:
                copy.wait_recv()
        for side, start, last in ((0, 0, PS - 1), (1, TOP, PS + 1)):
            rows = slice(start, start + FACE)
            for s in range(3):
                block = [vec[k, s, g, rows, :] for g in range(ER)]
                if k > 0:
                    block = [block[g] + meet(side, face_in[k - 1, side, s, g]) for g in range(ER)]
                for g in range(ER):
                    total = block[g]
                    if g + 1 < ER:
                        nearby = pltpu.roll(block[g + 1], PS - 1, 0)
                        total = total + jnp.where(block_row == last, nearby, 0.0)
                    if g > 0:
                        nearby = pltpu.roll(block[g - 1], FACE - PS + 1, 0)
                        total = total + jnp.where(block_row == last - PS + 1, nearby, 0.0)
                    vec[k, s, g, rows, :] = total * jac[s, g, rows, :]

    def split_rows(k, g, s, start, stop):
        high, low = split(vec[k, s, g, start:stop, :])
        cols = slice(s * LANES, (s + 1) * LANES)
        krhs[g, start:stop, cols] = high
        krhs[g, LANES + start : LANES + stop, cols] = low
        krhs[g, 2 * LANES + start : 2 * LANES + stop, cols] = high

    def apply_stiff(k):
        for g in range(ER):
            for s in range(3):
                split_rows(k, g, s, 0, FACE)
                split_rows(k, g, s, BULK, R)
            image = dot(stiff[g], krhs[g])
            for s in range(3):
                img[k + 1, s, g] = image[:, s * LANES : (s + 1) * LANES]

    share = 1.0 / sharing

    def inner(k, left, right):
        for s in range(3):
            products = vec[left, s, 0] * img[right, s, 0]
            for g in range(1, ER):
                products = products + vec[left, s, g] * img[right, s, g]
            if right == 0:
                products = products * share
            total = jnp.sum(products, axis=0, keepdims=True)
            index = k * 3 + s
            at = index % MOMENTS
            moment[index // MOMENTS, at : at + 1, :] = total

    inner_part(0)
    outer_part(0)
    apply_stiff(0)
    send_faces(1)
    inner(0, 0, 0)
    inner(1, 0, 1)
    inner_part(1)
    outer_part(1)
    apply_stiff(1)
    send_faces(2)
    inner(2, 1, 1)
    inner(3, 1, 2)
    inner_part(2)
    outer_part(2)
    apply_stiff(2)
    inner(4, 2, 2)
    inner(5, 2, 3)

    def arrange():
        for slot in range(ER):
            held = jnp.int32(0)
            for g in range(ER):
                held = jnp.where(slot_ref[0, g] == slot, g, held)
            for k in range(3):
                for s in range(3):
                    for j in range(PS):
                        rows = pl.ds(j * ER + slot, PS, stride=ER * PS)
                        ordered[k, s, rows, :] = vec[k, s, held, j * PS : (j + 1) * PS, :]

    def exchange(buffer, rank, size, member, send_sems, recv_sems, meanwhile):
        copies = []
        for off in range(1, size):
            copy = pltpu.make_async_remote_copy(
                src_ref=buffer.at[rank, pl.ds(0, MOMENTS)],
                dst_ref=buffer.at[rank, pl.ds(0, MOMENTS)],
                send_sem=send_sems.at[off],
                recv_sem=recv_sems.at[off],
                device_id=(mi, member(lax.rem(rank + off, size))),
                device_id_type=MESH,
            )
            copy.start()
            copies.append(copy)
        meanwhile()
        for copy in copies:
            copy.wait_recv()
        total = buffer[0, 0:MOMENTS, :]
        for t in range(1, size):
            total = total + buffer[t, 0:MOMENTS, :]
        return total, copies

    red_a[rank_a] = jnp.where(even, pair_sum(moment[0]), pair_sum(moment[1]))
    total, copies_a = exchange(red_a, rank_a, size_a, member_a, a_send, a_recv, arrange)
    red_b[zc, 0:MOMENTS, :] = total
    total, copies_b = exchange(red_b, zc, nz, member_b, b_send, b_recv, lambda: None)
    total_ref[...] = total

    sent = (forward.values(), backward.values(), side_copies, side_returns, copies_a, copies_b)
    for copies in (*sent, *halos):
        for copy in copies:
            copy.wait_send()


def combine(ordered, total_ref, out_hbm, out_ref, sems):
    span = NODES * ER
    lane = lax.broadcasted_iota(jnp.int32, (1, LANES), 1)
    even = lax.rem(lane, 2) == 0

    def times_unit(values):
        return jnp.where(even, -pltpu.roll(values, LANES - 1, 1), pltpu.roll(values, 1, 1))

    total = total_ref[...]
    first = jnp.where(even, total, pltpu.roll(total, 1, 1))
    second = jnp.where(even, pltpu.roll(total, LANES - 1, 1), total)

    coefs = []
    for s in range(3):
        h = [(first if k < 3 else second)[(k % 3) * 3 + s : (k % 3) * 3 + s + 1] for k in range(6)]
        g00, g01, g02, g12, g22 = [h[k] + h[k + 1] for k in range(5)]
        g11 = g02
        ratio1, ratio2 = g01 / g00, g02 / g00
        d1 = g11 - ratio1 * g01
        left = g12 - ratio1 * g02
        ratio = left / d1
        d2 = g22 - ratio2 * g02 - ratio * left
        y1 = h[1] - ratio1 * h[0]
        y2 = h[2] - ratio2 * h[0] - ratio * y1
        c2 = y2 / d2
        c1 = y1 / d1 - ratio * c2
        c0 = h[0] / g00 - ratio1 * c1 - ratio2 * c2
        coefs.append((c0, c1, c2))

    block = 2 * ER * PS
    copies = []
    for start in range(0, span, block):
        rows = slice(start, start + block)
        plus, minus, axial = [
            coefs[s][0] * ordered[0, s, rows, :]
            + coefs[s][1] * ordered[1, s, rows, :]
            + coefs[s][2] * ordered[2, s, rows, :]
            for s in range(3)
        ]
        results = ((plus + minus) * 0.5, times_unit(minus - plus) * 0.5, axial)
        for s, values in enumerate(results):
            out_ref[s * span + start : s * span + start + block, :] = values
            rows = pl.ds(s * span + start, block)
            copy = pltpu.make_async_copy(
                out_ref.at[rows], out_hbm.at[rows], sems.at[s, start // block]
            )
            copy.start()
            copies.append(copy)

    for copy in copies:
        copy.wait()


def on_device(grid_shape, velocity, element_slot, lid_noslip):
    ny, nz, nc = grid_shape
    slopes, stiff, geometry, to_planes, to_modes = constants()
    vmem = pltpu.VMEM
    dma = pltpu.SemaphoreType.DMA
    flat = velocity.transpose(0, 2, 3, 1, 4).reshape(3 * NODES * ER, LANES)
    ordered, total = pl.pallas_call(
        functools.partial(kernel, grid_shape),
        out_shape=(vmem((3, 3, NODES * ER, LANES), F32), vmem((MOMENTS, LANES), F32)),
        in_specs=[pl.BlockSpec(memory_space=pltpu.HBM)] * 8,
        out_specs=(pl.BlockSpec(memory_space=vmem),) * 2,
        scratch_shapes=[
            pltpu.SMEM((1, ER), jnp.int32),
            vmem((1, LANES // 2), jnp.int32),
            *[vmem((NODES * ER, LANES), F32)] * 3,
            vmem((ER, 3, R, LANES), F32),
            vmem((ER, 3, R, LANES), F32),
            vmem(slopes.shape, BF16),
            vmem(stiff.shape, BF16),
            vmem(geometry.shape, F32),
            vmem(to_planes.shape, BF16),
            vmem(to_modes.shape, BF16),
            vmem((3 * LANES, 3 * LANES), BF16),
            vmem((6 * R, 3 * LANES), BF16),
            vmem((6 * R, Q), F32),
            vmem((3 * BULK, Q), BF16),
            vmem((3 * BULK, Q), BF16),
            vmem((6 * FACE, Q), BF16),
            vmem((6 * FACE, Q), BF16),
            vmem((ER, 3, BULK, LANES), F32),
            vmem((ER, 3, BULK, LANES), F32),
            vmem((2, ER, 3, FACE, LANES), F32),
            vmem((2, ER, 3, FACE, LANES), F32),
            vmem((ER, 3, 2 * FACE, LANES), F32),
            vmem((ER, 3, 2 * FACE, LANES), F32),
            vmem((3, ER, R, LANES), F32),
            vmem((3, 3, ER, R, LANES), F32),
            vmem((4, 3, ER, R, LANES), F32),
            vmem((ER, 3 * LANES, 3 * LANES), BF16),
            vmem((2, 2, 3, ER, FACE, LANES), F32),
            vmem((2, 16, LANES), F32),
            vmem((ny * nc, 16, LANES), F32),
            vmem((nz, 16, LANES), F32),
            dma((10,)),
            dma((ER, 3)),
            dma((ER, 3)),
            dma((5,)),
            dma((5,)),
            dma((2, 2)),
            dma((ER,)),
            dma((ER,)),
            dma((2, 2)),
            dma((2, 2)),
            dma((ny * nc,)),
            dma((ny * nc,)),
            dma((nz,)),
            dma((nz,)),
        ],
        compiler_params=pltpu.CompilerParams(
            collective_id=0, has_side_effects=True, vmem_limit_bytes=48 * 1024 * 1024
        ),
    )(
        *[
            pltpu.with_memory_space_constraint(operand, pltpu.HBM)
            for operand in (
                element_slot,
                lid_noslip.reshape(1, -1),
                flat,
                *[jnp.asarray(table) for table in (slopes, stiff, geometry, to_planes, to_modes)],
            )
        ]
    )
    result = pl.pallas_call(
        combine,
        out_shape=jax.ShapeDtypeStruct((3 * NODES * ER, LANES), F32),
        in_specs=[pl.BlockSpec(memory_space=vmem)] * 2,
        out_specs=pl.BlockSpec(memory_space=pl.ANY),
        scratch_shapes=[vmem((3 * NODES * ER, LANES), F32), dma((3, 5))],
    )(*[pltpu.with_memory_space_constraint(held, pltpu.VMEM) for held in (ordered, total)])
    return result.reshape(3, PS, PS, ER, LANES).transpose(0, 3, 1, 2, 4)


def solution(mesh):
    n_elem = mesh.shape["elem"]
    nc = 2
    nz = min(8, n_elem // nc)
    ny = n_elem // (nc * nz)
    return jax.shard_map(
        functools.partial(on_device, (ny, nz, nc)),
        mesh=mesh,
        in_specs=(P(None, "elem", None, None, "modes"), P("elem", None), P("modes")),
        out_specs=P(None, "elem", None, None, "modes"),
        check_vma=False,
    )
```
